32 devices in a mesh: dp: 16 (over z, y, core), tensor: 2 (over x).
Axes of the slice: x: 2, y: 2, z: 4, core: 2. Of those that a mesh axis runs over, the one named last changes fastest.
Arguments:
- tokens: bfloat16 [32768, 1024], P('dp'), may hold values from -6 to 6
- cotangent: bfloat16 [32768, 1024], P('dp'), may hold values from -6 to 6
- lengths: int32 [16, 3], P('dp'), may hold values from 1 to 1228, 2048 in all within a row
- mixer_gain: bfloat16 [1024], replicated, may hold values from 0.5 to 1.5
- in_weight: bfloat16 [1024, 3, 1024], P(None, None, 'tensor'), may hold values from -0.1875 to 0.1875
- conv_weight: bfloat16 [3, 1024], P(None, 'tensor'), may hold values from -3.5 to 3.5
- out_weight: bfloat16 [1024, 1024], P('tensor'), may hold values from -0.1875 to 0.1875
- ffn_gain: bfloat16 [1024], replicated, may hold values from 0.5 to 1.5
- gate_weight: bfloat16 [1024, 4608], P(None, 'tensor'), may hold values from -0.1875 to 0.1875
- up_weight: bfloat16 [1024, 4608], P(None, 'tensor'), may hold values from -0.1875 to 0.1875
- down_weight: bfloat16 [4608, 1024], P('tensor'), may hold values from -0.09375 to 0.09375
Outputs:
- output: bfloat16 [32768, 1024], P('dp')
- input_grad: bfloat16 [32768, 1024], P('dp')
- mixer_gain_grad: float32 [1024], replicated
- in_weight_grad: float32 [1024, 3, 1024], P(None, None, 'tensor')
- conv_weight_grad: float32 [3, 1024], P(None, 'tensor')
- out_weight_grad: float32 [1024, 1024], P('tensor')
- ffn_gain_grad: float32 [1024], replicated
- gate_weight_grad: float32 [1024, 4608], P(None, 'tensor')
- up_weight_grad: float32 [1024, 4608], P(None, 'tensor')
- down_weight_grad: float32 [4608, 1024], P('tensor')
The draws below stay inside these ranges and needn't reach their ends.
Inputs may be any that keep to these rules, and one draw needn't show every extreme that they name: `lengths`: each row sums to 2048, and its largest entry is exactly 1228.
All inputs are finite; a program needn't handle non-finite values.
Results may differ from the reference program's by a relative error of at most 0.011.
Values may be sent and summed in bfloat16 or wider, within the bound.
A program may use at most 320 MiB of HBM per device.

```python
import math
import jax
import jax.numpy as jnp
import numpy as np
from jax import lax

D = 1024
FF = 4608
TOK_DEV = 2048
SEQS = 3
MOST = 1228
GROUPS = 16
TOKENS = 32768


def shard_levels(key, dims, pieces, low, high):
    def one(position, shards_of):
        steps = jax.random.uniform(jax.random.fold_in(jax.random.fold_in(key, 6), position), (shards_of,), jnp.float32, low / len(pieces), high / len(pieces))
        return jnp.repeat(jnp.exp(steps), dims[position] // shards_of).reshape((-1,) + (1,) * (len(dims) - position - 1))

    loudness = one(*pieces[0])
    for cut in pieces[1:]:
        loudness = loudness * one(*cut)
    return loudness


def length_profile(number_of, total, bound, skew):
    weights = [(1 << 20) // math.isqrt(rank ** skew) + 1 for rank in range(2, number_of + 1)]
    rest, given = total - bound - (number_of - 1), [1] * (number_of - 1)
    while rest > 0:
        candidates = [i for i in range(number_of - 1) if given[i] < bound]
        whole, remaining = sum([weights[i] for i in candidates]), rest
        for i in candidates:
            extra = min(bound - given[i], max(1, remaining * weights[i] // whole), rest)
            given[i] = given[i] + extra
            rest = rest - extra
    return np.array([bound] + given)


def ragged_sizes(rng, count, total, bound, lean):
    if count == 2:
        one = jax.random.randint(rng, (), max(1, total - bound), min(bound, total - 1) + 1)
        return jnp.stack([one, total - one])
    sizes = jnp.asarray(length_profile(count, total, bound, lean), jnp.int32)
    couples = (count - 1) // 2
    donor, receiver = sizes[1:1 + 2 * couples:2], sizes[2:2 + 2 * couples:2]
    slack = jnp.minimum(donor - 1, bound - receiver)
    moved = jax.random.randint(jax.random.fold_in(rng, 1), (couples,), 0, 1 << 20) % (slack + 1)
    sizes = sizes.at[1:1 + 2 * couples:2].set(donor - moved).at[2:2 + 2 * couples:2].set(receiver + moved)
    return sizes[jax.random.permutation(jax.random.fold_in(rng, 2), count)]


def scatter_about(key, extent, spread, reach, cuts=(), held_as=jnp.bfloat16):
    result = jax.random.normal(key, extent, jnp.float32) * spread
    if len(cuts) > 0:
        result = shard_levels(key, extent, cuts, -0.22, 0.18) * result
    return jnp.clip(result, min=-reach, max=reach).astype(held_as)


def setup_inputs(seed: int = 0) -> dict:
    streams_of = jax.random.split(jax.random.key(seed), 12)
    return {
        "tokens": scatter_about(streams_of[0], (TOKENS, D), 1.0, 6.0, ((0, 16),)),
        "cotangent": scatter_about(streams_of[1], (TOKENS, D), 1.0, 6.0, ((0, 16),)),
        "lengths": jax.vmap(lambda own: ragged_sizes(own, SEQS, TOK_DEV, MOST, 1))(jax.random.split(streams_of[2], GROUPS)).reshape((GROUPS, SEQS)).astype(jnp.int32),
        "mixer_gain": jnp.clip(1.0 + 0.1 * jax.random.normal(streams_of[3], (D,), jnp.float32), 0.5, 1.5).astype(jnp.bfloat16),
        "in_weight": scatter_about(streams_of[4], (D, 3, D), D ** -0.5, 0.1875, ((2, 2),)),
        "conv_weight": scatter_about(streams_of[5], (3, D), 3 ** -0.5, 3.5, ((1, 2),)),
        "out_weight": scatter_about(streams_of[6], (D, D), D ** -0.5, 0.1875, ((0, 2),)),
        "ffn_gain": jnp.clip(1.0 + 0.1 * jax.random.normal(streams_of[7], (D,), jnp.float32), 0.5, 1.5).astype(jnp.bfloat16),
        "gate_weight": scatter_about(streams_of[8], (D, FF), D ** -0.5, 0.1875, ((1, 2),)),
        "up_weight": scatter_about(streams_of[9], (D, FF), D ** -0.5, 0.1875, ((1, 2),)),
        "down_weight": scatter_about(streams_of[10], (FF, D), FF ** -0.5, 0.09375, ((0, 2),)),
    }


EPS = 1e-05
HIGH = lax.Precision.HIGHEST

@jax.custom_vjp
def low(v):
    return lax.optimization_barrier(v.astype(jnp.bfloat16)).astype(jnp.float32)

@jax.custom_vjp
def low_back(v):
    return v

def low_keep(v):
    return (low(v), None)

def low_pass(kept, grad):
    return (grad,)

def back_keep(v):
    return (v, None)

def back_low(kept, grad):
    return (low(grad),)
low.defvjp(low_keep, low_pass)
low_back.defvjp(back_keep, back_low)

def distances(lengths):
    lengths = lengths.astype(jnp.int32)
    ends = jnp.cumsum(lengths).astype(jnp.int32)
    starts = (ends - lengths).astype(jnp.int32)
    places = jnp.arange(TOK_DEV, dtype=jnp.int32)
    begin = lax.optimization_barrier(jnp.max(jnp.where(starts[None, :] <= places[:, None], starts[None, :], 0), axis=1)).astype(jnp.int32)
    return (places - begin).astype(jnp.int32)

def rms_scale(value):
    return lax.rsqrt(lax.optimization_barrier(jnp.mean(value * value, axis=-1, keepdims=True)) + EPS)

def conv_apply(mixed, taps, dist):
    one = jnp.concatenate([jnp.zeros_like(mixed[:1]), mixed[:-1]], 0) * (dist >= 1)[:, None].astype(mixed.dtype)
    two = jnp.concatenate([jnp.zeros_like(mixed[:2]), mixed[:-2]], 0) * (dist >= 2)[:, None].astype(mixed.dtype)
    return taps[0] * mixed + taps[1] * one + taps[2] * two

def layer(x, g1, w_in, taps, w_out, g2, w_gate, w_up, w_down, dist):
    h1 = low(x * rms_scale(x) * g1)
    proj = low_back(jnp.einsum('td,dkc->tkc', h1, w_in, precision=HIGH))
    mixed = proj[:, 0] * proj[:, 2]
    z = low(proj[:, 1] * conv_apply(mixed, taps, dist))
    a = low_back(jnp.dot(z, w_out, precision=HIGH))
    r1 = x + a
    h2 = low(r1 * rms_scale(r1) * g2)
    gate = low_back(jnp.dot(h2, w_gate, precision=HIGH))
    up = low_back(jnp.dot(h2, w_up, precision=HIGH))
    hid = low(jax.nn.silu(gate) * up)
    return r1 + jnp.dot(hid, w_down, precision=HIGH)

def reference(tokens, cotangent, lengths, mixer_gain, in_weight, conv_weight, out_weight, ffn_gain, gate_weight, up_weight, down_weight):
    params = tuple((w.astype(jnp.float32) for w in (mixer_gain, in_weight, conv_weight, out_weight, ffn_gain, gate_weight, up_weight, down_weight)))
    xs = tokens.astype(jnp.float32).reshape(GROUPS, TOK_DEV, D)
    cots = cotangent.astype(jnp.float32).reshape(GROUPS, TOK_DEV, D)

    def group(carry, item):
        x, cot, lens = item
        dist = distances(lens)
        out, pull = jax.vjp(lambda xv, *p: layer(xv, *p, dist), x, *params)
        grads = pull(cot)
        new = tuple((c + g for c, g in zip(carry, grads[1:])))
        return (new, (out.astype(jnp.bfloat16), grads[0].astype(jnp.bfloat16)))
    init = tuple((jnp.zeros(p.shape, jnp.float32) for p in params))
    sums, (outs, dxs) = lax.scan(group, init, (xs, cots, lengths.astype(jnp.int32)))
    return (outs.reshape(TOKENS, D), dxs.reshape(TOKENS, D), sums[0], sums[1], sums[2], sums[3], sums[4], sums[5], sums[6], sums[7])
```

```python
import jax
import jax.numpy as jnp
from jax import lax
from jax.sharding import PartitionSpec as P

EPS = 1e-05
F32 = jnp.float32
BF = jnp.bfloat16


def distances(lengths, count):
    ends = jnp.cumsum(lengths)
    starts = ends - lengths
    places = jnp.arange(count, dtype=jnp.int32)
    begin = jnp.max(jnp.where(starts[None, :] <= places[:, None], starts[None, :], 0), axis=1)
    return places - begin


def rms_scale(value):
    return lax.rsqrt(jnp.mean(value * value, axis=-1, keepdims=True) + EPS)


def shift_down(value, steps, keep):
    moved = jnp.concatenate([jnp.zeros_like(value[:steps]), value[:-steps]], 0)
    return moved * keep


def shift_up(value, steps):
    return jnp.concatenate([value[steps:], jnp.zeros_like(value[:steps])], 0)


def norm_back(grad_in, normed, scale, gain):
    weighted = grad_in * gain
    inner = jnp.mean(weighted * normed, axis=-1, keepdims=True)
    return (scale * (weighted - normed * inner), jnp.sum(grad_in * normed, axis=0))


def dot(a, b, ca, cb):
    return lax.dot_general(a, b, (((ca,), (cb,)), ((), ())), preferred_element_type=F32)


def swap_tensor(value):
    return lax.ppermute(value, "tensor", [(0, 1), (1, 0)])


def swap_core(value, count):
    return lax.ppermute(value, "dp", [(i, i ^ 1) for i in range(count)])


def fetch_other(weight, core, count):
    half = weight.shape[0] // 2
    mine = lax.dynamic_slice_in_dim(weight, core * half, half, 0)
    got = swap_tensor(mine)
    rest = swap_core(got, count)
    low = jnp.where(core == 0, got, rest)
    high = jnp.where(core == 0, rest, got)
    return jnp.concatenate([low, high], 0)


def pair_body(
    tokens,
    cotangent,
    lengths,
    mixer_gain,
    in_weight,
    conv_weight,
    out_weight,
    ffn_gain,
    gate_weight,
    up_weight,
    down_weight,
):
    rows, width = tokens.shape
    count = lax.axis_size("dp")
    core = lax.axis_index("dp") % 2
    side = lax.axis_index("tensor")
    half = out_weight.shape[0]
    in_flat = in_weight.reshape(width, 3 * half)
    in_other = fetch_other(in_flat, core, count).reshape(width, 3, half)
    out_other = fetch_other(out_weight, core, count)
    taps_other = swap_tensor(conv_weight)

    def ordered(own, other, axis):
        return jnp.concatenate(
            [jnp.where(side == 0, own, other), jnp.where(side == 0, other, own)], axis
        )

    in_full = ordered(in_weight, in_other, 2).reshape(width, 6 * half)
    out_full = ordered(out_weight, out_other, 0)
    taps = ordered(conv_weight, taps_other, 1).astype(F32)
    full = 2 * half

    dist = distances(lengths[0], rows)
    keep_one = (dist >= 1)[:, None].astype(F32)
    keep_two = (dist >= 2)[:, None].astype(F32)
    x = tokens.astype(F32)
    dy = cotangent.astype(F32)
    g1 = mixer_gain.astype(F32)
    g2 = ffn_gain.astype(F32)
    scale1 = rms_scale(x)
    normed1 = x * scale1
    h1b = (normed1 * g1).astype(BF)
    proj = dot(h1b, in_full, 1, 0)
    b_part, c_part, x_part = (proj[:, :full], proj[:, full : 2 * full], proj[:, 2 * full :])
    mixed = b_part * x_part
    mixed_one = shift_down(mixed, 1, keep_one)
    mixed_two = shift_down(mixed, 2, keep_two)
    conv_out = taps[0] * mixed + taps[1] * mixed_one + taps[2] * mixed_two
    zb = (c_part * conv_out).astype(BF)
    resid = x + dot(zb, out_full, 1, 0)
    scale2 = rms_scale(resid)
    normed2 = resid * scale2
    h2b = (normed2 * g2).astype(BF)

    gate = dot(h2b, gate_weight, 1, 0)
    up = dot(h2b, up_weight, 1, 0)
    sig = jax.nn.sigmoid(gate)
    silu = gate * sig
    hidb = (silu * up).astype(BF)
    down_grad = dot(hidb, cotangent, 0, 0).astype(BF)
    down_sum = lax.psum(down_grad, "dp")
    d_hid = dot(cotangent, down_weight, 1, 1)
    d_gate = (d_hid * up * sig * (1.0 + gate * (1.0 - sig))).astype(BF)
    d_up = (d_hid * silu).astype(BF)
    dh2_own = (dot(d_gate, gate_weight, 1, 1) + dot(d_up, up_weight, 1, 1)).astype(BF)
    dh2_got = swap_tensor(dh2_own)
    gate_grad = dot(h2b, d_gate, 0, 0).astype(BF)
    up_grad = dot(h2b, d_up, 0, 0).astype(BF)
    gate_sum, up_sum = lax.psum((gate_grad, up_grad), "dp")
    ffn_own = dot(hidb, down_weight, 1, 0).astype(BF)
    ffn_got = swap_tensor(ffn_own)

    dh2 = dh2_own.astype(F32) + dh2_got.astype(F32)
    d_resid, g2_grad = norm_back(dh2, normed2, scale2, g2)
    dr1 = dy + d_resid
    dr1b = dr1.astype(BF)
    own = lambda v, axis: lax.dynamic_slice_in_dim(v, side * half, half, axis)
    out_grad = dot(own(zb, 1), dr1b, 0, 0).astype(BF)
    d_z = dot(dr1b, out_full, 1, 1)
    d_c = d_z * conv_out
    d_conv = d_z * c_part
    d_own = own(d_conv, 1)
    conv_grad = jnp.stack(
        [
            jnp.sum(d_own * own(mixed, 1), axis=0),
            jnp.sum(d_own * own(mixed_one, 1), axis=0),
            jnp.sum(d_own * own(mixed_two, 1), axis=0),
        ],
        0,
    )
    d_mixed = (
        taps[0] * d_conv
        + taps[1] * shift_up(d_conv * keep_one, 1)
        + taps[2] * shift_up(d_conv * keep_two, 2)
    )
    d_b = (d_mixed * x_part).astype(BF)
    d_c = d_c.astype(BF)
    d_x = (d_mixed * b_part).astype(BF)
    in_grad = jnp.stack(
        [dot(h1b, own(d_b, 1), 0, 0), dot(h1b, own(d_c, 1), 0, 0), dot(h1b, own(d_x, 1), 0, 0)], 1
    ).astype(BF)
    d_proj = jnp.concatenate([d_b, d_c, d_x], 1)
    dh1 = dot(d_proj, in_full, 1, 1)
    d_input, g1_grad = norm_back(dh1, normed1, scale1, g1)
    input_grad = (dr1 + d_input).astype(BF)
    output = (resid + (ffn_own.astype(F32) + ffn_got.astype(F32))).astype(BF)
    in_sum, out_sum = lax.psum((in_grad, out_grad), "dp")
    g1_sum, conv_sum, g2_sum = lax.psum((g1_grad, conv_grad, g2_grad), "dp")
    return (
        output,
        input_grad,
        g1_sum,
        in_sum.astype(F32),
        conv_sum,
        out_sum.astype(F32),
        g2_sum,
        gate_sum.astype(F32),
        up_sum.astype(F32),
        down_sum.astype(F32),
    )


def body(
    tokens,
    cotangent,
    lengths,
    mixer_gain,
    in_weight,
    conv_weight,
    out_weight,
    ffn_gain,
    gate_weight,
    up_weight,
    down_weight,
):
    rows = tokens.shape[0]
    dist = distances(lengths[0], rows)
    keep_one = (dist >= 1)[:, None].astype(jnp.float32)
    keep_two = (dist >= 2)[:, None].astype(jnp.float32)
    parts = lax.axis_size("tensor")
    share = rows // parts
    first = lax.axis_index("tensor") * share
    x = tokens.astype(jnp.float32)
    dy = cotangent.astype(jnp.float32)
    g1 = mixer_gain.astype(jnp.float32)
    g2 = ffn_gain.astype(jnp.float32)
    taps = conv_weight.astype(jnp.float32)
    scale1 = rms_scale(x)
    normed1 = x * scale1
    h1b = (normed1 * g1).astype(jnp.bfloat16)
    proj = jnp.einsum("td,dkc->tkc", h1b, in_weight, preferred_element_type=jnp.float32)
    b_part, c_part, x_part = (proj[:, 0], proj[:, 1], proj[:, 2])
    mixed = b_part * x_part
    mixed_one = shift_down(mixed, 1, keep_one)
    mixed_two = shift_down(mixed, 2, keep_two)
    conv_out = taps[0] * mixed + taps[1] * mixed_one + taps[2] * mixed_two
    zb = (c_part * conv_out).astype(jnp.bfloat16)
    mix_part = jnp.dot(zb, out_weight, preferred_element_type=jnp.float32)
    mix_rows = lax.psum_scatter(mix_part, "tensor", scatter_dimension=0, tiled=True)
    x_rows = lax.dynamic_slice_in_dim(x, first, share, 0)
    resid = x_rows + mix_rows
    scale2 = rms_scale(resid)
    normed2 = resid * scale2
    h2b = lax.all_gather((normed2 * g2).astype(jnp.bfloat16), "tensor", axis=0, tiled=True)
    gate = jnp.dot(h2b, gate_weight, preferred_element_type=jnp.float32)
    up = jnp.dot(h2b, up_weight, preferred_element_type=jnp.float32)
    sig = jax.nn.sigmoid(gate)
    silu = gate * sig
    hidb = (silu * up).astype(jnp.bfloat16)
    ffn_part = jnp.dot(hidb, down_weight, preferred_element_type=jnp.float32)
    down_grad = jnp.einsum("tf,td->fd", hidb, cotangent, preferred_element_type=jnp.float32)
    d_hid = jnp.einsum("td,fd->tf", cotangent, down_weight, preferred_element_type=jnp.float32)
    d_gate = (d_hid * up * sig * (1.0 + gate * (1.0 - sig))).astype(jnp.bfloat16)
    d_up = (d_hid * silu).astype(jnp.bfloat16)
    gate_grad = jnp.einsum("td,tf->df", h2b, d_gate, preferred_element_type=jnp.float32)
    up_grad = jnp.einsum("td,tf->df", h2b, d_up, preferred_element_type=jnp.float32)
    dh2_part = jnp.einsum("tf,df->td", d_gate, gate_weight, preferred_element_type=jnp.float32)
    dh2_part = dh2_part + jnp.einsum(
        "tf,df->td", d_up, up_weight, preferred_element_type=jnp.float32
    )
    ffn_rows = lax.psum_scatter(
        ffn_part.astype(jnp.bfloat16), "tensor", scatter_dimension=0, tiled=True
    ).astype(jnp.float32)
    output = lax.all_gather((resid + ffn_rows).astype(jnp.bfloat16), "tensor", axis=0, tiled=True)
    dh2_rows = lax.psum_scatter(dh2_part, "tensor", scatter_dimension=0, tiled=True)
    d_resid, g2_grad = norm_back(dh2_rows, normed2, scale2, g2)
    dr1 = lax.dynamic_slice_in_dim(dy, first, share, 0) + d_resid
    dr1b = lax.all_gather(dr1.astype(jnp.bfloat16), "tensor", axis=0, tiled=True)
    out_grad = jnp.einsum("tc,td->cd", zb, dr1b, preferred_element_type=jnp.float32)
    d_z = jnp.einsum("td,cd->tc", dr1b, out_weight, preferred_element_type=jnp.float32)
    d_c = d_z * conv_out
    d_conv = d_z * c_part
    conv_grad = jnp.stack(
        [
            jnp.sum(d_conv * mixed, axis=0),
            jnp.sum(d_conv * mixed_one, axis=0),
            jnp.sum(d_conv * mixed_two, axis=0),
        ],
        0,
    )
    d_mixed = (
        taps[0] * d_conv
        + taps[1] * shift_up(d_conv * keep_one, 1)
        + taps[2] * shift_up(d_conv * keep_two, 2)
    )
    d_proj = jnp.stack([d_mixed * x_part, d_c, d_mixed * b_part], 1).astype(jnp.bfloat16)
    in_grad_w = jnp.einsum("td,tkc->dkc", h1b, d_proj, preferred_element_type=jnp.float32)
    dh1_part = jnp.einsum("tkc,dkc->td", d_proj, in_weight, preferred_element_type=jnp.float32)
    dh1_rows = lax.psum_scatter(dh1_part, "tensor", scatter_dimension=0, tiled=True)
    normed1_rows = lax.dynamic_slice_in_dim(normed1, first, share, 0)
    scale1_rows = lax.dynamic_slice_in_dim(scale1, first, share, 0)
    d_input, g1_grad = norm_back(dh1_rows, normed1_rows, scale1_rows, g1)
    input_grad = lax.all_gather((dr1 + d_input).astype(jnp.bfloat16), "tensor", axis=0, tiled=True)
    g1_grad, g2_grad = lax.psum((g1_grad, g2_grad), "tensor")
    summed = lax.psum(
        (g1_grad, in_grad_w, conv_grad, out_grad, g2_grad, gate_grad, up_grad, down_grad), "dp"
    )
    return (
        output,
        input_grad,
        summed[0],
        summed[1],
        summed[2],
        summed[3],
        summed[4],
        summed[5],
        summed[6],
        summed[7],
    )


def solution(mesh):
    paired = mesh.shape["tensor"] == 2 and mesh.shape["dp"] % 2 == 0
    return jax.shard_map(
        pair_body if paired else body,
        mesh=mesh,
        in_specs=(
            P("dp", None),
            P("dp", None),
            P("dp", None),
            P(),
            P(None, None, "tensor"),
            P(None, "tensor"),
            P("tensor", None),
            P(),
            P(None, "tensor"),
            P(None, "tensor"),
            P("tensor", None),
        ),
        out_specs=(
            P("dp", None),
            P("dp", None),
            P(),
            P(None, None, "tensor"),
            P(None, "tensor"),
            P("tensor", None),
            P(),
            P(None, "tensor"),
            P(None, "tensor"),
            P("tensor", None),
        ),
        check_vma=False,
    )
```

```python
import jax
import jax.numpy as jnp
from jax import lax
from jax.experimental import pallas as pl
from jax.experimental.pallas import tpu as pltpu
from jax.sharding import PartitionSpec as P

EPS = 1e-05
F32 = jnp.float32
BF = jnp.bfloat16
MESH = pl.DeviceIdType.MESH
TILE_ROWS, TILE_COLS = 1024, 256
BLOCK = 256
SLOTS = 10
VMEM_BYTES = 60 << 20


def distances(lengths, count):
    ends = jnp.cumsum(lengths)
    starts = ends - lengths
    places = jnp.arange(count, dtype=jnp.int32)
    begin = jnp.max(jnp.where(starts[None, :] <= places[:, None], starts[None, :], 0), axis=1)
    return places - begin


def rms_scale(value):
    return lax.rsqrt(jnp.mean(value * value, axis=-1, keepdims=True) + EPS)


def shift_down(value, steps, keep):
    moved = jnp.concatenate([jnp.zeros_like(value[:steps]), value[:-steps]], 0)
    return moved * keep


def shift_up(value, steps):
    return jnp.concatenate([value[steps:], jnp.zeros_like(value[:steps])], 0)


def norm_back(grad_in, normed, scale, gain):
    weighted = grad_in * gain
    inner = jnp.mean(weighted * normed, axis=-1, keepdims=True)
    return (scale * (weighted - normed * inner), jnp.sum(grad_in * normed, axis=0))


def dot(a, b, ca, cb):
    return lax.dot_general(a, b, (((ca,), (cb,)), ((), ())), preferred_element_type=F32)


def swap_tensor(value):
    return lax.ppermute(value, "tensor", [(0, 1), (1, 0)])


def swap_core(value, count):
    return lax.ppermute(value, "dp", [(i, i ^ 1) for i in range(count)])


def swiglu_kernel(h2_ref, gate_ref, up_ref, hid_ref, slope_ref, silu_ref):
    h2 = h2_ref[...]
    gate = dot(h2, gate_ref[...], 1, 0)
    up = dot(h2, up_ref[...], 1, 0)
    sig = jax.nn.sigmoid(gate)
    silu = gate * sig
    hid_ref[...] = (silu * up).astype(BF)
    slope_ref[...] = (up * sig * (1.0 + gate * (1.0 - sig))).astype(BF)
    silu_ref[...] = silu.astype(BF)


def swiglu(h2, gate_w, up_w):
    rows, width = h2.shape
    hidden = gate_w.shape[1]
    out = jax.ShapeDtypeStruct((rows, hidden), BF)
    row_spec = pl.BlockSpec((BLOCK, hidden), lambda i: (i, 0))
    whole = pl.BlockSpec((width, hidden), lambda i: (0, 0), pipeline_mode=pl.Buffered(1))
    return pl.pallas_call(
        swiglu_kernel,
        grid=(rows // BLOCK,),
        out_shape=(out, out, out),
        in_specs=[pl.BlockSpec((BLOCK, width), lambda i: (i, 0)), whole, whole],
        out_specs=(row_spec, row_spec, row_spec),
        compiler_params=pltpu.CompilerParams(vmem_limit_bytes=VMEM_BYTES),
    )(h2, gate_w, up_w)


class Reducer:
    def __init__(self, count, tiles, parts, whole, send, recv, out_ref, out_sem):
        self.count, self.slots = count, tiles.shape[0]
        self.tiles, self.parts, self.whole = tiles, parts, whole
        self.send, self.recv = send, recv
        self.out_ref, self.out_sem = out_ref, out_sem
        self.me = lax.axis_index("dp")
        self.side = lax.axis_index("tensor")

    def plan(self, n):
        me = self.me
        bit = [me % 2, (me // 2) % 2, (me // 4) % 2, (me // 8) % 2]
        swap = (n % 4) == 3
        mine = [bit[0], jnp.where(swap, bit[2], bit[1]), jnp.where(swap, bit[1], bit[2]), bit[3]]
        step = [1, jnp.where(swap, 4, 2), jnp.where(swap, 2, 4), 8]
        peer = [me + s * (1 - 2 * b) for s, b in zip(step, mine)]
        keep, off = [], 0
        give = []
        for s in range(4):
            size = TILE_ROWS >> (s + 1)
            give.append(pl.multiple_of(off + (1 - mine[s]) * size, size))
            off = off + mine[s] * size
            keep.append(pl.multiple_of(off, size))
        return peer, keep, give

    def scatter(self, n, s):
        peer, keep, give = self.plan(n)
        slot = n % self.slots
        size = TILE_ROWS >> (s + 1)
        return pltpu.make_async_remote_copy(
            src_ref=self.tiles.at[slot, pl.ds(give[s], size)],
            dst_ref=self.parts[s].at[slot],
            send_sem=self.send.at[slot, s],
            recv_sem=self.recv.at[slot, s],
            device_id=(peer[s], self.side),
            device_id_type=MESH,
        )

    def gather(self, n, s):
        peer, keep, give = self.plan(n)
        slot = n % self.slots
        size = TILE_ROWS >> (s + 1)
        block = self.whole.at[slot, pl.ds(keep[s], size)]
        return pltpu.make_async_remote_copy(
            src_ref=block,
            dst_ref=block,
            send_sem=self.send.at[slot, 4 + s],
            recv_sem=self.recv.at[slot, 4 + s],
            device_id=(peer[s], self.side),
            device_id_type=MESH,
        )

    def write(self, n):
        slot = n % self.slots
        column = pl.multiple_of(n * TILE_COLS, TILE_COLS)
        return pltpu.make_async_copy(
            self.whole.at[slot], self.out_ref.at[:, pl.ds(column, TILE_COLS)], self.out_sem.at[slot]
        )

    def add(self, n, s):
        peer, keep, give = self.plan(n)
        slot = n % self.slots
        size = TILE_ROWS >> (s + 1)
        rows = pl.ds(keep[s], size)
        total = self.tiles[slot, rows, :].astype(F32) + self.parts[s][slot].astype(F32)
        into = self.whole if s == 3 else self.tiles
        into[slot, rows, :] = total.astype(BF)

    def put(self, n, value):
        self.tiles[n % self.slots] = value.astype(BF)
        self.scatter(n, 0).start()

    def tick(self, n):
        def stage(k):
            m = n - k

            @pl.when((m >= 0) & (m < self.count))
            def _():
                if k <= 4:
                    self.scatter(m, k - 1).wait()
                    self.add(m, k - 1)
                    if k < 4:
                        self.scatter(m, k).start()
                    else:
                        self.gather(m, 3).start()
                elif k <= 8:
                    self.gather(m, 8 - k).wait()
                    if k < 8:
                        self.gather(m, 7 - k).start()
                    else:
                        self.write(m).start()
                else:
                    self.write(m).wait()

        for k in (1, 6, 2, 3, 4, 5, 7, 8, 9):
            stage(k)


def ffn_kernel(
    hid_ref,
    slope_ref,
    silu_ref,
    h2_ref,
    dy_ref,
    gate_ref,
    up_ref,
    down_ref,
    sums_ref,
    dgu_ref,
    dh2_own_ref,
    dh2_got_ref,
    ffn_own_ref,
    ffn_got_ref,
    dy_v,
    h2_v,
    gate_v,
    up_v,
    down_v,
    tile_v,
    slope_v,
    silu_v,
    dgu_v,
    row_v,
    hid_v,
    tiles,
    whole,
    part0,
    part1,
    part2,
    part3,
    load_sem,
    tile_sem,
    pair_sem,
    dgu_sem,
    own_sem,
    hid_sem,
    x_send,
    x_recv,
    send,
    recv,
    out_sem,
):
    me, side = lax.axis_index("dp"), lax.axis_index("tensor")
    hidden = hid_ref.shape[1]
    rows = hid_ref.shape[0]
    down_tiles = hidden // TILE_COLS
    count = 3 * down_tiles
    blocks = rows // BLOCK
    red = Reducer(count, tiles, (part0, part1, part2, part3), whole, send, recv, sums_ref, out_sem)

    loads = [
        pltpu.make_async_copy(src, dst, load_sem.at[i])
        for i, (src, dst) in enumerate(
            (
                (dy_ref, dy_v),
                (down_ref, down_v),
                (gate_ref, gate_v),
                (up_ref, up_v),
                (h2_ref, h2_v),
            )
        )
    ]

    def hid_tile(n):
        column = pl.multiple_of(n * TILE_COLS, TILE_COLS)
        return pltpu.make_async_copy(
            hid_ref.at[:, pl.ds(column, TILE_COLS)], tile_v.at[n % 2], tile_sem.at[n % 2]
        )

    def dgu_tile(n):
        column = pl.multiple_of(n * TILE_COLS, TILE_COLS)
        return pltpu.make_async_copy(
            dgu_ref.at[:, pl.ds(column, TILE_COLS)], tile_v.at[n % 2], tile_sem.at[n % 2]
        )

    def block_rows(i):
        return pl.ds(pl.multiple_of((blocks - 1 - i) * BLOCK, BLOCK), BLOCK)

    def pair(i):
        at = block_rows(i)
        return (
            pltpu.make_async_copy(slope_ref.at[at], slope_v.at[i % 2], pair_sem.at[i % 2, 0]),
            pltpu.make_async_copy(silu_ref.at[at], silu_v.at[i % 2], pair_sem.at[i % 2, 1]),
        )

    def dgu_out(i):
        return pltpu.make_async_copy(dgu_v.at[i % 2], dgu_ref.at[block_rows(i)], dgu_sem.at[i % 2])

    def hid_rows(i):
        return pltpu.make_async_copy(hid_ref.at[block_rows(i)], hid_v.at[i % 2], hid_sem.at[i % 2])

    def row_own(i, ref):
        return pltpu.make_async_copy(row_v.at[i % 2], ref.at[block_rows(i % blocks)], own_sem.at[i % 2])

    def row_send(i, ref):
        return pltpu.make_async_remote_copy(
            src_ref=row_v.at[i % 2],
            dst_ref=ref.at[block_rows(i % blocks)],
            send_sem=x_send.at[i % 2],
            recv_sem=x_recv.at[i],
            device_id=(me, 1 - side),
            device_id_type=MESH,
        )

    loads[0].start()
    hid_tile(0).start()
    for copy in loads[1:]:
        copy.start()
    for copy in pair(0):
        copy.start()

    barrier = pltpu.get_barrier_semaphore()
    for other in ((1, 2, 4, 8)):
        pl.semaphore_signal(
            barrier,
            inc=1,
            device_id=(me + other * (1 - 2 * ((me // other) % 2)), side),
            device_id_type=MESH,
        )
    pl.semaphore_signal(barrier, inc=1, device_id=(me, 1 - side), device_id_type=MESH)
    pl.semaphore_wait(barrier, 5)
    loads[0].wait()

    def down_step(n, carry):
        @pl.when(n + 1 < down_tiles)
        def _():
            hid_tile(n + 1).start()

        hid_tile(n).wait()
        red.put(n, dot(dy_v[...], tile_v[n % 2], 0, 0))
        return carry

    lax.fori_loop(0, 3, down_step, 0)
    red.tick(1)
    lax.fori_loop(3, down_tiles, down_step, 0)
    for copy in loads[1:4]:
        copy.wait()

    def grad_step(i, carry):
        slot = i % 2

        @pl.when(i + 1 < blocks)
        def _():
            for copy in pair(i + 1):
                copy.start()

        for copy in pair(i):
            copy.wait()

        @pl.when(i >= 2)
        def _():
            dgu_out(i - 2).wait()
            row_own(i - 2, dh2_own_ref).wait()
            row_send(i - 2, dh2_got_ref).wait_send()

        d_hid = dot(dy_v[block_rows(i), :], down_v[...], 1, 1)
        dgu_v[slot, :, :hidden] = (d_hid * slope_v[slot].astype(F32)).astype(BF)
        dgu_v[slot, :, hidden:] = (d_hid * silu_v[slot].astype(F32)).astype(BF)
        dgu_out(i).start()
        total = dot(dgu_v[slot, :, :hidden], gate_v[...], 1, 1)
        total = total + dot(dgu_v[slot, :, hidden:], up_v[...], 1, 1)
        row_v[slot] = total.astype(BF)
        row_own(i, dh2_own_ref).start()
        row_send(i, dh2_got_ref).start()
        red.tick(2 + i)
        return carry

    lax.fori_loop(0, blocks, grad_step, 0)
    for i in (blocks - 2, blocks - 1):
        dgu_out(i).wait()
    dgu_tile(0).start()
    hid_rows(0).start()
    loads[4].wait()

    def pair_tile(k):
        @pl.when(k + 1 < 2 * down_tiles)
        def _():
            dgu_tile(k + 1).start()

        dgu_tile(k).wait()
        red.put(down_tiles + k, dot(h2_v[...], tile_v[k % 2], 0, 0))
        red.tick(down_tiles + 1 + k)

    def ffn_step(k, carry):
        @pl.when(k + 1 < blocks)
        def _():
            hid_rows(k + 1).start()

        hid_rows(k).wait()
        i = blocks + k

        @pl.when(k < 2)
        def _():
            row_own(i - 2, dh2_own_ref).wait()
            row_send(i - 2, dh2_got_ref).wait_send()

        @pl.when(k >= 2)
        def _():
            row_own(i - 2, ffn_own_ref).wait()
            row_send(i - 2, ffn_got_ref).wait_send()

        row_v[k % 2] = dot(hid_v[k % 2], down_v[...], 1, 0).astype(BF)
        row_own(i, ffn_own_ref).start()
        row_send(i, ffn_got_ref).start()
        pair_tile(k)
        return carry

    lax.fori_loop(0, blocks, ffn_step, 0)

    def tail_step(k, carry):
        pair_tile(k)
        return carry

    lax.fori_loop(blocks, 2 * down_tiles, tail_step, 0)

    def drain_step(n, carry):
        red.tick(n)
        return carry

    lax.fori_loop(count + 1, count + 10, drain_step, 0)
    for i in range(blocks):
        row_send(i, dh2_got_ref).wait_recv()
    for i in range(blocks, 2 * blocks):
        row_send(i, ffn_got_ref).wait_recv()
    for i in (2 * blocks - 2, 2 * blocks - 1):
        row_own(i, ffn_own_ref).wait()
        row_send(i, ffn_got_ref).wait_send()


def ffn_backward(hid, slope, silu, h2, dy, gate_w, up_w, down_w):
    rows, hidden = hid.shape
    width = h2.shape[1]
    count = 3 * hidden // TILE_COLS
    blocks = rows // BLOCK
    any_spec = pl.BlockSpec(memory_space=pl.ANY)
    dma = pltpu.SemaphoreType.DMA
    shape = jax.ShapeDtypeStruct
    return pl.pallas_call(
        ffn_kernel,
        out_shape=(
            shape((TILE_ROWS, count * TILE_COLS), BF),
            shape((rows, 2 * hidden), BF),
            shape((rows, width), BF),
            shape((rows, width), BF),
            shape((rows, width), BF),
            shape((rows, width), BF),
        ),
        in_specs=[any_spec] * 8,
        out_specs=(any_spec,) * 6,
        scratch_shapes=[
            pltpu.VMEM((rows, width), BF),
            pltpu.VMEM((rows, width), BF),
            pltpu.VMEM(gate_w.shape, BF),
            pltpu.VMEM(up_w.shape, BF),
            pltpu.VMEM(down_w.shape, BF),
            pltpu.VMEM((2, rows, TILE_COLS), BF),
            pltpu.VMEM((2, BLOCK, hidden), BF),
            pltpu.VMEM((2, BLOCK, hidden), BF),
            pltpu.VMEM((2, BLOCK, 2 * hidden), BF),
            pltpu.VMEM((2, BLOCK, width), BF),
            pltpu.VMEM((2, BLOCK, hidden), BF),
            pltpu.VMEM((SLOTS, TILE_ROWS, TILE_COLS), BF),
            pltpu.VMEM((SLOTS, TILE_ROWS, TILE_COLS), BF),
            pltpu.VMEM((SLOTS, TILE_ROWS // 2, TILE_COLS), BF),
            pltpu.VMEM((SLOTS, TILE_ROWS // 4, TILE_COLS), BF),
            pltpu.VMEM((SLOTS, TILE_ROWS // 8, TILE_COLS), BF),
            pltpu.VMEM((SLOTS, TILE_ROWS // 16, TILE_COLS), BF),
            dma((5,)),
            dma((2,)),
            dma((2, 2)),
            dma((2,)),
            dma((2,)),
            dma((2,)),
            dma((2,)),
            dma((2 * blocks,)),
            dma((SLOTS, 8)),
            dma((SLOTS, 8)),
            dma((SLOTS,)),
        ],
        compiler_params=pltpu.CompilerParams(
            collective_id=1, has_side_effects=True, vmem_limit_bytes=VMEM_BYTES
        ),
    )(hid, slope, silu, h2, dy, gate_w, up_w, down_w)


def fetch_other(weight, core, count):
    half = weight.shape[0] // 2
    mine = lax.dynamic_slice_in_dim(weight, core * half, half, 0)
    got = swap_tensor(mine)
    rest = swap_core(got, count)
    low = jnp.where(core == 0, got, rest)
    high = jnp.where(core == 0, rest, got)
    return jnp.concatenate([low, high], 0)


def pair_body(
    tokens,
    cotangent,
    lengths,
    mixer_gain,
    in_weight,
    conv_weight,
    out_weight,
    ffn_gain,
    gate_weight,
    up_weight,
    down_weight,
):
    rows, width = tokens.shape
    count = lax.axis_size("dp")
    core = lax.axis_index("dp") % 2
    side = lax.axis_index("tensor")
    half = out_weight.shape[0]
    in_flat = in_weight.reshape(width, 3 * half)
    in_other = fetch_other(in_flat, core, count).reshape(width, 3, half)
    out_other = fetch_other(out_weight, core, count)
    taps_other = swap_tensor(conv_weight)

    def ordered(own, other, axis):
        return jnp.concatenate(
            [jnp.where(side == 0, own, other), jnp.where(side == 0, other, own)], axis
        )

    in_full = ordered(in_weight, in_other, 2).reshape(width, 6 * half)
    out_full = ordered(out_weight, out_other, 0)
    taps = ordered(conv_weight, taps_other, 1).astype(F32)
    full = 2 * half

    dist = distances(lengths[0], rows)
    keep_one = (dist >= 1)[:, None].astype(F32)
    keep_two = (dist >= 2)[:, None].astype(F32)
    x = tokens.astype(F32)
    dy = cotangent.astype(F32)
    g1 = mixer_gain.astype(F32)
    g2 = ffn_gain.astype(F32)
    scale1 = rms_scale(x)
    normed1 = x * scale1
    h1b = (normed1 * g1).astype(BF)
    proj = dot(h1b, in_full, 1, 0)
    b_part, c_part, x_part = (proj[:, :full], proj[:, full : 2 * full], proj[:, 2 * full :])
    mixed = b_part * x_part
    mixed_one = shift_down(mixed, 1, keep_one)
    mixed_two = shift_down(mixed, 2, keep_two)
    conv_out = taps[0] * mixed + taps[1] * mixed_one + taps[2] * mixed_two
    zb = (c_part * conv_out).astype(BF)
    resid = x + dot(zb, out_full, 1, 0)
    scale2 = rms_scale(resid)
    normed2 = resid * scale2
    h2b = (normed2 * g2).astype(BF)

    hidb, slope, silu = swiglu(h2b, gate_weight, up_weight)
    sums, _, dh2_own, dh2_got, ffn_own, ffn_got = ffn_backward(
        hidb, slope, silu, h2b, cotangent, gate_weight, up_weight, down_weight
    )
    hidden = gate_weight.shape[1]
    down_sum = sums[:, :hidden].T
    gate_sum = sums[:, hidden : 2 * hidden]
    up_sum = sums[:, 2 * hidden :]

    dh2 = dh2_own.astype(F32) + dh2_got.astype(F32)
    d_resid, g2_grad = norm_back(dh2, normed2, scale2, g2)
    dr1 = dy + d_resid
    dr1b = dr1.astype(BF)
    own = lambda v, axis: lax.dynamic_slice_in_dim(v, side * half, half, axis)
    out_grad = dot(own(zb, 1), dr1b, 0, 0).astype(BF)
    d_z = dot(dr1b, out_full, 1, 1)
    d_c = d_z * conv_out
    d_conv = d_z * c_part
    d_own = own(d_conv, 1)
    conv_grad = jnp.stack(
        [
            jnp.sum(d_own * own(mixed, 1), axis=0),
            jnp.sum(d_own * own(mixed_one, 1), axis=0),
            jnp.sum(d_own * own(mixed_two, 1), axis=0),
        ],
        0,
    )
    d_mixed = (
        taps[0] * d_conv
        + taps[1] * shift_up(d_conv * keep_one, 1)
        + taps[2] * shift_up(d_conv * keep_two, 2)
    )
    d_b = (d_mixed * x_part).astype(BF)
    d_c = d_c.astype(BF)
    d_x = (d_mixed * b_part).astype(BF)
    in_grad = jnp.stack(
        [dot(h1b, own(d_b, 1), 0, 0), dot(h1b, own(d_c, 1), 0, 0), dot(h1b, own(d_x, 1), 0, 0)], 1
    ).astype(BF)
    d_proj = jnp.concatenate([d_b, d_c, d_x], 1)
    dh1 = dot(d_proj, in_full, 1, 1)
    d_input, g1_grad = norm_back(dh1, normed1, scale1, g1)
    input_grad = (dr1 + d_input).astype(BF)
    output = (resid + (ffn_own.astype(F32) + ffn_got.astype(F32))).astype(BF)
    in_sum, out_sum = lax.psum((in_grad, out_grad), "dp")
    g1_sum, conv_sum, g2_sum = lax.psum((g1_grad, conv_grad, g2_grad), "dp")
    return (
        output,
        input_grad,
        g1_sum,
        in_sum.astype(F32),
        conv_sum,
        out_sum.astype(F32),
        g2_sum,
        gate_sum.astype(F32),
        up_sum.astype(F32),
        down_sum.astype(F32),
    )


def body(
    tokens,
    cotangent,
    lengths,
    mixer_gain,
    in_weight,
    conv_weight,
    out_weight,
    ffn_gain,
    gate_weight,
    up_weight,
    down_weight,
):
    rows = tokens.shape[0]
    dist = distances(lengths[0], rows)
    keep_one = (dist >= 1)[:, None].astype(jnp.float32)
    keep_two = (dist >= 2)[:, None].astype(jnp.float32)
    parts = lax.axis_size("tensor")
    share = rows // parts
    first = lax.axis_index("tensor") * share
    x = tokens.astype(jnp.float32)
    dy = cotangent.astype(jnp.float32)
    g1 = mixer_gain.astype(jnp.float32)
    g2 = ffn_gain.astype(jnp.float32)
    taps = conv_weight.astype(jnp.float32)
    scale1 = rms_scale(x)
    normed1 = x * scale1
    h1b = (normed1 * g1).astype(jnp.bfloat16)
    proj = jnp.einsum("td,dkc->tkc", h1b, in_weight, preferred_element_type=jnp.float32)
    b_part, c_part, x_part = (proj[:, 0], proj[:, 1], proj[:, 2])
    mixed = b_part * x_part
    mixed_one = shift_down(mixed, 1, keep_one)
    mixed_two = shift_down(mixed, 2, keep_two)
    conv_out = taps[0] * mixed + taps[1] * mixed_one + taps[2] * mixed_two
    zb = (c_part * conv_out).astype(jnp.bfloat16)
    mix_part = jnp.dot(zb, out_weight, preferred_element_type=jnp.float32)
    mix_rows = lax.psum_scatter(mix_part, "tensor", scatter_dimension=0, tiled=True)
    x_rows = lax.dynamic_slice_in_dim(x, first, share, 0)
    resid = x_rows + mix_rows
    scale2 = rms_scale(resid)
    normed2 = resid * scale2
    h2b = lax.all_gather((normed2 * g2).astype(jnp.bfloat16), "tensor", axis=0, tiled=True)
    gate = jnp.dot(h2b, gate_weight, preferred_element_type=jnp.float32)
    up = jnp.dot(h2b, up_weight, preferred_element_type=jnp.float32)
    sig = jax.nn.sigmoid(gate)
    silu = gate * sig
    hidb = (silu * up).astype(jnp.bfloat16)
    ffn_part = jnp.dot(hidb, down_weight, preferred_element_type=jnp.float32)
    down_grad = jnp.einsum("tf,td->fd", hidb, cotangent, preferred_element_type=jnp.float32)
    d_hid = jnp.einsum("td,fd->tf", cotangent, down_weight, preferred_element_type=jnp.float32)
    d_gate = (d_hid * up * sig * (1.0 + gate * (1.0 - sig))).astype(jnp.bfloat16)
    d_up = (d_hid * silu).astype(jnp.bfloat16)
    gate_grad = jnp.einsum("td,tf->df", h2b, d_gate, preferred_element_type=jnp.float32)
    up_grad = jnp.einsum("td,tf->df", h2b, d_up, preferred_element_type=jnp.float32)
    dh2_part = jnp.einsum("tf,df->td", d_gate, gate_weight, preferred_element_type=jnp.float32)
    dh2_part = dh2_part + jnp.einsum(
        "tf,df->td", d_up, up_weight, preferred_element_type=jnp.float32
    )
    ffn_rows = lax.psum_scatter(
        ffn_part.astype(jnp.bfloat16), "tensor", scatter_dimension=0, tiled=True
    ).astype(jnp.float32)
    output = lax.all_gather((resid + ffn_rows).astype(jnp.bfloat16), "tensor", axis=0, tiled=True)
    dh2_rows = lax.psum_scatter(dh2_part, "tensor", scatter_dimension=0, tiled=True)
    d_resid, g2_grad = norm_back(dh2_rows, normed2, scale2, g2)
    dr1 = lax.dynamic_slice_in_dim(dy, first, share, 0) + d_resid
    dr1b = lax.all_gather(dr1.astype(jnp.bfloat16), "tensor", axis=0, tiled=True)
    out_grad = jnp.einsum("tc,td->cd", zb, dr1b, preferred_element_type=jnp.float32)
    d_z = jnp.einsum("td,cd->tc", dr1b, out_weight, preferred_element_type=jnp.float32)
    d_c = d_z * conv_out
    d_conv = d_z * c_part
    conv_grad = jnp.stack(
        [
            jnp.sum(d_conv * mixed, axis=0),
            jnp.sum(d_conv * mixed_one, axis=0),
            jnp.sum(d_conv * mixed_two, axis=0),
        ],
        0,
    )
    d_mixed = (
        taps[0] * d_conv
        + taps[1] * shift_up(d_conv * keep_one, 1)
        + taps[2] * shift_up(d_conv * keep_two, 2)
    )
    d_proj = jnp.stack([d_mixed * x_part, d_c, d_mixed * b_part], 1).astype(jnp.bfloat16)
    in_grad_w = jnp.einsum("td,tkc->dkc", h1b, d_proj, preferred_element_type=jnp.float32)
    dh1_part = jnp.einsum("tkc,dkc->td", d_proj, in_weight, preferred_element_type=jnp.float32)
    dh1_rows = lax.psum_scatter(dh1_part, "tensor", scatter_dimension=0, tiled=True)
    normed1_rows = lax.dynamic_slice_in_dim(normed1, first, share, 0)
    scale1_rows = lax.dynamic_slice_in_dim(scale1, first, share, 0)
    d_input, g1_grad = norm_back(dh1_rows, normed1_rows, scale1_rows, g1)
    input_grad = lax.all_gather((dr1 + d_input).astype(jnp.bfloat16), "tensor", axis=0, tiled=True)
    g1_grad, g2_grad = lax.psum((g1_grad, g2_grad), "tensor")
    summed = lax.psum(
        (g1_grad, in_grad_w, conv_grad, out_grad, g2_grad, gate_grad, up_grad, down_grad), "dp"
    )
    return (
        output,
        input_grad,
        summed[0],
        summed[1],
        summed[2],
        summed[3],
        summed[4],
        summed[5],
        summed[6],
        summed[7],
    )


def solution(mesh):
    paired = mesh.shape["tensor"] == 2 and mesh.shape["dp"] == 16
    return jax.shard_map(
        pair_body if paired else body,
        mesh=mesh,
        in_specs=(
            P("dp", None),
            P("dp", None),
            P("dp", None),
            P(),
            P(None, None, "tensor"),
            P(None, "tensor"),
            P("tensor", None),
            P(),
            P(None, "tensor"),
            P(None, "tensor"),
            P("tensor", None),
        ),
        out_specs=(
            P("dp", None),
            P("dp", None),
            P(),
            P(None, None, "tensor"),
            P(None, "tensor"),
            P("tensor", None),
            P(),
            P(None, "tensor"),
            P(None, "tensor"),
            P("tensor", None),
        ),
        check_vma=False,
    )
```

```python
import jax
import jax.numpy as jnp
from jax import lax
from jax.experimental import pallas as pl
from jax.experimental.pallas import tpu as pltpu
from jax.sharding import PartitionSpec as P

EPS = 1e-05
F32 = jnp.float32
BF = jnp.bfloat16
MESH = pl.DeviceIdType.MESH
TILE_ROWS, TILE_COLS = 1024, 256
BLOCK = 256
SLOTS = 10
VMEM_BYTES = 63 << 20


def distances(lengths, count):
    ends = jnp.cumsum(lengths)
    starts = ends - lengths
    places = jnp.arange(count, dtype=jnp.int32)
    begin = jnp.max(jnp.where(starts[None, :] <= places[:, None], starts[None, :], 0), axis=1)
    return places - begin


def rms_scale(value):
    return lax.rsqrt(jnp.mean(value * value, axis=-1, keepdims=True) + EPS)


def shift_down(value, steps, keep):
    moved = jnp.concatenate([jnp.zeros_like(value[:steps]), value[:-steps]], 0)
    return moved * keep


def shift_up(value, steps):
    return jnp.concatenate([value[steps:], jnp.zeros_like(value[:steps])], 0)


def norm_back(grad_in, normed, scale, gain):
    weighted = grad_in * gain
    inner = jnp.mean(weighted * normed, axis=-1, keepdims=True)
    return (scale * (weighted - normed * inner), jnp.sum(grad_in * normed, axis=0))


def dot(a, b, ca, cb):
    return lax.dot_general(a, b, (((ca,), (cb,)), ((), ())), preferred_element_type=F32)


def swap_tensor(value):
    return lax.ppermute(value, "tensor", [(0, 1), (1, 0)])


def swap_core(value, count):
    return lax.ppermute(value, "dp", [(i, i ^ 1) for i in range(count)])


def block_keeps(lengths_ref, first, count):
    place = first + lax.broadcasted_iota(jnp.int32, (count, 1), 0)
    one = place != 0
    two = (place != 0) & (place != 1)
    start = 0
    for j in range(lengths_ref.shape[1] - 1):
        start = start + lengths_ref[0, j]
        one = one & (place != start)
        two = two & (place != start) & (place != start + 1)
    return one, two


def mixer_kernel(
    lengths_ref,
    x_ref,
    gain1_ref,
    in_ref,
    taps_ref,
    out_ref,
    gain2_ref,
    h1_ref,
    keep_ref,
    z_ref,
    resid_ref,
    h2_ref,
    last,
):
    i = pl.program_id(0)
    count, width = x_ref.shape

    @pl.when(i == 0)
    def _():
        last[...] = jnp.zeros_like(last)

    x = x_ref[...].astype(F32)
    h1 = (x * rms_scale(x) * gain1_ref[...].astype(F32)).astype(BF)
    h1_ref[...] = h1
    b_part = dot(h1, in_ref[:, :width], 1, 0)
    x_part = dot(h1, in_ref[:, 2 * width :], 1, 0)
    keep_ref[:, :width] = b_part.astype(BF)
    keep_ref[:, 2 * width : 3 * width] = x_part.astype(BF)
    m = b_part * x_part
    one, two = block_keeps(lengths_ref, i * count, count)
    row = lax.broadcasted_iota(jnp.int32, (count, 1), 0)
    m_one = jnp.where(row == 0, last[7:8, :], pltpu.roll(m, 1, 0))
    m_two = jnp.where(row == 0, last[6:7, :], jnp.where(row == 1, last[7:8, :], pltpu.roll(m, 2, 0)))
    last[...] = m[count - 8 :, :]
    taps = taps_ref[...].astype(F32)
    v = taps[0:1] * m + taps[1:2] * jnp.where(one, m_one, 0.0) + taps[2:3] * jnp.where(two, m_two, 0.0)
    keep_ref[:, 3 * width :] = v.astype(BF)
    c_part = dot(h1, in_ref[:, width : 2 * width], 1, 0)
    keep_ref[:, width : 2 * width] = c_part.astype(BF)
    z = (c_part * v).astype(BF)
    z_ref[...] = z
    resid = x + dot(z, out_ref[...], 1, 0)
    resid_ref[...] = resid
    h2_ref[...] = (resid * rms_scale(resid) * gain2_ref[...].astype(F32)).astype(BF)


def mixer_forward(lengths, x, gain1, in_full, taps, out_full, gain2):
    rows, width = x.shape
    block = pl.BlockSpec((BLOCK, width), lambda i: (i, 0))

    def whole(shape):
        return pl.BlockSpec(shape, lambda i: (0, 0), pipeline_mode=pl.Buffered(1))

    low = jax.ShapeDtypeStruct((rows, width), BF)
    return pl.pallas_call(
        mixer_kernel,
        grid=(rows // BLOCK,),
        out_shape=(
            low,
            jax.ShapeDtypeStruct((rows, 4 * width), BF),
            low,
            jax.ShapeDtypeStruct((rows, width), F32),
            low,
        ),
        in_specs=[
            pl.BlockSpec(memory_space=pltpu.SMEM),
            block,
            whole((1, width)),
            whole(in_full.shape),
            whole(taps.shape),
            whole(out_full.shape),
            whole((1, width)),
        ],
        out_specs=(block, pl.BlockSpec((BLOCK, 4 * width), lambda i: (i, 0)), block, block, block),
        scratch_shapes=[pltpu.VMEM((8, width), F32)],
        compiler_params=pltpu.CompilerParams(vmem_limit_bytes=VMEM_BYTES),
    )(lengths, x, gain1.reshape(1, width), in_full, taps, out_full, gain2.reshape(1, width))


def swiglu_kernel(h2_ref, gate_ref, up_ref, hid_ref, slope_ref, silu_ref):
    h2 = h2_ref[...]
    gate = dot(h2, gate_ref[...], 1, 0)
    up = dot(h2, up_ref[...], 1, 0)
    sig = jax.nn.sigmoid(gate)
    silu = gate * sig
    hid_ref[...] = (silu * up).astype(BF)
    slope_ref[...] = (up * sig * (1.0 + gate * (1.0 - sig))).astype(BF)
    silu_ref[...] = silu.astype(BF)


def swiglu(h2, gate_w, up_w):
    rows, width = h2.shape
    hidden = gate_w.shape[1]
    out = jax.ShapeDtypeStruct((rows, hidden), BF)
    row_spec = pl.BlockSpec((BLOCK, hidden), lambda i: (i, 0))
    whole = pl.BlockSpec((width, hidden), lambda i: (0, 0), pipeline_mode=pl.Buffered(1))
    return pl.pallas_call(
        swiglu_kernel,
        grid=(rows // BLOCK,),
        out_shape=(out, out, out),
        in_specs=[pl.BlockSpec((BLOCK, width), lambda i: (i, 0)), whole, whole],
        out_specs=(row_spec, row_spec, row_spec),
        compiler_params=pltpu.CompilerParams(vmem_limit_bytes=VMEM_BYTES),
    )(h2, gate_w, up_w)


class Reducer:
    def __init__(self, count, tiles, parts, whole, send, recv, out_ref, out_sem):
        self.count, self.slots = count, tiles.shape[0]
        self.tiles, self.parts, self.whole = tiles, parts, whole
        self.send, self.recv = send, recv
        self.out_ref, self.out_sem = out_ref, out_sem
        self.me = lax.axis_index("dp")
        self.side = lax.axis_index("tensor")

    def plan(self, n):
        me = self.me
        bit = [me % 2, (me // 2) % 2, (me // 4) % 2, (me // 8) % 2]
        swap = (n % 4) == 3
        mine = [bit[0], jnp.where(swap, bit[2], bit[1]), jnp.where(swap, bit[1], bit[2]), bit[3]]
        step = [1, jnp.where(swap, 4, 2), jnp.where(swap, 2, 4), 8]
        peer = [me + s * (1 - 2 * b) for s, b in zip(step, mine)]
        keep, off = [], 0
        give = []
        for s in range(4):
            size = TILE_ROWS >> (s + 1)
            give.append(pl.multiple_of(off + (1 - mine[s]) * size, size))
            off = off + mine[s] * size
            keep.append(pl.multiple_of(off, size))
        return peer, keep, give

    def scatter(self, n, s):
        peer, keep, give = self.plan(n)
        slot = n % self.slots
        size = TILE_ROWS >> (s + 1)
        return pltpu.make_async_remote_copy(
            src_ref=self.tiles.at[slot, pl.ds(give[s], size)],
            dst_ref=self.parts[s].at[slot],
            send_sem=self.send.at[slot, s],
            recv_sem=self.recv.at[slot, s],
            device_id=(peer[s], self.side),
            device_id_type=MESH,
        )

    def gather(self, n, s):
        peer, keep, give = self.plan(n)
        slot = n % self.slots
        size = TILE_ROWS >> (s + 1)
        block = self.whole.at[slot, pl.ds(keep[s], size)]
        return pltpu.make_async_remote_copy(
            src_ref=block,
            dst_ref=block,
            send_sem=self.send.at[slot, 4 + s],
            recv_sem=self.recv.at[slot, 4 + s],
            device_id=(peer[s], self.side),
            device_id_type=MESH,
        )

    def write(self, n):
        slot = n % self.slots
        column = pl.multiple_of(n * TILE_COLS, TILE_COLS)
        return pltpu.make_async_copy(
            self.whole.at[slot], self.out_ref.at[:, pl.ds(column, TILE_COLS)], self.out_sem.at[slot]
        )

    def add(self, n, s):
        peer, keep, give = self.plan(n)
        slot = n % self.slots
        size = TILE_ROWS >> (s + 1)
        rows = pl.ds(keep[s], size)
        total = self.tiles[slot, rows, :].astype(F32) + self.parts[s][slot].astype(F32)
        into = self.whole if s == 3 else self.tiles
        into[slot, rows, :] = total.astype(BF)

    def put(self, n, value):
        self.tiles[n % self.slots] = value.astype(BF)
        self.scatter(n, 0).start()

    def tick(self, n):
        def stage(k):
            m = n - k

            @pl.when((m >= 0) & (m < self.count))
            def _():
                if k <= 4:
                    self.scatter(m, k - 1).wait()
                    self.add(m, k - 1)
                    if k < 4:
                        self.scatter(m, k).start()
                    else:
                        self.gather(m, 3).start()
                elif k <= 8:
                    self.gather(m, 8 - k).wait()
                    if k < 8:
                        self.gather(m, 7 - k).start()
                    else:
                        self.write(m).start()
                else:
                    self.write(m).wait()

        for k in (1, 6, 2, 3, 4, 5, 7, 8, 9):
            stage(k)


def back_kernel(
    lengths_ref,
    hid_ref,
    slope_ref,
    silu_ref,
    h2_ref,
    dy_ref,
    gate_ref,
    up_ref,
    down_ref,
    resid_ref,
    x_ref,
    keep_ref,
    z_ref,
    h1_ref,
    in_ref,
    out_ref,
    gain1_ref,
    gain2_ref,
    taps_ref,
    sums_ref,
    dgu_ref,
    dh2_own_ref,
    dh2_got_ref,
    ffn_own_ref,
    ffn_got_ref,
    dp_ref,
    grad_ref,
    result_ref,
    small_ref,
    dy_v,
    h2_v,
    wide_v,
    down_v,
    tile_v,
    row_v,
    small_v,
    small_in,
    next_v,
    tiles,
    whole,
    part0,
    part1,
    part2,
    part3,
    load_sem,
    tile_sem,
    stream_sem,
    dgu_sem,
    own_sem,
    hid_sem,
    dp_sem,
    grad_sem,
    small_send,
    small_recv,
    x_send,
    x_recv,
    send,
    recv,
    out_sem,
):
    me, side = lax.axis_index("dp"), lax.axis_index("tensor")
    rows, width = dy_v.shape
    hidden = hid_ref.shape[1]
    half = width // 2
    blocks = rows // BLOCK
    n_down = hidden // TILE_COLS
    n_out = half // TILE_COLS
    first_gate, first_out = n_down, 3 * n_down
    first_in = first_out + n_out
    count = first_in + 3 * n_out
    red = Reducer(count, tiles, (part0, part1, part2, part3), whole, send, recv, sums_ref, out_sem)

    def peer(bit):
        return me + bit * (1 - 2 * ((me // bit) % 2))

    def block_rows(i):
        return pl.ds(pl.multiple_of((blocks - 1 - i) * BLOCK, BLOCK), BLOCK)

    load_dy = pltpu.make_async_copy(dy_ref, dy_v, load_sem.at[0])
    load_down = pltpu.make_async_copy(down_ref, down_v, load_sem.at[1])
    load_gate = pltpu.make_async_copy(gate_ref, wide_v.at[:, pl.ds(0, hidden)], load_sem.at[2])
    load_up = pltpu.make_async_copy(up_ref, wide_v.at[:, pl.ds(hidden, hidden)], load_sem.at[3])
    load_h2 = pltpu.make_async_copy(h2_ref, h2_v, load_sem.at[4])
    load_in = pltpu.make_async_copy(in_ref, wide_v.at[:, pl.ds(0, 3 * width)], load_sem.at[2])
    load_out = pltpu.make_async_copy(out_ref, wide_v.at[:, pl.ds(3 * width, width)], load_sem.at[3])
    load_h1 = pltpu.make_async_copy(h1_ref, h2_v, load_sem.at[4])

    def tile_of(ref, column, n):
        column = pl.multiple_of(column, TILE_COLS)
        return pltpu.make_async_copy(
            ref.at[:, pl.ds(column, TILE_COLS)], tile_v.at[n % 2], tile_sem.at[n % 2]
        )

    def hid_tile(n):
        return tile_of(hid_ref, n * TILE_COLS, n)

    def dgu_tile(n):
        return tile_of(dgu_ref, (n - first_gate) * TILE_COLS, n)

    def z_tile(n):
        return tile_of(z_ref, side * half + (n - first_out) * TILE_COLS, n)

    def dp_tile(n):
        return tile_of(dp_ref, (n - first_in) * TILE_COLS, n)

    def row_own(i, ref):
        return pltpu.make_async_copy(row_v.at[i % 2], ref.at[block_rows(i % blocks)], own_sem.at[i % 2])

    def row_send(i, own, got):
        at = block_rows(i % blocks)
        return pltpu.make_async_remote_copy(
            src_ref=own.at[at],
            dst_ref=got.at[at],
            send_sem=x_send.at[i],
            recv_sem=x_recv.at[i],
            device_id=(me, 1 - side),
            device_id_type=MESH,
        )

    def dh2_send(i):
        return row_send(i, dh2_own_ref, dh2_got_ref)

    def ffn_send(i):
        return row_send(blocks + i, ffn_own_ref, ffn_got_ref)

    def small_copy(s):
        return pltpu.make_async_remote_copy(
            src_ref=small_v,
            dst_ref=small_in.at[s],
            send_sem=small_send.at[s],
            recv_sem=small_recv.at[s],
            device_id=(peer(1 << s), side),
            device_id_type=MESH,
        )

    def small_add(s):
        small_copy(s).wait()
        small_v[...] = small_v[...] + small_in[s]

    load_dy.start()
    hid_tile(0).start()
    load_down.start()
    load_gate.start()
    load_up.start()
    load_h2.start()

    barrier = pltpu.get_barrier_semaphore()
    for bit in (1, 2, 4, 8):
        pl.semaphore_signal(barrier, inc=1, device_id=(peer(bit), side), device_id_type=MESH)
    pl.semaphore_signal(barrier, inc=1, device_id=(me, 1 - side), device_id_type=MESH)
    pl.semaphore_wait(barrier, 5)

    small_v[...] = jnp.zeros_like(small_v)
    next_v[...] = jnp.zeros_like(next_v)

    def down_step(n, carry):
        @pl.when(n + 1 < n_down)
        def _():
            hid_tile(n + 1).start()

        hid_tile(n).wait()
        red.put(n, dot(dy_v[...], tile_v[n % 2], 0, 0))
        return carry

    def grads(slope_v, silu_v, dgu_v):
        def pair(i):
            at = block_rows(i)
            return (
                pltpu.make_async_copy(slope_ref.at[at], slope_v.at[i % 2], stream_sem.at[i % 2, 0]),
                pltpu.make_async_copy(silu_ref.at[at], silu_v.at[i % 2], stream_sem.at[i % 2, 1]),
            )

        def dgu_out(i):
            return pltpu.make_async_copy(
                dgu_v.at[i % 2], dgu_ref.at[block_rows(i)], dgu_sem.at[i % 2]
            )

        for copy in pair(0):
            copy.start()
        load_dy.wait()
        lax.fori_loop(0, 3, down_step, 0)
        red.tick(1)
        lax.fori_loop(3, n_down, down_step, 0)
        load_down.wait()
        load_gate.wait()
        load_up.wait()

        def grad_step(i, carry):
            slot = i % 2

            @pl.when(i + 1 < blocks)
            def _():
                for copy in pair(i + 1):
                    copy.start()

            for copy in pair(i):
                copy.wait()

            @pl.when(i >= 2)
            def _():
                dgu_out(i - 2).wait()

            d_hid = dot(dy_v[block_rows(i), :], down_v[...], 1, 1)
            dgu_v[slot, :, :hidden] = (d_hid * slope_v[slot].astype(F32)).astype(BF)
            dgu_v[slot, :, hidden:] = (d_hid * silu_v[slot].astype(F32)).astype(BF)
            dgu_out(i).start()
            row_v[slot] = dot(dgu_v[slot], wide_v[...], 1, 1).astype(BF)
            row_own(i, dh2_own_ref).start()
            red.tick(2 + i)
            row_own(i, dh2_own_ref).wait()
            dh2_send(i).start()
            return carry

        lax.fori_loop(0, blocks, grad_step, 0)
        load_in.start()
        load_out.start()
        for i in (blocks - 2, blocks - 1):
            dgu_out(i).wait()
        dgu_tile(first_gate).start()

    pl.run_scoped(
        grads,
        pltpu.VMEM((2, BLOCK, hidden), BF),
        pltpu.VMEM((2, BLOCK, hidden), BF),
        pltpu.VMEM((2, BLOCK, 2 * hidden), BF),
    )

    def gate_put(n):
        dgu_tile(n).wait()
        red.put(n, dot(h2_v[...], tile_v[n % 2], 0, 0))

    def mixer(keep_v, resid_v, x_v, pair_v, hid_v, dp_v, grad_v):
        def hid_rows(i):
            return pltpu.make_async_copy(hid_ref.at[block_rows(i)], hid_v.at[i % 2], hid_sem.at[i % 2])

        def inputs(i):
            at, slot = block_rows(i), i % 2
            return (
                pltpu.make_async_copy(keep_ref.at[at], keep_v.at[slot], stream_sem.at[slot, 0]),
                pltpu.make_async_copy(resid_ref.at[at], resid_v.at[slot], stream_sem.at[slot, 1]),
                pltpu.make_async_copy(x_ref.at[at], x_v.at[slot], stream_sem.at[slot, 2]),
                pltpu.make_async_copy(dh2_own_ref.at[at], pair_v.at[0], stream_sem.at[slot, 3]),
            )

        def got(i):
            return pltpu.make_async_copy(dh2_got_ref.at[block_rows(i)], pair_v.at[1], dgu_sem.at[0])

        def dp_out(i):
            at = block_rows(i)
            return [
                pltpu.make_async_copy(
                    dp_v.at[:, pl.ds(pl.multiple_of(k * width + side * half, half), half)],
                    dp_ref.at[at, pl.ds(k * half, half)],
                    dp_sem.at[k],
                )
                for k in range(3)
            ]

        def grad_out(i):
            return pltpu.make_async_copy(grad_v, grad_ref.at[block_rows(i)], grad_sem)

        def finish(i):
            for copy in dp_out(i):
                copy.wait()
            grad_out(i).wait()

        def mixer_block(i):
            slot = i % 2
            at = block_rows(i)
            for copy in inputs(i):
                copy.wait()
            got(i).wait()

            @pl.when(i > 0)
            def _():
                finish(i - 1)

            resid = resid_v[slot]
            scale2 = rms_scale(resid)
            n2 = resid * scale2
            dh2 = pair_v[0].astype(F32) + pair_v[1].astype(F32)
            d_resid, gain2_part = norm_back(dh2, n2, scale2, gain2_ref[...].astype(F32))
            dr1 = dy_v[at, :].astype(F32) + d_resid
            dr1b = dr1.astype(BF)
            dy_v[at, :] = dr1b
            dz = dot(dr1b, wide_v[:, 3 * width : 4 * width], 1, 1)
            dc = dz * keep_v[slot, :, 3 * width :].astype(F32)
            dp_v[:, width : 2 * width] = dc.astype(BF)
            dv = dz * keep_v[slot, :, width : 2 * width].astype(F32)
            b_part = keep_v[slot, :, :width].astype(F32)
            x_part = keep_v[slot, :, 2 * width : 3 * width].astype(F32)
            m = b_part * x_part
            one, two = block_keeps(lengths_ref, (blocks - 1 - i) * BLOCK, BLOCK)
            row = lax.broadcasted_iota(jnp.int32, (BLOCK, 1), 0)
            dv_one = jnp.where(one, dv, 0.0)
            dv_two = jnp.where(two, dv, 0.0)
            up_one = jnp.where(row == BLOCK - 1, next_v[0:1, :], pltpu.roll(dv_one, BLOCK - 1, 0))
            up_two = jnp.where(
                row == BLOCK - 2,
                next_v[8:9, :],
                jnp.where(row == BLOCK - 1, next_v[9:10, :], pltpu.roll(dv_two, BLOCK - 2, 0)),
            )
            next_v[0:8, :] = dv_one[0:8]
            next_v[8:16, :] = dv_two[0:8]
            taps = taps_ref[...].astype(F32)
            dm = taps[0:1] * dv + taps[1:2] * up_one + taps[2:3] * up_two
            dp_v[:, :width] = (dm * x_part).astype(BF)
            dp_v[:, 2 * width :] = (dm * b_part).astype(BF)
            for copy in dp_out(i):
                copy.start()
            dh1 = dot(dp_v[...], wide_v[:, : 3 * width], 1, 1)
            x = x_v[slot].astype(F32)
            scale1 = rms_scale(x)
            d_input, gain1_part = norm_back(dh1, x * scale1, scale1, gain1_ref[...].astype(F32))
            grad_v[...] = (dr1 + d_input).astype(BF)
            grad_out(i).start()
            small_v[0:1, :] += gain1_part.reshape(1, width)
            small_v[1:2, :] += gain2_part.reshape(1, width)
            small_v[2:3, :] += jnp.sum(dv * m, axis=0, keepdims=True)
            small_v[3:4, :] += jnp.sum(up_one * m, axis=0, keepdims=True)
            small_v[4:5, :] += jnp.sum(up_two * m, axis=0, keepdims=True)

        hid_rows(0).start()
        for copy in inputs(0):
            copy.start()
        load_h2.wait()
        load_in.wait()
        load_out.wait()

        def mixer_step(i, carry):
            n = first_gate + 2 * i
            dh2_send(i).wait_recv()
            got(i).start()
            dgu_tile(n + 1).start()
            gate_put(n)
            red.tick(n + 1)
            mixer_block(i)

            @pl.when(i + 1 < blocks)
            def _():
                hid_rows(i + 1).start()
                for copy in inputs(i + 1):
                    copy.start()

            hid_rows(i).wait()
            row_v[i % 2] = dot(hid_v[i % 2], down_v[...], 1, 0).astype(BF)
            row_own(i, ffn_own_ref).start()
            dgu_tile(n + 2).start()
            gate_put(n + 1)
            row_own(i, ffn_own_ref).wait()
            ffn_send(i).start()
            red.tick(n + 2)
            return carry

        lax.fori_loop(0, blocks, mixer_step, 0)
        finish(blocks - 1)

    pl.run_scoped(
        mixer,
        pltpu.VMEM((2, BLOCK, 4 * width), BF),
        pltpu.VMEM((2, BLOCK, width), F32),
        pltpu.VMEM((2, BLOCK, width), BF),
        pltpu.VMEM((2, BLOCK, width), BF),
        pltpu.VMEM((2, BLOCK, hidden), BF),
        pltpu.VMEM((BLOCK, 3 * width), BF),
        pltpu.VMEM((BLOCK, width), BF),
    )

    small_copy(0).start()

    def tail(resid_v, pair_v, result_v):
        def inputs(i):
            at = block_rows(i)
            return (
                pltpu.make_async_copy(resid_ref.at[at], resid_v, stream_sem.at[0, 0]),
                pltpu.make_async_copy(ffn_own_ref.at[at], pair_v.at[0], stream_sem.at[0, 1]),
                pltpu.make_async_copy(ffn_got_ref.at[at], pair_v.at[1], stream_sem.at[0, 2]),
            )

        def result_out(i):
            return pltpu.make_async_copy(result_v, result_ref.at[block_rows(i)], grad_sem)

        def post(p):
            i = p // 2

            @pl.when((p % 2 == 0) & (i < blocks))
            def _():
                ffn_send(i).wait_recv()
                for copy in inputs(i):
                    copy.start()

            @pl.when((p % 2 == 1) & (i < blocks))
            def _():
                for copy in inputs(i):
                    copy.wait()

                @pl.when(i > 0)
                def _():
                    result_out(i - 1).wait()

                both = pair_v[0].astype(F32) + pair_v[1].astype(F32)
                result_v[...] = (resid_v[...] + both).astype(BF)
                result_out(i).start()

        base = first_gate + 2 * blocks

        def step(n, put):
            put(n)
            red.tick(n + 1)
            post(n - base)

        for n in range(base, first_out):
            (dgu_tile if n + 1 < first_out else z_tile)(n + 1).start()
            step(n, gate_put)
        load_h1.start()
        small_add(0)
        small_copy(1).start()

        def out_put(n):
            z_tile(n).wait()
            red.put(n, dot(dy_v[...], tile_v[n % 2], 0, 0))

        for n in range(first_out, first_in):
            (z_tile if n + 1 < first_in else dp_tile)(n + 1).start()
            step(n, out_put)
        small_add(1)
        small_copy(2).start()
        load_h1.wait()

        def in_step(n, carry):
            @pl.when(n + 1 < count)
            def _():
                dp_tile(n + 1).start()

            def in_put(n):
                dp_tile(n).wait()
                red.put(n, dot(h2_v[...], tile_v[n % 2], 0, 0))

            step(n, in_put)
            return carry

        middle = (first_in + count) // 2
        lax.fori_loop(first_in, middle, in_step, 0)
        small_add(2)
        small_copy(3).start()
        lax.fori_loop(middle, count, in_step, 0)
        small_add(3)
        small_out = pltpu.make_async_copy(small_v, small_ref, load_sem.at[0])
        small_out.start()

        def drain_step(n, carry):
            red.tick(n + 1)
            post(n - base)
            return carry

        lax.fori_loop(count, count + 9, drain_step, 0)
        result_out(blocks - 1).wait()
        small_out.wait()
        for i in range(blocks):
            dh2_send(i).wait_send()
            ffn_send(i).wait_send()

    pl.run_scoped(
        tail,
        pltpu.VMEM((BLOCK, width), F32),
        pltpu.VMEM((2, BLOCK, width), BF),
        pltpu.VMEM((BLOCK, width), BF),
    )


def block_backward(
    lengths, hid, slope, silu, h2, dy, gate_w, up_w, down_w, resid, x, keep, z, h1, in_full, out_full,
    gain1, gain2, taps,
):
    rows, hidden = hid.shape
    width = h2.shape[1]
    count = (3 * hidden + 2 * width) // TILE_COLS
    blocks = rows // BLOCK
    any_spec = pl.BlockSpec(memory_space=pl.ANY)
    vmem_spec = pl.BlockSpec(memory_space=pltpu.VMEM)
    dma = pltpu.SemaphoreType.DMA
    shape = jax.ShapeDtypeStruct
    low = shape((rows, width), BF)
    ring = [pltpu.VMEM((SLOTS, TILE_ROWS, TILE_COLS), BF)]
    ring += [pltpu.VMEM((SLOTS, TILE_ROWS >> s, TILE_COLS), BF) for s in range(5)]
    return pl.pallas_call(
        back_kernel,
        out_shape=(
            shape((TILE_ROWS, count * TILE_COLS), BF),
            shape((rows, 2 * hidden), BF),
            low,
            low,
            low,
            low,
            shape((rows, 3 * width // 2), BF),
            low,
            low,
            shape((8, width), F32),
        ),
        in_specs=[pl.BlockSpec(memory_space=pltpu.SMEM)] + [any_spec] * 15 + [vmem_spec] * 3,
        out_specs=(any_spec,) * 10,
        scratch_shapes=[
            pltpu.VMEM((rows, width), BF),
            pltpu.VMEM((rows, width), BF),
            pltpu.VMEM((width, 2 * hidden), BF),
            pltpu.VMEM(down_w.shape, BF),
            pltpu.VMEM((2, rows, TILE_COLS), BF),
            pltpu.VMEM((2, BLOCK, width), BF),
            pltpu.VMEM((8, width), F32),
            pltpu.VMEM((4, 8, width), F32),
            pltpu.VMEM((16, width), F32),
            *ring,
            dma((5,)),
            dma((2,)),
            dma((2, 4)),
            dma((2,)),
            dma((2,)),
            dma((2,)),
            dma((3,)),
            dma,
            dma((4,)),
            dma((4,)),
            dma((2 * blocks,)),
            dma((2 * blocks,)),
            dma((SLOTS, 8)),
            dma((SLOTS, 8)),
            dma((SLOTS,)),
        ],
        compiler_params=pltpu.CompilerParams(
            collective_id=1, has_side_effects=True, vmem_limit_bytes=VMEM_BYTES
        ),
    )(
        lengths, hid, slope, silu, h2, dy, gate_w, up_w, down_w, resid, x, keep, z, h1, in_full, out_full,
        gain1.reshape(1, width), gain2.reshape(1, width), taps,
    )


def fetch_other(weight, core, count):
    half = weight.shape[0] // 2
    mine = lax.dynamic_slice_in_dim(weight, core * half, half, 0)
    got = swap_tensor(mine)
    rest = swap_core(got, count)
    low = jnp.where(core == 0, got, rest)
    high = jnp.where(core == 0, rest, got)
    return jnp.concatenate([low, high], 0)


def pair_body(
    tokens,
    cotangent,
    lengths,
    mixer_gain,
    in_weight,
    conv_weight,
    out_weight,
    ffn_gain,
    gate_weight,
    up_weight,
    down_weight,
):
    rows, width = tokens.shape
    count = lax.axis_size("dp")
    core = lax.axis_index("dp") % 2
    side = lax.axis_index("tensor")
    half = out_weight.shape[0]
    in_flat = in_weight.reshape(width, 3 * half)
    in_other = fetch_other(in_flat, core, count).reshape(width, 3, half)
    out_other = fetch_other(out_weight, core, count)
    taps_other = swap_tensor(conv_weight)

    def ordered(own, other, axis):
        return jnp.concatenate(
            [jnp.where(side == 0, own, other), jnp.where(side == 0, other, own)], axis
        )

    in_full = ordered(in_weight, in_other, 2).reshape(width, 6 * half)
    out_full = ordered(out_weight, out_other, 0)
    taps = ordered(conv_weight, taps_other, 1)
    full = 2 * half

    h1b, keep, zb, resid, h2b = mixer_forward(
        lengths, tokens, mixer_gain, in_full, taps, out_full, ffn_gain
    )
    hidb, slope, silu = swiglu(h2b, gate_weight, up_weight)
    sums, _, _, _, _, _, _, input_grad, output, small = block_backward(
        lengths, hidb, slope, silu, h2b, cotangent, gate_weight, up_weight, down_weight, resid, tokens,
        keep, zb, h1b, in_full, out_full, mixer_gain, ffn_gain, taps,
    )
    hidden = gate_weight.shape[1]

    def columns(first, size):
        return sums[:, first : first + size].astype(F32)

    return (
        output,
        input_grad,
        small[0],
        columns(3 * hidden + half, 3 * half).reshape(width, 3, half),
        lax.dynamic_slice_in_dim(small[2:5], side * half, half, 1),
        columns(3 * hidden, half).T,
        small[1],
        columns(hidden, hidden),
        columns(2 * hidden, hidden),
        columns(0, hidden).T,
    )


def body(
    tokens,
    cotangent,
    lengths,
    mixer_gain,
    in_weight,
    conv_weight,
    out_weight,
    ffn_gain,
    gate_weight,
    up_weight,
    down_weight,
):
    rows = tokens.shape[0]
    dist = distances(lengths[0], rows)
    keep_one = (dist >= 1)[:, None].astype(jnp.float32)
    keep_two = (dist >= 2)[:, None].astype(jnp.float32)
    parts = lax.axis_size("tensor")
    share = rows // parts
    first = lax.axis_index("tensor") * share
    x = tokens.astype(jnp.float32)
    dy = cotangent.astype(jnp.float32)
    g1 = mixer_gain.astype(jnp.float32)
    g2 = ffn_gain.astype(jnp.float32)
    taps = conv_weight.astype(jnp.float32)
    scale1 = rms_scale(x)
    normed1 = x * scale1
    h1b = (normed1 * g1).astype(jnp.bfloat16)
    proj = jnp.einsum("td,dkc->tkc", h1b, in_weight, preferred_element_type=jnp.float32)
    b_part, c_part, x_part = (proj[:, 0], proj[:, 1], proj[:, 2])
    mixed = b_part * x_part
    mixed_one = shift_down(mixed, 1, keep_one)
    mixed_two = shift_down(mixed, 2, keep_two)
    conv_out = taps[0] * mixed + taps[1] * mixed_one + taps[2] * mixed_two
    zb = (c_part * conv_out).astype(jnp.bfloat16)
    mix_part = jnp.dot(zb, out_weight, preferred_element_type=jnp.float32)
    mix_rows = lax.psum_scatter(mix_part, "tensor", scatter_dimension=0, tiled=True)
    x_rows = lax.dynamic_slice_in_dim(x, first, share, 0)
    resid = x_rows + mix_rows
    scale2 = rms_scale(resid)
    normed2 = resid * scale2
    h2b = lax.all_gather((normed2 * g2).astype(jnp.bfloat16), "tensor", axis=0, tiled=True)
    gate = jnp.dot(h2b, gate_weight, preferred_element_type=jnp.float32)
    up = jnp.dot(h2b, up_weight, preferred_element_type=jnp.float32)
    sig = jax.nn.sigmoid(gate)
    silu = gate * sig
    hidb = (silu * up).astype(jnp.bfloat16)
    ffn_part = jnp.dot(hidb, down_weight, preferred_element_type=jnp.float32)
    down_grad = jnp.einsum("tf,td->fd", hidb, cotangent, preferred_element_type=jnp.float32)
    d_hid = jnp.einsum("td,fd->tf", cotangent, down_weight, preferred_element_type=jnp.float32)
    d_gate = (d_hid * up * sig * (1.0 + gate * (1.0 - sig))).astype(jnp.bfloat16)
    d_up = (d_hid * silu).astype(jnp.bfloat16)
    gate_grad = jnp.einsum("td,tf->df", h2b, d_gate, preferred_element_type=jnp.float32)
    up_grad = jnp.einsum("td,tf->df", h2b, d_up, preferred_element_type=jnp.float32)
    dh2_part = jnp.einsum("tf,df->td", d_gate, gate_weight, preferred_element_type=jnp.float32)
    dh2_part = dh2_part + jnp.einsum(
        "tf,df->td", d_up, up_weight, preferred_element_type=jnp.float32
    )
    ffn_rows = lax.psum_scatter(
        ffn_part.astype(jnp.bfloat16), "tensor", scatter_dimension=0, tiled=True
    ).astype(jnp.float32)
    output = lax.all_gather((resid + ffn_rows).astype(jnp.bfloat16), "tensor", axis=0, tiled=True)
    dh2_rows = lax.psum_scatter(dh2_part, "tensor", scatter_dimension=0, tiled=True)
    d_resid, g2_grad = norm_back(dh2_rows, normed2, scale2, g2)
    dr1 = lax.dynamic_slice_in_dim(dy, first, share, 0) + d_resid
    dr1b = lax.all_gather(dr1.astype(jnp.bfloat16), "tensor", axis=0, tiled=True)
    out_grad = jnp.einsum("tc,td->cd", zb, dr1b, preferred_element_type=jnp.float32)
    d_z = jnp.einsum("td,cd->tc", dr1b, out_weight, preferred_element_type=jnp.float32)
    d_c = d_z * conv_out
    d_conv = d_z * c_part
    conv_grad = jnp.stack(
        [
            jnp.sum(d_conv * mixed, axis=0),
            jnp.sum(d_conv * mixed_one, axis=0),
            jnp.sum(d_conv * mixed_two, axis=0),
        ],
        0,
    )
    d_mixed = (
        taps[0] * d_conv
        + taps[1] * shift_up(d_conv * keep_one, 1)
        + taps[2] * shift_up(d_conv * keep_two, 2)
    )
    d_proj = jnp.stack([d_mixed * x_part, d_c, d_mixed * b_part], 1).astype(jnp.bfloat16)
    in_grad_w = jnp.einsum("td,tkc->dkc", h1b, d_proj, preferred_element_type=jnp.float32)
    dh1_part = jnp.einsum("tkc,dkc->td", d_proj, in_weight, preferred_element_type=jnp.float32)
    dh1_rows = lax.psum_scatter(dh1_part, "tensor", scatter_dimension=0, tiled=True)
    normed1_rows = lax.dynamic_slice_in_dim(normed1, first, share, 0)
    scale1_rows = lax.dynamic_slice_in_dim(scale1, first, share, 0)
    d_input, g1_grad = norm_back(dh1_rows, normed1_rows, scale1_rows, g1)
    input_grad = lax.all_gather((dr1 + d_input).astype(jnp.bfloat16), "tensor", axis=0, tiled=True)
    g1_grad, g2_grad = lax.psum((g1_grad, g2_grad), "tensor")
    summed = lax.psum(
        (g1_grad, in_grad_w, conv_grad, out_grad, g2_grad, gate_grad, up_grad, down_grad), "dp"
    )
    return (
        output,
        input_grad,
        summed[0],
        summed[1],
        summed[2],
        summed[3],
        summed[4],
        summed[5],
        summed[6],
        summed[7],
    )


def solution(mesh):
    paired = mesh.shape["tensor"] == 2 and mesh.shape["dp"] == 16
    return jax.shard_map(
        pair_body if paired else body,
        mesh=mesh,
        in_specs=(
            P("dp", None),
            P("dp", None),
            P("dp", None),
            P(),
            P(None, None, "tensor"),
            P(None, "tensor"),
            P("tensor", None),
            P(),
            P(None, "tensor"),
            P(None, "tensor"),
            P("tensor", None),
        ),
        out_specs=(
            P("dp", None),
            P("dp", None),
            P(),
            P(None, None, "tensor"),
            P(None, "tensor"),
            P("tensor", None),
            P(),
            P(None, "tensor"),
            P(None, "tensor"),
            P("tensor", None),
        ),
        check_vma=False,
    )
```

```python
import jax
import jax.numpy as jnp
from jax import lax
from jax.experimental import pallas as pl
from jax.experimental.pallas import tpu as pltpu
from jax.sharding import PartitionSpec as P

EPS = 1e-05
F32 = jnp.float32
BF = jnp.bfloat16
MESH = pl.DeviceIdType.MESH
TILE_ROWS, TILE_COLS = 1024, 256
BLOCK = 256
SLOTS, TILE_SLOTS, PART_SLOTS, WHOLE_SLOTS = 14, 9, (12, 10, 8, 4), 13
LAGS = (1, 3, 5, 6, 7, 9, 11, 12, 13)
FRONT = 512
PIECES = 8
VMEM_BYTES = 61 << 20


def distances(lengths, count):
    ends = jnp.cumsum(lengths)
    starts = ends - lengths
    places = jnp.arange(count, dtype=jnp.int32)
    begin = jnp.max(jnp.where(starts[None, :] <= places[:, None], starts[None, :], 0), axis=1)
    return places - begin


def rms_scale(value):
    return lax.rsqrt(jnp.mean(value * value, axis=-1, keepdims=True) + EPS)


def shift_down(value, steps, keep):
    moved = jnp.concatenate([jnp.zeros_like(value[:steps]), value[:-steps]], 0)
    return moved * keep


def shift_up(value, steps):
    return jnp.concatenate([value[steps:], jnp.zeros_like(value[:steps])], 0)


def norm_back(grad_in, normed, scale, gain):
    weighted = grad_in * gain
    inner = jnp.mean(weighted * normed, axis=-1, keepdims=True)
    return (scale * (weighted - normed * inner), jnp.sum(grad_in * normed, axis=0))


def dot(a, b, ca, cb):
    return lax.dot_general(a, b, (((ca,), (cb,)), ((), ())), preferred_element_type=F32)


def block_keeps(lengths_ref, first, count):
    place = first + lax.broadcasted_iota(jnp.int32, (count, 1), 0)
    one = place != 0
    two = (place != 0) & (place != 1)
    start = 0
    for j in range(lengths_ref.shape[1] - 1):
        start = start + lengths_ref[0, j]
        one = one & (place != start)
        two = two & (place != start) & (place != start + 1)
    return one, two


def mixer_kernel(
    lengths_ref,
    x_ref,
    in_ref,
    out_ref,
    taps_ref,
    gain1_ref,
    gain2_ref,
    h1_ref,
    keep_ref,
    z_ref,
    resid_ref,
    h2_ref,
    in_full_ref,
    out_full_ref,
    taps_full_ref,
    x_v,
    h1_v,
    z_v,
    in_v,
    out_v,
    taps_v,
    keep_v,
    resid_v,
    h2_v,
    last_v,
    load_sem,
    keep_sem,
    store_sem,
    side_sem,
    x_send,
    x_recv,
    y_send,
    y_recv,
    core_send,
    core_recv,
):
    me, side = lax.axis_index("dp"), lax.axis_index("tensor")
    other = 1 - side
    rows, width = x_v.shape
    half = width // 2
    blocks = rows // FRONT
    core_peer = me + 1 - 2 * (me % 2)
    y_peer = me + 2 - 4 * ((me // 2) % 2)
    quarter = me % 4

    def piece(j, which, owner):
        if j < 6:
            size = width // 8
            at = pl.multiple_of(which * 2 * size + (j % 2) * size, size)
            return in_v.at[owner, pl.ds(at, size), pl.ds((j // 2) * half, half)]
        size = half // 8
        at = pl.multiple_of(which * 2 * size + (j % 2) * size, size)
        return out_v.at[owner, pl.ds(at, size)]

    def source(j):
        if j < 6:
            size = width // 8
            at = pl.multiple_of(quarter * 2 * size + (j % 2) * size, size)
            return in_ref.at[j // 2, pl.ds(at, size)]
        size = half // 8
        at = pl.multiple_of(quarter * 2 * size + (j % 2) * size, size)
        return out_ref.at[pl.ds(at, size)]

    def remote(src, dst, send, recv, device):
        return pltpu.make_async_remote_copy(
            src_ref=src, dst_ref=dst, send_sem=send, recv_sem=recv, device_id=device, device_id_type=MESH
        )

    def cross(j):
        return remote(source(j), piece(j, quarter, side), x_send.at[j], x_recv.at[j], (me, other))

    def along_y(j):
        ref = piece(j, quarter, other)
        return remote(ref, ref, y_send.at[j], y_recv.at[j], (y_peer, side))

    def to_core(j, which, slot):
        ref = piece(j, which, other)
        return remote(ref, ref, core_send.at[slot, j], core_recv.at[slot, j], (core_peer, side))

    y_quarter = quarter + 2 - 4 * (quarter // 2)
    first_core = lambda j: to_core(j, quarter, 0)
    second_core = lambda j: to_core(j, y_quarter, 1)
    taps_copy = remote(taps_v.at[side], taps_v.at[side], side_sem.at[0], side_sem.at[1], (me, other))

    def forward(j):
        cross(j).wait_recv()
        along_y(j).start()
        first_core(j).start()

    def forward_y(j):
        along_y(j).wait_recv()
        second_core(j).start()

    def arrived(j):
        first_core(j).wait_recv()
        second_core(j).wait_recv()

    load_x = pltpu.make_async_copy(x_ref, x_v, load_sem.at[0])
    load_taps = pltpu.make_async_copy(taps_ref, taps_v.at[side], load_sem.at[1])
    load_out = pltpu.make_async_copy(out_ref, out_v.at[side], load_sem.at[2])
    load_in = [
        pltpu.make_async_copy(in_ref.at[k], in_v.at[side, :, pl.ds(k * half, half)], load_sem.at[3 + k])
        for k in range(3)
    ]
    load_taps.start()
    load_x.start()
    for copy in load_in:
        copy.start()
    load_out.start()
    barrier = pltpu.get_barrier_semaphore()
    for device in ((me, other), (y_peer, side), (core_peer, side)):
        pl.semaphore_signal(barrier, inc=1, device_id=device, device_id_type=MESH)
    pl.semaphore_wait(barrier, 3)
    for j in range(PIECES):
        cross(j).start()
    load_taps.wait()
    taps_copy.start()
    last_v[...] = jnp.zeros_like(last_v)
    load_x.wait()
    for copy in load_in:
        copy.wait()

    def block_rows(i):
        return pl.ds(pl.multiple_of(i * FRONT, FRONT), FRONT)

    def keep_out(i, owner, slot):
        column = pl.multiple_of(owner * 4 * half, 4 * half)
        return pltpu.make_async_copy(
            keep_v.at[slot], keep_ref.at[block_rows(i), pl.ds(column, 4 * half)], keep_sem.at[slot]
        )

    def half_block(i, owner, slot):
        at = block_rows(i)
        parts = dot(h1_v[at, :], in_v[owner], 1, 0)
        b_part, c_part, x_part = (parts[:, :half], parts[:, half : 2 * half], parts[:, 2 * half :])
        m = b_part * x_part
        one, two = block_keeps(lengths_ref, i * FRONT, FRONT)
        row = lax.broadcasted_iota(jnp.int32, (FRONT, 1), 0)
        before = last_v[owner]
        m_one = jnp.where(row == 0, before[7:8], pltpu.roll(m, 1, 0))
        m_two = jnp.where(row == 0, before[6:7], jnp.where(row == 1, before[7:8], pltpu.roll(m, 2, 0)))
        last_v[owner] = m[FRONT - 8 :]
        taps = taps_v[owner]
        v = taps[0:1] * m + taps[1:2] * jnp.where(one, m_one, 0.0)
        v = v + taps[2:3] * jnp.where(two, m_two, 0.0)
        keep_v[slot, :, :half] = b_part.astype(BF)
        keep_v[slot, :, half : 2 * half] = c_part.astype(BF)
        keep_v[slot, :, 2 * half : 3 * half] = x_part.astype(BF)
        keep_v[slot, :, 3 * half :] = v.astype(BF)
        z_v[owner, at, :] = (c_part * v).astype(BF)

    for i in range(blocks):
        at = block_rows(i)
        x = x_v[at, :].astype(F32)
        h1_v[at, :] = (x * rms_scale(x) * gain1_ref[...].astype(F32)).astype(BF)
        if i >= 2:
            keep_out(i - 2, side, i % 2).wait()
        half_block(i, side, i % 2)
        keep_out(i, side, i % 2).start()
        forward(i)
    store_h1 = pltpu.make_async_copy(h1_v, h1_ref, store_sem.at[0])
    store_h1.start()
    for j in range(blocks, PIECES):
        forward_y(j - blocks)
        forward(j)
    for j in range(PIECES - blocks, PIECES - 2):
        forward_y(j)
    for j in range(PIECES - 2):
        arrived(j)
    taps_copy.wait()
    for copy in (keep_out(i, side, i % 2) for i in (blocks - 2, blocks - 1)):
        copy.wait()

    for i in range(blocks):
        if i >= 2:
            keep_out(i - 2, other, i % 2).wait()
        half_block(i, other, i % 2)
        keep_out(i, other, i % 2).start()
        if i == 1:
            forward_y(PIECES - 2)
        if i == 2:
            forward_y(PIECES - 1)
    store_z = pltpu.make_async_copy(z_v, z_ref, store_sem.at[1])
    store_z.start()
    load_out.wait()
    for j in (PIECES - 2, PIECES - 1):
        arrived(j)
    stores = [
        pltpu.make_async_copy(
            in_v.at[h], in_full_ref.at[:, pl.ds(h * 3 * half, 3 * half)], store_sem.at[2 + h]
        )
        for h in range(2)
    ]
    stores += [
        pltpu.make_async_copy(out_v.at[h], out_full_ref.at[pl.ds(h * half, half)], store_sem.at[4 + h])
        for h in range(2)
    ]
    stores += [
        pltpu.make_async_copy(
            taps_v.at[h], taps_full_ref.at[:, pl.ds(h * half, half)], store_sem.at[6 + h]
        )
        for h in range(2)
    ]
    for copy in stores:
        copy.start()
    for copy in (keep_out(i, other, i % 2) for i in (blocks - 2, blocks - 1)):
        copy.wait()

    def row_out(i):
        slot = i % 2
        return (
            pltpu.make_async_copy(resid_v.at[slot], resid_ref.at[block_rows(i)], keep_sem.at[slot]),
            pltpu.make_async_copy(h2_v.at[slot], h2_ref.at[block_rows(i)], side_sem.at[2 + slot]),
        )

    for i in range(blocks):
        at = block_rows(i)
        if i >= 2:
            for copy in row_out(i - 2):
                copy.wait()
        z = jnp.concatenate([z_v[0, at, :], z_v[1, at, :]], 1)
        total = dot(z, out_v[...].reshape(width, width), 1, 0)
        resid = x_v[at, :].astype(F32) + total
        resid_v[i % 2] = resid
        h2_v[i % 2] = (resid * rms_scale(resid) * gain2_ref[...].astype(F32)).astype(BF)
        for copy in row_out(i):
            copy.start()
    for i in (blocks - 2, blocks - 1):
        for copy in row_out(i):
            copy.wait()
    for j in range(PIECES):
        cross(j).wait_send()
        along_y(j).wait_send()
        first_core(j).wait_send()
        second_core(j).wait_send()
    for copy in [store_h1, store_z, *stores]:
        copy.wait()


def mixer_forward(lengths, x, in_w, out_w, taps, gain1, gain2):
    rows, width = x.shape
    half = out_w.shape[0]
    any_spec = pl.BlockSpec(memory_space=pl.ANY)
    vmem_spec = pl.BlockSpec(memory_space=pltpu.VMEM)
    dma = pltpu.SemaphoreType.DMA
    shape = jax.ShapeDtypeStruct
    low = shape((rows, width), BF)
    return pl.pallas_call(
        mixer_kernel,
        out_shape=(
            low,
            shape((rows, 4 * width), BF),
            shape((2, rows, half), BF),
            shape((rows, width), F32),
            low,
            shape((width, 3 * width), BF),
            shape((width, width), BF),
            shape((8, width), F32),
        ),
        in_specs=[pl.BlockSpec(memory_space=pltpu.SMEM)] + [any_spec] * 4 + [vmem_spec] * 2,
        out_specs=(any_spec,) * 8,
        scratch_shapes=[
            pltpu.VMEM((rows, width), BF),
            pltpu.VMEM((rows, width), BF),
            pltpu.VMEM((2, rows, half), BF),
            pltpu.VMEM((2, width, 3 * half), BF),
            pltpu.VMEM((2, half, width), BF),
            pltpu.VMEM((2, 8, half), F32),
            pltpu.VMEM((2, FRONT, 4 * half), BF),
            pltpu.VMEM((2, FRONT, width), F32),
            pltpu.VMEM((2, FRONT, width), BF),
            pltpu.VMEM((2, 8, half), F32),
            dma((6,)),
            dma((2,)),
            dma((8,)),
            dma((4,)),
            *[dma((PIECES,))] * 4,
            dma((2, PIECES)),
            dma((2, PIECES)),
        ],
        compiler_params=pltpu.CompilerParams(
            collective_id=2, has_side_effects=True, vmem_limit_bytes=VMEM_BYTES
        ),
    )(lengths, x, in_w, out_w, taps, gain1.reshape(1, width), gain2.reshape(1, width))


def swiglu_kernel(h2_ref, gate_ref, up_ref, hid_ref, slope_ref, silu_ref):
    h2 = h2_ref[...]
    gate = dot(h2, gate_ref[...], 1, 0)
    up = dot(h2, up_ref[...], 1, 0)
    sig = jax.nn.sigmoid(gate)
    silu = gate * sig
    hid_ref[...] = (silu * up).astype(BF)
    slope_ref[...] = (up * sig * (1.0 + gate * (1.0 - sig))).astype(BF)
    silu_ref[...] = silu.astype(BF)


def swiglu(h2, gate_w, up_w):
    rows, width = h2.shape
    hidden = gate_w.shape[1]
    out = jax.ShapeDtypeStruct((rows, hidden), BF)
    row_spec = pl.BlockSpec((BLOCK, hidden), lambda i: (i, 0))
    whole = pl.BlockSpec((width, hidden), lambda i: (0, 0), pipeline_mode=pl.Buffered(1))
    return pl.pallas_call(
        swiglu_kernel,
        grid=(rows // BLOCK,),
        out_shape=(out, out, out),
        in_specs=[pl.BlockSpec((BLOCK, width), lambda i: (i, 0)), whole, whole],
        out_specs=(row_spec, row_spec, row_spec),
        compiler_params=pltpu.CompilerParams(vmem_limit_bytes=VMEM_BYTES),
    )(h2, gate_w, up_w)


class Reducer:
    def __init__(self, count, tiles, parts, whole, send, recv, kinds, out_sem):
        self.count, self.slots = count, send.shape[0]
        self.tiles, self.parts, self.whole = tiles, parts, whole
        self.send, self.recv = send, recv
        self.kinds, self.out_sem = kinds, out_sem
        self.me = lax.axis_index("dp")
        self.side = lax.axis_index("tensor")

    def plan(self, n):
        me = self.me
        bit = [me % 2, (me // 2) % 2, (me // 4) % 2, (me // 8) % 2]
        swap = (n % 2 == 1) & (me % 2 == 1)
        mine = [bit[0], jnp.where(swap, bit[2], bit[1]), jnp.where(swap, bit[1], bit[2]), bit[3]]
        step = [1, jnp.where(swap, 4, 2), jnp.where(swap, 2, 4), 8]
        peer = [me + s * (1 - 2 * b) for s, b in zip(step, mine)]
        keep, off = [], 0
        give = []
        for s in range(4):
            size = TILE_ROWS >> (s + 1)
            give.append(pl.multiple_of(off + (1 - mine[s]) * size, size))
            off = off + mine[s] * size
            keep.append(pl.multiple_of(off, size))
        return peer, keep, give

    def scatter(self, n, s):
        peer, keep, give = self.plan(n)
        size = TILE_ROWS >> (s + 1)
        part = self.parts[s]
        return pltpu.make_async_remote_copy(
            src_ref=self.tiles.at[n % TILE_SLOTS, pl.ds(give[s], size)],
            dst_ref=part.at[n % part.shape[0]],
            send_sem=self.send.at[n % self.slots, s],
            recv_sem=self.recv.at[n % self.slots, s],
            device_id=(peer[s], self.side),
            device_id_type=MESH,
        )

    def gather(self, n, s):
        peer, keep, give = self.plan(n)
        size = TILE_ROWS >> (s + 1)
        block = self.whole.at[n % WHOLE_SLOTS, pl.ds(keep[s], size)]
        return pltpu.make_async_remote_copy(
            src_ref=block,
            dst_ref=block,
            send_sem=self.send.at[n % self.slots, 4 + s],
            recv_sem=self.recv.at[n % self.slots, 4 + s],
            device_id=(peer[s], self.side),
            device_id_type=MESH,
        )

    def write(self, n, act):
        quarter = TILE_ROWS // 4
        for first, last, place in self.kinds:

            @pl.when((n >= first) & (n < last))
            def _():
                for q in range(4):
                    copy = pltpu.make_async_copy(
                        self.whole.at[n % WHOLE_SLOTS, pl.ds(q * quarter, quarter)],
                        place(n - first, q),
                        self.out_sem.at[n % self.slots, q],
                    )
                    act(copy)

    def add(self, n, s):
        peer, keep, give = self.plan(n)
        size = TILE_ROWS >> (s + 1)
        rows = pl.ds(keep[s], size)
        part = self.parts[s]
        total = self.tiles[n % TILE_SLOTS, rows, :].astype(F32) + part[n % part.shape[0]].astype(F32)
        if s == 3:
            self.whole[n % WHOLE_SLOTS, rows, :] = total.astype(BF)
        else:
            self.tiles[n % TILE_SLOTS, rows, :] = total.astype(BF)

    def put(self, n, value):
        self.tiles[n % TILE_SLOTS] = value.astype(BF)
        self.scatter(n, 0).start()

    def put_blocks(self, n, value):
        size = TILE_ROWS // 4
        for q in range(4):
            block = value[:, q * TILE_COLS : (q + 1) * TILE_COLS]
            self.tiles[n % TILE_SLOTS, q * size : (q + 1) * size, :] = block.astype(BF)
        self.scatter(n, 0).start()

    def tick(self, n):
        def stage(k, lag):
            m = n - lag

            @pl.when((m >= 0) & (m < self.count))
            def _():
                if k <= 4:
                    self.scatter(m, k - 1).wait()
                    self.add(m, k - 1)
                    if k < 4:
                        self.scatter(m, k).start()
                    else:
                        self.gather(m, 3).start()
                elif k <= 8:
                    self.gather(m, 8 - k).wait()
                    if k < 8:
                        self.gather(m, 7 - k).start()
                    else:
                        self.write(m, lambda copy: copy.start())
                else:
                    self.write(m, lambda copy: copy.wait())

        for k in (1, 6, 2, 3, 4, 5, 7, 8, 9):
            stage(k, LAGS[k - 1])


def back_kernel(
    lengths_ref,
    hid_ref,
    slope_ref,
    silu_ref,
    h2_ref,
    dy_ref,
    gate_ref,
    up_ref,
    down_ref,
    resid_ref,
    x_ref,
    keep_ref,
    z_ref,
    h1_ref,
    in_ref,
    out_ref,
    gain1_ref,
    gain2_ref,
    taps_ref,
    down_sum_ref,
    gate_sum_ref,
    up_sum_ref,
    out_sum_ref,
    in_sum_ref,
    dgu_ref,
    dh2_own_ref,
    dh2_got_ref,
    ffn_own_ref,
    ffn_got_ref,
    dp_ref,
    grad_ref,
    result_ref,
    small_ref,
    dy_v,
    h2_v,
    wide_v,
    down_v,
    tile_v,
    row_v,
    small_v,
    small_in,
    next_v,
    tiles,
    whole,
    part0,
    part1,
    part2,
    part3,
    load_sem,
    tile_sem,
    stream_sem,
    dgu_sem,
    own_sem,
    hid_sem,
    dp_sem,
    grad_sem,
    small_send,
    small_recv,
    x_send,
    x_recv,
    send,
    recv,
    out_sem,
):
    me, side = lax.axis_index("dp"), lax.axis_index("tensor")
    rows, width = dy_v.shape
    hidden = hid_ref.shape[1]
    half = width // 2
    blocks = rows // BLOCK
    n_down = hidden // TILE_COLS
    n_out = half // TILE_COLS
    first_gate, first_out = n_down, 3 * n_down
    first_in = first_out + n_out
    count = first_in + 3 * n_out

    def rows_of(ref):
        return lambda t, q: ref.at[
            pl.ds(pl.multiple_of(t * TILE_COLS, TILE_COLS), TILE_COLS), pl.ds(q * TILE_COLS, TILE_COLS)
        ]

    def columns_of(ref):
        return lambda t, q: ref.at[
            pl.ds(q * TILE_COLS, TILE_COLS), pl.ds(pl.multiple_of(t * TILE_COLS, TILE_COLS), TILE_COLS)
        ]

    def in_place(t, q):
        column = pl.multiple_of((t % n_out) * TILE_COLS, TILE_COLS)
        return in_sum_ref.at[t // n_out, pl.ds(q * TILE_COLS, TILE_COLS), pl.ds(column, TILE_COLS)]

    first_up = 2 * n_down
    kinds = (
        (0, first_gate, rows_of(down_sum_ref)),
        (first_gate, first_up, columns_of(gate_sum_ref)),
        (first_up, first_out, columns_of(up_sum_ref)),
        (first_out, first_in, rows_of(out_sum_ref)),
        (first_in, count, in_place),
    )
    red = Reducer(count, tiles, (part0, part1, part2, part3), whole, send, recv, kinds, out_sem)

    def peer(bit):
        return me + bit * (1 - 2 * ((me // bit) % 2))

    def block_rows(i):
        return pl.ds(pl.multiple_of((blocks - 1 - i) * BLOCK, BLOCK), BLOCK)

    load_dy = pltpu.make_async_copy(dy_ref, dy_v, load_sem.at[0])
    load_down = pltpu.make_async_copy(down_ref, down_v, load_sem.at[1])
    load_gate = pltpu.make_async_copy(gate_ref, wide_v.at[:, pl.ds(0, hidden)], load_sem.at[2])
    load_up = pltpu.make_async_copy(up_ref, wide_v.at[:, pl.ds(hidden, hidden)], load_sem.at[3])
    load_h2 = pltpu.make_async_copy(h2_ref, h2_v, load_sem.at[4])
    load_in = pltpu.make_async_copy(in_ref, wide_v.at[:, pl.ds(0, 3 * width)], load_sem.at[2])
    load_out = pltpu.make_async_copy(out_ref, wide_v.at[:, pl.ds(3 * width, width)], load_sem.at[3])
    load_h1 = pltpu.make_async_copy(h1_ref, h2_v, load_sem.at[4])

    def tile_of(ref, column, n):
        column = pl.multiple_of(column, TILE_COLS)
        return pltpu.make_async_copy(
            ref.at[:, pl.ds(column, TILE_COLS)], tile_v.at[n % 2], tile_sem.at[n % 2]
        )

    def hid_tile(n):
        return tile_of(hid_ref, n * TILE_COLS, n)

    def dgu_tile(n):
        return tile_of(dgu_ref, (n - first_gate) * TILE_COLS, n)

    def z_tile(n):
        return tile_of(z_ref.at[side], (n - first_out) * TILE_COLS, n)

    def dp_tile(n):
        return tile_of(dp_ref, (n - first_in) * TILE_COLS, n)

    def row_own(i, ref):
        return pltpu.make_async_copy(row_v.at[i % 2], ref.at[block_rows(i % blocks)], own_sem.at[i % 2])

    def row_send(i, own, got):
        at = block_rows(i % blocks)
        return pltpu.make_async_remote_copy(
            src_ref=own.at[at],
            dst_ref=got.at[at],
            send_sem=x_send.at[i],
            recv_sem=x_recv.at[i],
            device_id=(me, 1 - side),
            device_id_type=MESH,
        )

    def dh2_send(i):
        return row_send(i, dh2_own_ref, dh2_got_ref)

    def ffn_send(i):
        return row_send(blocks + i, ffn_own_ref, ffn_got_ref)

    def small_copy(s):
        return pltpu.make_async_remote_copy(
            src_ref=small_v,
            dst_ref=small_in.at[s],
            send_sem=small_send.at[s],
            recv_sem=small_recv.at[s],
            device_id=(peer(1 << s), side),
            device_id_type=MESH,
        )

    def small_add(s):
        small_copy(s).wait()
        small_v[...] = small_v[...] + small_in[s]

    load_dy.start()
    hid_tile(0).start()
    load_down.start()
    load_gate.start()
    load_up.start()
    load_h2.start()

    barrier = pltpu.get_barrier_semaphore()
    for bit in (1, 2, 4, 8):
        pl.semaphore_signal(barrier, inc=1, device_id=(peer(bit), side), device_id_type=MESH)
    pl.semaphore_signal(barrier, inc=1, device_id=(me, 1 - side), device_id_type=MESH)
    pl.semaphore_wait(barrier, 5)

    small_v[...] = jnp.zeros_like(small_v)
    next_v[...] = jnp.zeros_like(next_v)

    def down_step(n, carry):
        @pl.when(n + 1 < n_down)
        def _():
            hid_tile(n + 1).start()

        hid_tile(n).wait()
        red.put_blocks(n, dot(tile_v[n % 2], dy_v[...], 0, 0))
        return carry

    def grads(slope_v, silu_v, dgu_v):
        def pair(i):
            at = block_rows(i)
            return (
                pltpu.make_async_copy(slope_ref.at[at], slope_v.at[i % 2], stream_sem.at[i % 2, 0]),
                pltpu.make_async_copy(silu_ref.at[at], silu_v.at[i % 2], stream_sem.at[i % 2, 1]),
            )

        def dgu_out(i):
            return pltpu.make_async_copy(
                dgu_v.at[i % 2], dgu_ref.at[block_rows(i)], dgu_sem.at[i % 2]
            )

        for copy in pair(0):
            copy.start()
        load_dy.wait()
        def down_group(g, carry):
            lax.fori_loop(3 * g, 3 * g + 3, down_step, 0)
            red.tick(1 + g)
            return carry

        lax.fori_loop(0, n_down // 3, down_group, 0)
        load_down.wait()
        load_gate.wait()
        load_up.wait()

        def grad_step(i, carry):
            slot = i % 2

            @pl.when(i + 1 < blocks)
            def _():
                for copy in pair(i + 1):
                    copy.start()

            for copy in pair(i):
                copy.wait()

            @pl.when(i >= 2)
            def _():
                dgu_out(i - 2).wait()

            d_hid = dot(dy_v[block_rows(i), :], down_v[...], 1, 1)
            dgu_v[slot, :, :hidden] = (d_hid * slope_v[slot].astype(F32)).astype(BF)
            dgu_v[slot, :, hidden:] = (d_hid * silu_v[slot].astype(F32)).astype(BF)
            dgu_out(i).start()
            row_v[slot] = dot(dgu_v[slot], wide_v[...], 1, 1).astype(BF)
            row_own(i, dh2_own_ref).start()

            @pl.when(i % 3 != 2)
            def _():
                red.tick(4 + i - (i + 1) // 3)

            row_own(i, dh2_own_ref).wait()
            dh2_send(i).start()
            return carry

        lax.fori_loop(0, blocks, grad_step, 0)
        load_in.start()
        load_out.start()
        for i in (blocks - 2, blocks - 1):
            dgu_out(i).wait()
        dgu_tile(first_gate).start()

    pl.run_scoped(
        grads,
        pltpu.VMEM((2, BLOCK, hidden), BF),
        pltpu.VMEM((2, BLOCK, hidden), BF),
        pltpu.VMEM((2, BLOCK, 2 * hidden), BF),
    )

    def gate_put(n):
        dgu_tile(n).wait()
        red.put(n, dot(h2_v[...], tile_v[n % 2], 0, 0))

    def mixer(keep_v, resid_v, x_v, pair_v, hid_v, dp_v, grad_v, dr1_v):
        def hid_rows(i):
            return pltpu.make_async_copy(hid_ref.at[block_rows(i)], hid_v.at[i % 2], hid_sem.at[i % 2])

        def inputs(i):
            at, slot = block_rows(i), i % 2
            return (
                pltpu.make_async_copy(keep_ref.at[at], keep_v.at[slot], stream_sem.at[slot, 0]),
                pltpu.make_async_copy(resid_ref.at[at], resid_v.at[slot], stream_sem.at[slot, 1]),
                pltpu.make_async_copy(x_ref.at[at], x_v.at[slot], stream_sem.at[slot, 2]),
                pltpu.make_async_copy(dh2_own_ref.at[at], pair_v.at[0], stream_sem.at[slot, 3]),
            )

        def got(i):
            return pltpu.make_async_copy(dh2_got_ref.at[block_rows(i)], pair_v.at[1], dgu_sem.at[0])

        def dp_out(i):
            column = pl.multiple_of(side * 3 * half, 3 * half)
            return pltpu.make_async_copy(
                dp_v.at[:, pl.ds(column, 3 * half)], dp_ref.at[block_rows(i)], dp_sem
            )

        def put_dp(k, value):
            for h in range(2):
                first = (3 * h + k) * half
                dp_v[:, first : first + half] = value[:, h * half : (h + 1) * half].astype(BF)

        def kept(slot, k):
            return jnp.concatenate(
                [keep_v[slot, :, (4 * h + k) * half : (4 * h + k + 1) * half] for h in range(2)], 1
            ).astype(F32)

        def grad_out(i):
            return pltpu.make_async_copy(grad_v, grad_ref.at[block_rows(i)], grad_sem)

        def finish(i):
            dp_out(i).wait()
            grad_out(i).wait()

        def mixer_first(i):
            slot = i % 2
            at = block_rows(i)
            for copy in inputs(i):
                copy.wait()
            got(i).wait()

            @pl.when(i > 0)
            def _():
                finish(i - 1)

            resid = resid_v[slot]
            scale2 = rms_scale(resid)
            n2 = resid * scale2
            dh2 = pair_v[0].astype(F32) + pair_v[1].astype(F32)
            d_resid, gain2_part = norm_back(dh2, n2, scale2, gain2_ref[...].astype(F32))
            dr1 = dy_v[at, :].astype(F32) + d_resid
            dr1b = dr1.astype(BF)
            dr1_v[...] = dr1
            dy_v[at, :] = dr1b
            dz = dot(dr1b, wide_v[:, 3 * width : 4 * width], 1, 1)
            put_dp(1, dz * kept(slot, 3))
            dv = dz * kept(slot, 1)
            b_part = kept(slot, 0)
            x_part = kept(slot, 2)
            m = b_part * x_part
            one, two = block_keeps(lengths_ref, (blocks - 1 - i) * BLOCK, BLOCK)
            row = lax.broadcasted_iota(jnp.int32, (BLOCK, 1), 0)
            dv_one = jnp.where(one, dv, 0.0)
            dv_two = jnp.where(two, dv, 0.0)
            up_one = jnp.where(row == BLOCK - 1, next_v[0:1, :], pltpu.roll(dv_one, BLOCK - 1, 0))
            up_two = jnp.where(
                row == BLOCK - 2,
                next_v[8:9, :],
                jnp.where(row == BLOCK - 1, next_v[9:10, :], pltpu.roll(dv_two, BLOCK - 2, 0)),
            )
            next_v[0:8, :] = dv_one[0:8]
            next_v[8:16, :] = dv_two[0:8]
            taps = taps_ref[...]
            dm = taps[0:1] * dv + taps[1:2] * up_one + taps[2:3] * up_two
            put_dp(0, dm * x_part)
            put_dp(2, dm * b_part)
            dp_out(i).start()
            small_v[1:2, :] += gain2_part.reshape(1, width)
            small_v[2:3, :] += jnp.sum(dv * m, axis=0, keepdims=True)
            small_v[3:4, :] += jnp.sum(up_one * m, axis=0, keepdims=True)
            small_v[4:5, :] += jnp.sum(up_two * m, axis=0, keepdims=True)

        def mixer_second(i):
            dh1 = dot(dp_v[...], wide_v[:, : 3 * width], 1, 1)
            x = x_v[i % 2].astype(F32)
            scale1 = rms_scale(x)
            d_input, gain1_part = norm_back(dh1, x * scale1, scale1, gain1_ref[...].astype(F32))
            grad_v[...] = (dr1_v[...] + d_input).astype(BF)
            grad_out(i).start()
            small_v[0:1, :] += gain1_part.reshape(1, width)

        hid_rows(0).start()
        for copy in inputs(0):
            copy.start()
        load_h2.wait()
        load_in.wait()
        load_out.wait()

        def mixer_step(i, carry):
            n = first_gate + 2 * i
            dh2_send(i).wait_recv()
            got(i).start()
            dgu_tile(n + 1).start()
            gate_put(n)
            mixer_first(i)
            red.tick(n + 1)
            mixer_second(i)

            @pl.when(i + 1 < blocks)
            def _():
                hid_rows(i + 1).start()
                for copy in inputs(i + 1):
                    copy.start()

            hid_rows(i).wait()
            row_v[i % 2] = dot(hid_v[i % 2], down_v[...], 1, 0).astype(BF)
            row_own(i, ffn_own_ref).start()
            dgu_tile(n + 2).start()
            gate_put(n + 1)
            row_own(i, ffn_own_ref).wait()
            ffn_send(i).start()
            red.tick(n + 2)
            return carry

        lax.fori_loop(0, blocks, mixer_step, 0)
        finish(blocks - 1)

    pl.run_scoped(
        mixer,
        pltpu.VMEM((2, BLOCK, 4 * width), BF),
        pltpu.VMEM((2, BLOCK, width), F32),
        pltpu.VMEM((2, BLOCK, width), BF),
        pltpu.VMEM((2, BLOCK, width), BF),
        pltpu.VMEM((2, BLOCK, hidden), BF),
        pltpu.VMEM((BLOCK, 3 * width), BF),
        pltpu.VMEM((BLOCK, width), BF),
        pltpu.VMEM((BLOCK, width), F32),
    )

    small_copy(0).start()

    def tail(resid_v, pair_v, result_v):
        def inputs(i):
            at = block_rows(i)
            return (
                pltpu.make_async_copy(resid_ref.at[at], resid_v, stream_sem.at[0, 0]),
                pltpu.make_async_copy(ffn_own_ref.at[at], pair_v.at[0], stream_sem.at[0, 1]),
                pltpu.make_async_copy(ffn_got_ref.at[at], pair_v.at[1], stream_sem.at[0, 2]),
            )

        def result_out(i):
            return pltpu.make_async_copy(result_v, result_ref.at[block_rows(i)], grad_sem)

        def post(p):
            i = p // 2

            @pl.when((p % 2 == 0) & (i < blocks))
            def _():
                ffn_send(i).wait_recv()
                for copy in inputs(i):
                    copy.start()

            @pl.when((p % 2 == 1) & (i < blocks))
            def _():
                for copy in inputs(i):
                    copy.wait()

                @pl.when(i > 0)
                def _():
                    result_out(i - 1).wait()

                both = pair_v[0].astype(F32) + pair_v[1].astype(F32)
                result_v[...] = (resid_v[...] + both).astype(BF)
                result_out(i).start()

        base = first_gate + 2 * blocks

        def step(n, put):
            put(n)
            red.tick(n + 1)
            post(n - base)

        for n in range(base, first_out):
            (dgu_tile if n + 1 < first_out else z_tile)(n + 1).start()
            step(n, gate_put)
        load_h1.start()
        small_add(0)
        small_copy(1).start()

        def out_put(n):
            z_tile(n).wait()
            red.put_blocks(n, dot(tile_v[n % 2], dy_v[...], 0, 0))

        for n in range(first_out, first_in):
            (z_tile if n + 1 < first_in else dp_tile)(n + 1).start()
            step(n, out_put)
        small_add(1)
        small_copy(2).start()
        load_h1.wait()

        def in_step(n, carry):
            @pl.when(n + 1 < count)
            def _():
                dp_tile(n + 1).start()

            def in_put(n):
                dp_tile(n).wait()
                red.put(n, dot(h2_v[...], tile_v[n % 2], 0, 0))

            step(n, in_put)
            return carry

        middle = (first_in + count) // 2
        lax.fori_loop(first_in, middle, in_step, 0)
        small_add(2)
        small_copy(3).start()
        lax.fori_loop(middle, count, in_step, 0)
        small_add(3)
        small_out = pltpu.make_async_copy(small_v, small_ref, load_sem.at[0])
        small_out.start()

        def drain_step(n, carry):
            red.tick(n + 1)
            post(n - base)
            return carry

        lax.fori_loop(count, count + LAGS[-1] - 1, drain_step, 0)
        result_out(blocks - 1).wait()
        small_out.wait()
        for i in range(blocks):
            dh2_send(i).wait_send()
            ffn_send(i).wait_send()

    pl.run_scoped(
        tail,
        pltpu.VMEM((BLOCK, width), F32),
        pltpu.VMEM((2, BLOCK, width), BF),
        pltpu.VMEM((BLOCK, width), BF),
    )


def block_backward(
    lengths, hid, slope, silu, h2, dy, gate_w, up_w, down_w, resid, x, keep, z, h1, in_full, out_full,
    gain1, gain2, taps,
):
    rows, hidden = hid.shape
    width = h2.shape[1]
    blocks = rows // BLOCK
    any_spec = pl.BlockSpec(memory_space=pl.ANY)
    vmem_spec = pl.BlockSpec(memory_space=pltpu.VMEM)
    dma = pltpu.SemaphoreType.DMA
    shape = jax.ShapeDtypeStruct
    low = shape((rows, width), BF)
    ring = [pltpu.VMEM((slots, TILE_ROWS, TILE_COLS), BF) for slots in (TILE_SLOTS, WHOLE_SLOTS)]
    ring += [
        pltpu.VMEM((slots, TILE_ROWS >> (s + 1), TILE_COLS), BF) for s, slots in enumerate(PART_SLOTS)
    ]
    return pl.pallas_call(
        back_kernel,
        out_shape=(
            shape(down_w.shape, BF),
            shape(gate_w.shape, BF),
            shape(up_w.shape, BF),
            shape((width // 2, width), BF),
            shape((3, width, width // 2), BF),
            shape((rows, 2 * hidden), BF),
            low,
            low,
            low,
            low,
            shape((rows, 3 * width // 2), BF),
            low,
            low,
            shape((8, width), F32),
        ),
        in_specs=[pl.BlockSpec(memory_space=pltpu.SMEM)] + [any_spec] * 15 + [vmem_spec] * 3,
        out_specs=(any_spec,) * 14,
        scratch_shapes=[
            pltpu.VMEM((rows, width), BF),
            pltpu.VMEM((rows, width), BF),
            pltpu.VMEM((width, 2 * hidden), BF),
            pltpu.VMEM(down_w.shape, BF),
            pltpu.VMEM((2, rows, TILE_COLS), BF),
            pltpu.VMEM((2, BLOCK, width), BF),
            pltpu.VMEM((8, width), F32),
            pltpu.VMEM((4, 8, width), F32),
            pltpu.VMEM((16, width), F32),
            *ring,
            dma((5,)),
            dma((2,)),
            dma((2, 4)),
            dma((2,)),
            dma((2,)),
            dma((2,)),
            dma,
            dma,
            dma((4,)),
            dma((4,)),
            dma((2 * blocks,)),
            dma((2 * blocks,)),
            dma((SLOTS, 8)),
            dma((SLOTS, 8)),
            dma((SLOTS, 4)),
        ],
        compiler_params=pltpu.CompilerParams(
            collective_id=1, has_side_effects=True, vmem_limit_bytes=VMEM_BYTES
        ),
    )(
        lengths, hid, slope, silu, h2, dy, gate_w, up_w, down_w, resid, x, keep, z, h1, in_full, out_full,
        gain1.reshape(1, width), gain2.reshape(1, width), taps,
    )


def pair_body(
    tokens,
    cotangent,
    lengths,
    mixer_gain,
    in_weight,
    conv_weight,
    out_weight,
    ffn_gain,
    gate_weight,
    up_weight,
    down_weight,
):
    side = lax.axis_index("tensor")
    half = out_weight.shape[0]
    taps_own = jnp.pad(conv_weight.astype(F32), ((0, 5), (0, 0)))
    h1b, keep, zb, resid, h2b, in_full, out_full, taps = mixer_forward(
        lengths, tokens, in_weight.transpose(1, 0, 2), out_weight, taps_own, mixer_gain, ffn_gain
    )
    hidb, slope, silu = swiglu(h2b, gate_weight, up_weight)
    down_sum, gate_sum, up_sum, out_sum, in_sum, *_, input_grad, output, small = block_backward(
        lengths, hidb, slope, silu, h2b, cotangent, gate_weight, up_weight, down_weight, resid, tokens,
        keep, zb, h1b, in_full, out_full, mixer_gain, ffn_gain, taps,
    )
    return (
        output,
        input_grad,
        small[0],
        in_sum.astype(F32).transpose(1, 0, 2),
        lax.dynamic_slice_in_dim(small[2:5], side * half, half, 1),
        out_sum.astype(F32),
        small[1],
        gate_sum.astype(F32),
        up_sum.astype(F32),
        down_sum.astype(F32),
    )


def body(
    tokens,
    cotangent,
    lengths,
    mixer_gain,
    in_weight,
    conv_weight,
    out_weight,
    ffn_gain,
    gate_weight,
    up_weight,
    down_weight,
):
    rows = tokens.shape[0]
    dist = distances(lengths[0], rows)
    keep_one = (dist >= 1)[:, None].astype(jnp.float32)
    keep_two = (dist >= 2)[:, None].astype(jnp.float32)
    parts = lax.axis_size("tensor")
    share = rows // parts
    first = lax.axis_index("tensor") * share
    x = tokens.astype(jnp.float32)
    dy = cotangent.astype(jnp.float32)
    g1 = mixer_gain.astype(jnp.float32)
    g2 = ffn_gain.astype(jnp.float32)
    taps = conv_weight.astype(jnp.float32)
    scale1 = rms_scale(x)
    normed1 = x * scale1
    h1b = (normed1 * g1).astype(jnp.bfloat16)
    proj = jnp.einsum("td,dkc->tkc", h1b, in_weight, preferred_element_type=jnp.float32)
    b_part, c_part, x_part = (proj[:, 0], proj[:, 1], proj[:, 2])
    mixed = b_part * x_part
    mixed_one = shift_down(mixed, 1, keep_one)
    mixed_two = shift_down(mixed, 2, keep_two)
    conv_out = taps[0] * mixed + taps[1] * mixed_one + taps[2] * mixed_two
    zb = (c_part * conv_out).astype(jnp.bfloat16)
    mix_part = jnp.dot(zb, out_weight, preferred_element_type=jnp.float32)
    mix_rows = lax.psum_scatter(mix_part, "tensor", scatter_dimension=0, tiled=True)
    x_rows = lax.dynamic_slice_in_dim(x, first, share, 0)
    resid = x_rows + mix_rows
    scale2 = rms_scale(resid)
    normed2 = resid * scale2
    h2b = lax.all_gather((normed2 * g2).astype(jnp.bfloat16), "tensor", axis=0, tiled=True)
    gate = jnp.dot(h2b, gate_weight, preferred_element_type=jnp.float32)
    up = jnp.dot(h2b, up_weight, preferred_element_type=jnp.float32)
    sig = jax.nn.sigmoid(gate)
    silu = gate * sig
    hidb = (silu * up).astype(jnp.bfloat16)
    ffn_part = jnp.dot(hidb, down_weight, preferred_element_type=jnp.float32)
    down_grad = jnp.einsum("tf,td->fd", hidb, cotangent, preferred_element_type=jnp.float32)
    d_hid = jnp.einsum("td,fd->tf", cotangent, down_weight, preferred_element_type=jnp.float32)
    d_gate = (d_hid * up * sig * (1.0 + gate * (1.0 - sig))).astype(jnp.bfloat16)
    d_up = (d_hid * silu).astype(jnp.bfloat16)
    gate_grad = jnp.einsum("td,tf->df", h2b, d_gate, preferred_element_type=jnp.float32)
    up_grad = jnp.einsum("td,tf->df", h2b, d_up, preferred_element_type=jnp.float32)
    dh2_part = jnp.einsum("tf,df->td", d_gate, gate_weight, preferred_element_type=jnp.float32)
    dh2_part = dh2_part + jnp.einsum(
        "tf,df->td", d_up, up_weight, preferred_element_type=jnp.float32
    )
    ffn_rows = lax.psum_scatter(
        ffn_part.astype(jnp.bfloat16), "tensor", scatter_dimension=0, tiled=True
    ).astype(jnp.float32)
    output = lax.all_gather((resid + ffn_rows).astype(jnp.bfloat16), "tensor", axis=0, tiled=True)
    dh2_rows = lax.psum_scatter(dh2_part, "tensor", scatter_dimension=0, tiled=True)
    d_resid, g2_grad = norm_back(dh2_rows, normed2, scale2, g2)
    dr1 = lax.dynamic_slice_in_dim(dy, first, share, 0) + d_resid
    dr1b = lax.all_gather(dr1.astype(jnp.bfloat16), "tensor", axis=0, tiled=True)
    out_grad = jnp.einsum("tc,td->cd", zb, dr1b, preferred_element_type=jnp.float32)
    d_z = jnp.einsum("td,cd->tc", dr1b, out_weight, preferred_element_type=jnp.float32)
    d_c = d_z * conv_out
    d_conv = d_z * c_part
    conv_grad = jnp.stack(
        [
            jnp.sum(d_conv * mixed, axis=0),
            jnp.sum(d_conv * mixed_one, axis=0),
            jnp.sum(d_conv * mixed_two, axis=0),
        ],
        0,
    )
    d_mixed = (
        taps[0] * d_conv
        + taps[1] * shift_up(d_conv * keep_one, 1)
        + taps[2] * shift_up(d_conv * keep_two, 2)
    )
    d_proj = jnp.stack([d_mixed * x_part, d_c, d_mixed * b_part], 1).astype(jnp.bfloat16)
    in_grad_w = jnp.einsum("td,tkc->dkc", h1b, d_proj, preferred_element_type=jnp.float32)
    dh1_part = jnp.einsum("tkc,dkc->td", d_proj, in_weight, preferred_element_type=jnp.float32)
    dh1_rows = lax.psum_scatter(dh1_part, "tensor", scatter_dimension=0, tiled=True)
    normed1_rows = lax.dynamic_slice_in_dim(normed1, first, share, 0)
    scale1_rows = lax.dynamic_slice_in_dim(scale1, first, share, 0)
    d_input, g1_grad = norm_back(dh1_rows, normed1_rows, scale1_rows, g1)
    input_grad = lax.all_gather((dr1 + d_input).astype(jnp.bfloat16), "tensor", axis=0, tiled=True)
    g1_grad, g2_grad = lax.psum((g1_grad, g2_grad), "tensor")
    summed = lax.psum(
        (g1_grad, in_grad_w, conv_grad, out_grad, g2_grad, gate_grad, up_grad, down_grad), "dp"
    )
    return (
        output,
        input_grad,
        summed[0],
        summed[1],
        summed[2],
        summed[3],
        summed[4],
        summed[5],
        summed[6],
        summed[7],
    )


def solution(mesh):
    paired = mesh.shape["tensor"] == 2 and mesh.shape["dp"] == 16
    return jax.shard_map(
        pair_body if paired else body,
        mesh=mesh,
        in_specs=(
            P("dp", None),
            P("dp", None),
            P("dp", None),
            P(),
            P(None, None, "tensor"),
            P(None, "tensor"),
            P("tensor", None),
            P(),
            P(None, "tensor"),
            P(None, "tensor"),
            P("tensor", None),
        ),
        out_specs=(
            P("dp", None),
            P("dp", None),
            P(),
            P(None, None, "tensor"),
            P(None, "tensor"),
            P("tensor", None),
            P(),
            P(None, "tensor"),
            P(None, "tensor"),
            P("tensor", None),
        ),
        check_vma=False,
    )
```

```python
import jax
import jax.numpy as jnp
from jax import lax
from jax.experimental import pallas as pl
from jax.experimental.pallas import tpu as pltpu
from jax.sharding import PartitionSpec as P

EPS = 1e-05
F32 = jnp.float32
BF = jnp.bfloat16
MESH = pl.DeviceIdType.MESH
TILE_ROWS, TILE_COLS = 1024, 256
BLOCK = 256
SLOTS, TILE_SLOTS, PART_SLOTS, WHOLE_SLOTS = 14, 9, (12, 10, 8, 4), 13
LAGS = (1, 3, 5, 6, 7, 9, 11, 12, 13)
FRONT = 512
PIECES = 8
VMEM_BYTES = 61 << 20


def distances(lengths, count):
    ends = jnp.cumsum(lengths)
    starts = ends - lengths
    places = jnp.arange(count, dtype=jnp.int32)
    begin = jnp.max(jnp.where(starts[None, :] <= places[:, None], starts[None, :], 0), axis=1)
    return places - begin


def rms_scale(value):
    return lax.rsqrt(jnp.mean(value * value, axis=-1, keepdims=True) + EPS)


def shift_down(value, steps, keep):
    moved = jnp.concatenate([jnp.zeros_like(value[:steps]), value[:-steps]], 0)
    return moved * keep


def shift_up(value, steps):
    return jnp.concatenate([value[steps:], jnp.zeros_like(value[:steps])], 0)


def norm_back(grad_in, normed, scale, gain):
    weighted = grad_in * gain
    inner = jnp.mean(weighted * normed, axis=-1, keepdims=True)
    return (scale * (weighted - normed * inner), jnp.sum(grad_in * normed, axis=0))


def dot(a, b, ca, cb):
    return lax.dot_general(a, b, (((ca,), (cb,)), ((), ())), preferred_element_type=F32)


def block_keeps(lengths_ref, first, count):
    place = first + lax.broadcasted_iota(jnp.int32, (count, 1), 0)
    one = place != 0
    two = (place != 0) & (place != 1)
    start = 0
    for j in range(lengths_ref.shape[1] - 1):
        start = start + lengths_ref[0, j]
        one = one & (place != start)
        two = two & (place != start) & (place != start + 1)
    return one, two


def mixer_kernel(
    lengths_ref,
    x_ref,
    in_ref,
    out_ref,
    values_ref,
    h1_ref,
    keep_ref,
    z_ref,
    resid_ref,
    h2_ref,
    in_full_ref,
    out_full_ref,
    taps_full_ref,
    x_v,
    h1_v,
    z_v,
    in_v,
    out_v,
    taps_v,
    keep_v,
    resid_v,
    h2_v,
    last_v,
    load_sem,
    keep_sem,
    store_sem,
    side_sem,
    x_send,
    x_recv,
    y_send,
    y_recv,
    core_send,
    core_recv,
):
    me, side = lax.axis_index("dp"), lax.axis_index("tensor")
    other = 1 - side
    rows, width = x_v.shape
    half = width // 2
    blocks = rows // FRONT
    core_peer = me + 1 - 2 * lax.rem(me, 2)
    y_peer = me + 2 - 4 * ((me // 2) % 2)
    quarter = me % 4

    def piece(j, which, owner):
        if j < 6:
            size = width // 8
            at = pl.multiple_of(which * 2 * size + (j % 2) * size, size)
            return in_v.at[owner, pl.ds(at, size), pl.ds((j // 2) * half, half)]
        size = half // 8
        at = pl.multiple_of(which * 2 * size + (j % 2) * size, size)
        return out_v.at[owner, pl.ds(at, size)]

    def source(j):
        if j < 6:
            size = width // 8
            at = pl.multiple_of(quarter * 2 * size + (j % 2) * size, size)
            return in_ref.at[j // 2, pl.ds(at, size)]
        size = half // 8
        at = pl.multiple_of(quarter * 2 * size + (j % 2) * size, size)
        return out_ref.at[pl.ds(at, size)]

    def remote(src, dst, send, recv, device):
        return pltpu.make_async_remote_copy(
            src_ref=src, dst_ref=dst, send_sem=send, recv_sem=recv, device_id=device, device_id_type=MESH
        )

    def cross(j):
        return remote(source(j), piece(j, quarter, side), x_send.at[j], x_recv.at[j], (me, other))

    def along_y(j):
        ref = piece(j, quarter, other)
        return remote(ref, ref, y_send.at[j], y_recv.at[j], (y_peer, side))

    def to_core(j, which, slot):
        ref = piece(j, which, other)
        return remote(ref, ref, core_send.at[slot, j], core_recv.at[slot, j], (core_peer, side))

    y_quarter = quarter + 2 - 4 * (quarter // 2)
    first_core = lambda j: to_core(j, quarter, 0)
    second_core = lambda j: to_core(j, y_quarter, 1)
    taps_copy = remote(taps_v.at[side], taps_v.at[side], side_sem.at[0], side_sem.at[1], (me, other))

    def forward(j):
        cross(j).wait_recv()
        along_y(j).start()
        first_core(j).start()

    def forward_y(j):
        along_y(j).wait_recv()
        second_core(j).start()

    def arrived(j):
        first_core(j).wait_recv()
        second_core(j).wait_recv()

    load_x = pltpu.make_async_copy(x_ref, x_v, load_sem.at[0])
    load_out = pltpu.make_async_copy(out_ref, out_v.at[side], load_sem.at[2])
    load_in = [
        pltpu.make_async_copy(in_ref.at[k], in_v.at[side, :, pl.ds(k * half, half)], load_sem.at[3 + k])
        for k in range(3)
    ]
    taps_v[side] = values_ref[:, :half]
    load_x.start()
    for copy in load_in:
        copy.start()
    load_out.start()
    barrier = pltpu.get_barrier_semaphore()
    for device in ((me, other), (y_peer, side), (core_peer, side)):
        pl.semaphore_signal(barrier, inc=1, device_id=device, device_id_type=MESH)
    pl.semaphore_wait(barrier, 3)
    for j in range(PIECES):
        cross(j).start()
    taps_copy.start()
    last_v[...] = jnp.zeros_like(last_v)
    load_x.wait()
    for copy in load_in:
        copy.wait()

    def block_rows(i):
        return pl.ds(pl.multiple_of(i * FRONT, FRONT), FRONT)

    def keep_out(i, owner, slot):
        column = pl.multiple_of(owner * 4 * half, 4 * half)
        return pltpu.make_async_copy(
            keep_v.at[slot], keep_ref.at[block_rows(i), pl.ds(column, 4 * half)], keep_sem.at[slot]
        )

    def half_block(i, owner, slot):
        at = block_rows(i)
        parts = dot(h1_v[at, :], in_v[owner], 1, 0)
        b_part, c_part, x_part = (parts[:, :half], parts[:, half : 2 * half], parts[:, 2 * half :])
        m = b_part * x_part
        one, two = block_keeps(lengths_ref, i * FRONT, FRONT)
        row = lax.broadcasted_iota(jnp.int32, (FRONT, 1), 0)
        before = last_v[owner]
        m_one = jnp.where(row == 0, before[7:8], pltpu.roll(m, 1, 0))
        m_two = jnp.where(row == 0, before[6:7], jnp.where(row == 1, before[7:8], pltpu.roll(m, 2, 0)))
        last_v[owner] = m[FRONT - 8 :]
        taps = taps_v[owner]
        v = taps[2:3] * m + taps[3:4] * jnp.where(one, m_one, 0.0)
        v = v + taps[4:5] * jnp.where(two, m_two, 0.0)
        keep_v[slot, :, :half] = b_part.astype(BF)
        keep_v[slot, :, half : 2 * half] = c_part.astype(BF)
        keep_v[slot, :, 2 * half : 3 * half] = x_part.astype(BF)
        keep_v[slot, :, 3 * half :] = v.astype(BF)
        z_v[owner, at, :] = (c_part * v).astype(BF)

    for i in range(blocks):
        at = block_rows(i)
        x = x_v[at, :].astype(F32)
        h1_v[at, :] = (x * rms_scale(x) * values_ref[0:1, :]).astype(BF)
        if i >= 2:
            keep_out(i - 2, side, i % 2).wait()
        half_block(i, side, i % 2)
        keep_out(i, side, i % 2).start()
        forward(i)
    store_h1 = pltpu.make_async_copy(h1_v, h1_ref, store_sem.at[0])
    store_h1.start()
    for j in range(blocks, PIECES):
        forward_y(j - blocks)
        forward(j)
    for j in range(PIECES - blocks, PIECES - 2):
        forward_y(j)
    for j in range(PIECES - 2):
        arrived(j)
    taps_copy.wait()
    for copy in (keep_out(i, side, i % 2) for i in (blocks - 2, blocks - 1)):
        copy.wait()

    for i in range(blocks):
        if i >= 2:
            keep_out(i - 2, other, i % 2).wait()
        half_block(i, other, i % 2)
        keep_out(i, other, i % 2).start()
        if i == 1:
            forward_y(PIECES - 2)
        if i == 2:
            forward_y(PIECES - 1)
    store_z = pltpu.make_async_copy(z_v, z_ref, store_sem.at[1])
    store_z.start()
    load_out.wait()
    for j in (PIECES - 2, PIECES - 1):
        arrived(j)
    stores = [
        pltpu.make_async_copy(
            in_v.at[h], in_full_ref.at[:, pl.ds(h * 3 * half, 3 * half)], store_sem.at[2 + h]
        )
        for h in range(2)
    ]
    stores += [
        pltpu.make_async_copy(out_v.at[h], out_full_ref.at[pl.ds(h * half, half)], store_sem.at[4 + h])
        for h in range(2)
    ]
    stores += [
        pltpu.make_async_copy(
            taps_v.at[h], taps_full_ref.at[:, pl.ds(h * half, half)], store_sem.at[6 + h]
        )
        for h in range(2)
    ]
    for copy in stores:
        copy.start()
    for copy in (keep_out(i, other, i % 2) for i in (blocks - 2, blocks - 1)):
        copy.wait()

    def row_out(i):
        slot = lax.rem(i, 2)
        return (
            pltpu.make_async_copy(resid_v.at[slot], resid_ref.at[block_rows(i)], keep_sem.at[slot]),
            pltpu.make_async_copy(h2_v.at[slot], h2_ref.at[block_rows(i)], side_sem.at[2 + slot]),
        )

    for i in range(blocks):
        at = block_rows(i)
        if i >= 2:
            for copy in row_out(i - 2):
                copy.wait()
        z = jnp.concatenate([z_v[0, at, :], z_v[1, at, :]], 1)
        total = dot(z, out_v[...].reshape(width, width), 1, 0)
        resid = x_v[at, :].astype(F32) + total
        resid_v[i % 2] = resid
        h2_v[i % 2] = (resid * rms_scale(resid) * values_ref[1:2, :]).astype(BF)
        for copy in row_out(i):
            copy.start()
    for i in (blocks - 2, blocks - 1):
        for copy in row_out(i):
            copy.wait()
    for j in range(PIECES):
        cross(j).wait_send()
        along_y(j).wait_send()
        first_core(j).wait_send()
        second_core(j).wait_send()
    for copy in [store_h1, store_z, *stores]:
        copy.wait()


def mixer_forward(lengths, x, in_w, out_w, values):
    rows, width = x.shape
    half = out_w.shape[0]
    any_spec = pl.BlockSpec(memory_space=pl.ANY)
    vmem_spec = pl.BlockSpec(memory_space=pltpu.VMEM)
    dma = pltpu.SemaphoreType.DMA
    shape = jax.ShapeDtypeStruct
    low = shape((rows, width), BF)
    return pl.pallas_call(
        mixer_kernel,
        out_shape=(
            low,
            shape((rows, 4 * width), BF),
            shape((2, rows, half), BF),
            shape((rows, width), F32),
            low,
            shape((width, 3 * width), BF),
            shape((width, width), BF),
            shape((8, width), F32),
        ),
        in_specs=[pl.BlockSpec(memory_space=pltpu.SMEM)] + [any_spec] * 3 + [vmem_spec],
        out_specs=(any_spec,) * 8,
        scratch_shapes=[
            pltpu.VMEM((rows, width), BF),
            pltpu.VMEM((rows, width), BF),
            pltpu.VMEM((2, rows, half), BF),
            pltpu.VMEM((2, width, 3 * half), BF),
            pltpu.VMEM((2, half, width), BF),
            pltpu.VMEM((2, 8, half), F32),
            pltpu.VMEM((2, FRONT, 4 * half), BF),
            pltpu.VMEM((2, FRONT, width), F32),
            pltpu.VMEM((2, FRONT, width), BF),
            pltpu.VMEM((2, 8, half), F32),
            dma((6,)),
            dma((2,)),
            dma((8,)),
            dma((4,)),
            *[dma((PIECES,))] * 4,
            dma((2, PIECES)),
            dma((2, PIECES)),
        ],
        compiler_params=pltpu.CompilerParams(
            collective_id=2, has_side_effects=True, vmem_limit_bytes=VMEM_BYTES
        ),
    )(lengths, x, in_w, out_w, values)


def swiglu_kernel(h2_ref, gate_ref, up_ref, hid_ref, slope_ref, silu_ref):
    h2 = h2_ref[...]
    gate = dot(h2, gate_ref[...], 1, 0)
    up = dot(h2, up_ref[...], 1, 0)
    sig = jax.nn.sigmoid(gate)
    silu = gate * sig
    hid_ref[...] = (silu * up).astype(BF)
    slope_ref[...] = (up * sig * (1.0 + gate * (1.0 - sig))).astype(BF)
    silu_ref[...] = silu.astype(BF)


def swiglu(h2, gate_w, up_w):
    rows, width = h2.shape
    hidden = gate_w.shape[1]
    out = jax.ShapeDtypeStruct((rows, hidden), BF)
    row_spec = pl.BlockSpec((BLOCK, hidden), lambda i: (i, 0))
    whole = pl.BlockSpec((width, hidden), lambda i: (0, 0), pipeline_mode=pl.Buffered(1))
    return pl.pallas_call(
        swiglu_kernel,
        grid=(rows // BLOCK,),
        out_shape=(out, out, out),
        in_specs=[pl.BlockSpec((BLOCK, width), lambda i: (i, 0)), whole, whole],
        out_specs=(row_spec, row_spec, row_spec),
        compiler_params=pltpu.CompilerParams(vmem_limit_bytes=VMEM_BYTES),
    )(h2, gate_w, up_w)


class Reducer:
    def __init__(self, count, tiles, parts, whole, send, recv, kinds, out_sem):
        self.count = count
        self.tiles, self.parts, self.whole = tiles, parts, whole
        self.send, self.recv = send, recv
        self.kinds, self.out_sem = kinds, out_sem
        me, self.side = lax.axis_index("dp"), lax.axis_index("tensor")
        bit = [lax.rem(lax.div(me, 1 << b), 2) for b in range(4)]
        odd_core = bit[0] == 1
        self.plans = []
        for order in ((0, 1, 2, 3), (0, 2, 1, 3)):
            peer, keep, give, off = [], [], [], 0
            for s, b in enumerate(order):
                size = TILE_ROWS >> (s + 1)
                peer.append(me + (1 << b) * (1 - 2 * bit[b]))
                give.append(off + (1 - bit[b]) * size)
                off = off + bit[b] * size
                keep.append(off)
            self.plans.append((peer, keep, give))
        even, odd = self.plans
        self.plans[1] = tuple(
            [jnp.where(odd_core, o, e) for o, e in zip(odd[k], even[k])] for k in range(3)
        )

    def at(self, n, lag=0):
        sizes = (SLOTS, TILE_SLOTS, WHOLE_SLOTS) + PART_SLOTS
        if not isinstance(n, dict):
            n = {"n": n, "parity": lax.rem(n, 2), "slots": [lax.rem(n, size) for size in sizes]}
        slots = []
        for size, slot in zip(sizes, n["slots"]):
            back = slot - lag % size
            slots.append(jnp.where(back < 0, back + size, back) if lag % size else slot)
        parity = n["parity"] if lag % 2 == 0 else 1 - n["parity"]
        return {"n": n["n"] - lag, "parity": parity, "slots": slots}

    def plan(self, tile, s):
        even, odd = self.plans
        size = TILE_ROWS >> (s + 1)
        pick = [jnp.where(tile["parity"] == 1, odd[k][s], even[k][s]) for k in range(3)]
        return pick[0], pl.multiple_of(pick[1], size), pl.multiple_of(pick[2], size), size

    def scatter(self, tile, s):
        peer, keep, give, size = self.plan(tile, s)
        sem, slot, _, *part = tile["slots"]
        return pltpu.make_async_remote_copy(
            src_ref=self.tiles.at[slot, pl.ds(give, size)],
            dst_ref=self.parts[s].at[part[s]],
            send_sem=self.send.at[sem, s],
            recv_sem=self.recv.at[sem, s],
            device_id=(peer, self.side),
            device_id_type=MESH,
        )

    def gather(self, tile, s):
        peer, keep, give, size = self.plan(tile, s)
        sem, _, slot, *_ = tile["slots"]
        block = self.whole.at[slot, pl.ds(keep, size)]
        return pltpu.make_async_remote_copy(
            src_ref=block,
            dst_ref=block,
            send_sem=self.send.at[sem, 4 + s],
            recv_sem=self.recv.at[sem, 4 + s],
            device_id=(peer, self.side),
            device_id_type=MESH,
        )

    def write(self, tile, act):
        n = tile["n"]
        sem, _, slot, *_ = tile["slots"]
        for first, last, stride, pieces, place in self.kinds:
            size = TILE_ROWS // pieces

            @pl.when((n >= first) & (n < last) & (lax.rem(n - first, stride) == 0))
            def _():
                for q in range(pieces):
                    copy = pltpu.make_async_copy(
                        self.whole.at[slot, pl.ds(q * size, size)],
                        place(lax.div(n - first, stride), q),
                        self.out_sem.at[sem, q],
                    )
                    act(copy)

    def add(self, tile, s):
        peer, keep, give, size = self.plan(tile, s)
        _, slot, whole, *part = tile["slots"]
        rows = pl.ds(keep, size)
        total = self.tiles[slot, rows, :].astype(F32) + self.parts[s][part[s]].astype(F32)
        if s == 3:
            self.whole[whole, rows, :] = total.astype(BF)
        else:
            self.tiles[slot, rows, :] = total.astype(BF)

    def put(self, n, value):
        tile = self.at(n)
        self.tiles[tile["slots"][1]] = value.astype(BF)
        self.scatter(tile, 0).start()

    def put_blocks(self, n, value):
        tile = self.at(n)
        size = TILE_ROWS // 4
        for q in range(4):
            block = value[:, q * TILE_COLS : (q + 1) * TILE_COLS]
            self.tiles[tile["slots"][1], q * size : (q + 1) * size, :] = block.astype(BF)
        self.scatter(tile, 0).start()

    def tick(self, n):
        now = self.at(n)

        def stage(k, lag):
            m = now["n"] - lag

            @pl.when((m >= 0) & (m < self.count))
            def _():
                tile = self.at(now, lag)
                if k <= 4:
                    self.scatter(tile, k - 1).wait()
                    self.add(tile, k - 1)
                    if k < 4:
                        self.scatter(tile, k).start()
                    else:
                        self.gather(tile, 3).start()
                elif k <= 8:
                    self.gather(tile, 8 - k).wait()
                    if k < 8:
                        self.gather(tile, 7 - k).start()
                    else:
                        self.write(tile, lambda copy: copy.start())
                else:
                    self.write(tile, lambda copy: copy.wait())

        for k in (1, 6, 2, 3, 4, 5, 7, 8, 9):
            stage(k, LAGS[k - 1])


def back_kernel(
    lengths_ref,
    hid_ref,
    slope_ref,
    silu_ref,
    h2_ref,
    dy_ref,
    gate_ref,
    up_ref,
    down_ref,
    resid_ref,
    x_ref,
    keep_ref,
    z_ref,
    h1_ref,
    in_ref,
    out_ref,
    values_ref,
    taps_ref,
    down_sum_ref,
    gate_sum_ref,
    up_sum_ref,
    out_sum_ref,
    in_sum_ref,
    dgu_ref,
    dh2_own_ref,
    dh2_got_ref,
    ffn_own_ref,
    ffn_got_ref,
    dp_ref,
    grad_ref,
    result_ref,
    small_ref,
    dy_v,
    h2_v,
    wide_v,
    down_v,
    tile_v,
    row_v,
    small_v,
    small_in,
    next_v,
    tiles,
    whole,
    part0,
    part1,
    part2,
    part3,
    load_sem,
    tile_sem,
    stream_sem,
    dgu_sem,
    own_sem,
    hid_sem,
    dp_sem,
    grad_sem,
    small_send,
    small_recv,
    x_send,
    x_recv,
    send,
    recv,
    out_sem,
):
    me, side = lax.axis_index("dp"), lax.axis_index("tensor")
    rows, width = dy_v.shape
    hidden = hid_ref.shape[1]
    half = width // 2
    blocks = rows // BLOCK
    n_down = hidden // TILE_COLS
    n_out = half // TILE_COLS
    first_gate, first_out = n_down, 3 * n_down
    first_late = first_gate + 4
    first_in = first_out + n_out
    count = first_in + 3 * n_out

    def rows_of(ref):
        return lambda t, q: ref.at[
            pl.ds(pl.multiple_of(t * TILE_COLS, TILE_COLS), TILE_COLS), pl.ds(q * TILE_COLS, TILE_COLS)
        ]

    def columns_of(ref):
        return lambda t, q: ref.at[:, pl.ds(pl.multiple_of(t * TILE_COLS, TILE_COLS), TILE_COLS)]

    def in_place(t, q):
        column = pl.multiple_of(lax.rem(t, n_out) * TILE_COLS, TILE_COLS)
        return in_sum_ref.at[lax.div(t, n_out), :, pl.ds(column, TILE_COLS)]

    kinds = (
        (0, first_gate, 1, 4, rows_of(down_sum_ref)),
        (first_gate, first_out, 2, 1, columns_of(gate_sum_ref)),
        (first_gate + 1, first_out, 2, 1, columns_of(up_sum_ref)),
        (first_out, first_in, 1, 4, rows_of(out_sum_ref)),
        (first_in, count, 1, 1, in_place),
    )
    red = Reducer(count, tiles, (part0, part1, part2, part3), whole, send, recv, kinds, out_sem)

    def peer(bit):
        return me + bit * (1 - 2 * ((me // bit) % 2))

    def block_rows(i):
        return pl.ds(pl.multiple_of((blocks - 1 - i) * BLOCK, BLOCK), BLOCK)

    load_dy = pltpu.make_async_copy(dy_ref, dy_v, load_sem.at[0])
    load_down = pltpu.make_async_copy(down_ref, down_v, load_sem.at[1])
    load_gate = pltpu.make_async_copy(gate_ref, wide_v.at[:, pl.ds(0, hidden)], load_sem.at[2])
    load_up = pltpu.make_async_copy(up_ref, wide_v.at[:, pl.ds(hidden, hidden)], load_sem.at[3])
    load_h2 = pltpu.make_async_copy(h2_ref, h2_v, load_sem.at[4])
    load_in = pltpu.make_async_copy(in_ref, wide_v.at[:, pl.ds(0, 3 * width)], load_sem.at[2])
    load_out = pltpu.make_async_copy(out_ref, wide_v.at[:, pl.ds(3 * width, width)], load_sem.at[3])
    load_h1 = pltpu.make_async_copy(h1_ref, h2_v, load_sem.at[4])

    def tile_of(ref, column, n):
        column = pl.multiple_of(column, TILE_COLS)
        return pltpu.make_async_copy(
            ref.at[:, pl.ds(column, TILE_COLS)], tile_v.at[lax.rem(n, 2)], tile_sem.at[lax.rem(n, 2)]
        )

    def hid_tile(n):
        return tile_of(hid_ref, n * TILE_COLS, n)

    def dgu_tile(n):
        k = n - first_gate
        return tile_of(dgu_ref, lax.rem(k, 2) * hidden + lax.div(k, 2) * TILE_COLS, n)

    def z_tile(n):
        return tile_of(z_ref.at[side], (n - first_out) * TILE_COLS, n)

    def dp_tile(n):
        return tile_of(dp_ref, (n - first_in) * TILE_COLS, n)

    def row_own(i, ref):
        slot = lax.rem(i, 2)
        return pltpu.make_async_copy(row_v.at[slot], ref.at[block_rows(i)], own_sem.at[slot])

    def row_send(i, own, got, first):
        at = block_rows(i)
        return pltpu.make_async_remote_copy(
            src_ref=own.at[at],
            dst_ref=got.at[at],
            send_sem=x_send.at[first + i],
            recv_sem=x_recv.at[first + i],
            device_id=(me, 1 - side),
            device_id_type=MESH,
        )

    def dh2_send(i):
        return row_send(i, dh2_own_ref, dh2_got_ref, 0)

    def ffn_send(i):
        return row_send(i, ffn_own_ref, ffn_got_ref, blocks)

    def small_copy(s):
        return pltpu.make_async_remote_copy(
            src_ref=small_v,
            dst_ref=small_in.at[s],
            send_sem=small_send.at[s],
            recv_sem=small_recv.at[s],
            device_id=(peer(1 << s), side),
            device_id_type=MESH,
        )

    def small_add(s):
        small_copy(s).wait()
        small_v[...] = small_v[...] + small_in[s]

    load_dy.start()
    hid_tile(0).start()
    load_down.start()
    load_gate.start()
    load_up.start()
    load_h2.start()

    barrier = pltpu.get_barrier_semaphore()
    for bit in (1, 2, 4, 8):
        pl.semaphore_signal(barrier, inc=1, device_id=(peer(bit), side), device_id_type=MESH)
    pl.semaphore_signal(barrier, inc=1, device_id=(me, 1 - side), device_id_type=MESH)
    pl.semaphore_wait(barrier, 5)

    small_v[...] = jnp.zeros_like(small_v)
    next_v[...] = jnp.zeros_like(next_v)

    def down_step(n, carry):
        @pl.when(n + 1 < n_down)
        def _():
            hid_tile(n + 1).start()

        hid_tile(n).wait()
        red.put_blocks(n, dot(tile_v[lax.rem(n, 2)], dy_v[...], 0, 0))
        return carry

    def grads(slope_v, silu_v, dgu_v):
        def pair(i):
            at = block_rows(i)
            return (
                pltpu.make_async_copy(slope_ref.at[at], slope_v.at[lax.rem(i, 2)], stream_sem.at[lax.rem(i, 2), 0]),
                pltpu.make_async_copy(silu_ref.at[at], silu_v.at[lax.rem(i, 2)], stream_sem.at[lax.rem(i, 2), 1]),
            )

        def dgu_out(i):
            return pltpu.make_async_copy(
                dgu_v.at[lax.rem(i, 2)], dgu_ref.at[block_rows(i)], dgu_sem.at[lax.rem(i, 2)]
            )

        for copy in pair(0):
            copy.start()
        load_dy.wait()
        def down_group(g, carry):
            lax.fori_loop(3 * g, 3 * g + 3, down_step, 0)
            red.tick(1 + g)
            return carry

        lax.fori_loop(0, n_down // 3, down_group, 0)
        load_down.wait()
        load_gate.wait()
        load_up.wait()

        def early_tiles(j):
            column = pl.ds(pl.multiple_of(j * TILE_COLS, TILE_COLS), TILE_COLS)
            return (
                pltpu.make_async_copy(slope_ref.at[:, column], tile_v.at[0], tile_sem.at[0]),
                pltpu.make_async_copy(silu_ref.at[:, column], tile_v.at[1], tile_sem.at[1]),
            )

        def early(j):
            for copy in early_tiles(j):
                copy.wait()
            n = first_gate + 2 * j
            hidden_rows = pl.ds(pl.multiple_of(j * TILE_COLS, TILE_COLS), TILE_COLS)
            d_hid = dot(dy_v[...], down_v[hidden_rows, :], 1, 1)
            red.put(n, dot(h2_v[...], (d_hid * tile_v[0].astype(F32)).astype(BF), 0, 0))
            red.put(n + 1, dot(h2_v[...], (d_hid * tile_v[1].astype(F32)).astype(BF), 0, 0))
            red.tick(8 + 3 * j)

            @pl.when(j == 0)
            def _():
                for copy in early_tiles(1):
                    copy.start()

        for copy in early_tiles(0):
            copy.start()
        load_h2.wait()

        def grad_step(i, carry):
            slot = lax.rem(i, 2)

            @pl.when(i + 1 < blocks)
            def _():
                for copy in pair(i + 1):
                    copy.start()

            for copy in pair(i):
                copy.wait()

            @pl.when(i >= 2)
            def _():
                dgu_out(i - 2).wait()

            d_hid = dot(dy_v[block_rows(i), :], down_v[...], 1, 1)
            dgu_v[slot, :, :hidden] = (d_hid * slope_v[slot].astype(F32)).astype(BF)
            dgu_v[slot, :, hidden:] = (d_hid * silu_v[slot].astype(F32)).astype(BF)
            dgu_out(i).start()
            row_v[slot] = dot(dgu_v[slot], wide_v[...], 1, 1).astype(BF)
            row_own(i, dh2_own_ref).start()

            red.tick(4 + i + jnp.where(i >= 4, 1, 0) + jnp.where(i >= 6, 1, 0))
            row_own(i, dh2_own_ref).wait()
            dh2_send(i).start()

            @pl.when((i == 3) | (i == 5))
            def _():
                early(lax.div(i - 3, 2))
            return carry

        lax.fori_loop(0, blocks, grad_step, 0)
        load_in.start()
        load_out.start()
        for i in (blocks - 2, blocks - 1):
            dgu_out(i).wait()
        dgu_tile(first_late).start()

    pl.run_scoped(
        grads,
        pltpu.VMEM((2, BLOCK, hidden), BF),
        pltpu.VMEM((2, BLOCK, hidden), BF),
        pltpu.VMEM((2, BLOCK, 2 * hidden), BF),
    )

    def gate_put(n):
        dgu_tile(n).wait()
        red.put(n, dot(h2_v[...], tile_v[lax.rem(n, 2)], 0, 0))

    late = blocks // 2
    twice = first_out - first_late - blocks

    def hid_rows(i, hid_v):
        slot = lax.rem(i, 2)
        return pltpu.make_async_copy(hid_ref.at[block_rows(i)], hid_v.at[slot], hid_sem.at[slot])

    def ffn_block(i, hid_v):
        @pl.when((i + 1 < late) | ((i >= late) & (i + 1 < blocks)))
        def _():
            hid_rows(i + 1, hid_v).start()

        hid_rows(i, hid_v).wait()
        slot = lax.rem(i, 2)
        row_v[slot] = dot(hid_v[slot], down_v[...], 1, 0).astype(BF)
        row_own(i, ffn_own_ref).start()

    def ffn_pass(i):
        row_own(i, ffn_own_ref).wait()
        ffn_send(i).start()

    def mixer(keep_v, resid_v, x_v, pair_v, hid_v, dp_v, grad_v, dr1_v):
        def inputs(i):
            at, slot = block_rows(i), lax.rem(i, 2)
            return (
                pltpu.make_async_copy(keep_ref.at[at], keep_v.at[slot], stream_sem.at[slot, 0]),
                pltpu.make_async_copy(resid_ref.at[at], resid_v.at[slot], stream_sem.at[slot, 1]),
                pltpu.make_async_copy(x_ref.at[at], x_v.at[slot], stream_sem.at[slot, 2]),
                pltpu.make_async_copy(dh2_own_ref.at[at], pair_v.at[0], stream_sem.at[slot, 3]),
            )

        def got(i):
            return pltpu.make_async_copy(dh2_got_ref.at[block_rows(i)], pair_v.at[1], dgu_sem.at[0])

        def dp_out(i):
            column = pl.multiple_of(side * 3 * half, 3 * half)
            return pltpu.make_async_copy(
                dp_v.at[:, pl.ds(column, 3 * half)], dp_ref.at[block_rows(i)], dp_sem
            )

        def put_dp(k, value):
            for h in range(2):
                first = (3 * h + k) * half
                dp_v[:, first : first + half] = value[:, h * half : (h + 1) * half].astype(BF)

        def kept(slot, k):
            return jnp.concatenate(
                [keep_v[slot, :, (4 * h + k) * half : (4 * h + k + 1) * half] for h in range(2)], 1
            ).astype(F32)

        def grad_out(i):
            return pltpu.make_async_copy(grad_v, grad_ref.at[block_rows(i)], grad_sem)

        def finish(i):
            dp_out(i).wait()
            grad_out(i).wait()

        def mixer_first(i):
            slot = lax.rem(i, 2)
            at = block_rows(i)
            for copy in inputs(i):
                copy.wait()
            got(i).wait()

            @pl.when(i > 0)
            def _():
                finish(i - 1)

            resid = resid_v[slot]
            scale2 = rms_scale(resid)
            n2 = resid * scale2
            dh2 = pair_v[0].astype(F32) + pair_v[1].astype(F32)
            d_resid, gain2_part = norm_back(dh2, n2, scale2, values_ref[1:2, :])
            dr1 = dy_v[at, :].astype(F32) + d_resid
            dr1b = dr1.astype(BF)
            dr1_v[...] = dr1
            dy_v[at, :] = dr1b
            dz = dot(dr1b, wide_v[:, 3 * width : 4 * width], 1, 1)
            put_dp(1, dz * kept(slot, 3))
            dv = dz * kept(slot, 1)
            b_part = kept(slot, 0)
            x_part = kept(slot, 2)
            m = b_part * x_part
            one, two = block_keeps(lengths_ref, (blocks - 1 - i) * BLOCK, BLOCK)
            row = lax.broadcasted_iota(jnp.int32, (BLOCK, 1), 0)
            dv_one = jnp.where(one, dv, 0.0)
            dv_two = jnp.where(two, dv, 0.0)
            up_one = jnp.where(row == BLOCK - 1, next_v[0:1, :], pltpu.roll(dv_one, BLOCK - 1, 0))
            up_two = jnp.where(
                row == BLOCK - 2,
                next_v[8:9, :],
                jnp.where(row == BLOCK - 1, next_v[9:10, :], pltpu.roll(dv_two, BLOCK - 2, 0)),
            )
            next_v[0:8, :] = dv_one[0:8]
            next_v[8:16, :] = dv_two[0:8]
            taps = taps_ref[2:5, :]
            dm = taps[0:1] * dv + taps[1:2] * up_one + taps[2:3] * up_two
            put_dp(0, dm * x_part)
            put_dp(2, dm * b_part)
            dp_out(i).start()
            small_v[1:2, :] += gain2_part.reshape(1, width)
            small_v[2:3, :] += jnp.sum(dv * m, axis=0, keepdims=True)
            small_v[3:4, :] += jnp.sum(up_one * m, axis=0, keepdims=True)
            small_v[4:5, :] += jnp.sum(up_two * m, axis=0, keepdims=True)

        def mixer_second(i):
            dh1 = dot(dp_v[...], wide_v[:, : 3 * width], 1, 1)
            x = x_v[lax.rem(i, 2)].astype(F32)
            scale1 = rms_scale(x)
            d_input, gain1_part = norm_back(dh1, x * scale1, scale1, values_ref[0:1, :])
            grad_v[...] = (dr1_v[...] + d_input).astype(BF)
            grad_out(i).start()
            small_v[0:1, :] += gain1_part.reshape(1, width)

        hid_rows(0, hid_v).start()
        for copy in inputs(0):
            copy.start()
        load_in.wait()
        load_out.wait()

        def mixer_step(i, carry):
            n = first_late + i + jnp.minimum(i, twice)
            dh2_send(i).wait_recv()
            got(i).start()

            @pl.when(n + 1 < first_out)
            def _():
                dgu_tile(n + 1).start()

            @pl.when(n + 1 == first_out)
            def _():
                z_tile(n + 1).start()

            gate_put(n)
            mixer_first(i)
            red.tick(n + 1)
            mixer_second(i)

            @pl.when(i + 1 < blocks)
            def _():
                for copy in inputs(i + 1):
                    copy.start()

            @pl.when(i >= late)
            def _():
                ffn_block(i - late, hid_v)

            @pl.when(i < twice)
            def _():
                dgu_tile(n + 2).start()
                gate_put(n + 1)

            @pl.when(i >= late)
            def _():
                ffn_pass(i - late)

            @pl.when(i < twice)
            def _():
                red.tick(n + 2)

            return carry

        lax.fori_loop(0, blocks, mixer_step, 0)
        finish(blocks - 1)

    pl.run_scoped(
        mixer,
        pltpu.VMEM((2, BLOCK, 4 * width), BF),
        pltpu.VMEM((2, BLOCK, width), F32),
        pltpu.VMEM((2, BLOCK, width), BF),
        pltpu.VMEM((2, BLOCK, width), BF),
        pltpu.VMEM((2, BLOCK, hidden), BF),
        pltpu.VMEM((BLOCK, 3 * width), BF),
        pltpu.VMEM((BLOCK, width), BF),
        pltpu.VMEM((BLOCK, width), F32),
    )

    small_copy(0).start()

    def tail(resid_v, pair_v, result_v, hid_v):
        def inputs(i):
            at = block_rows(i)
            return (
                pltpu.make_async_copy(resid_ref.at[at], resid_v, stream_sem.at[0, 0]),
                pltpu.make_async_copy(ffn_own_ref.at[at], pair_v.at[0], stream_sem.at[0, 1]),
                pltpu.make_async_copy(ffn_got_ref.at[at], pair_v.at[1], stream_sem.at[0, 2]),
            )

        def result_out(i):
            return pltpu.make_async_copy(result_v, result_ref.at[block_rows(i)], grad_sem)

        def post(p):
            i = lax.div(p, 2)

            @pl.when((lax.rem(p, 2) == 0) & (i < blocks))
            def _():
                ffn_send(i).wait_recv()
                for copy in inputs(i):
                    copy.start()

            @pl.when((lax.rem(p, 2) == 1) & (i < blocks))
            def _():
                for copy in inputs(i):
                    copy.wait()

                @pl.when(i > 0)
                def _():
                    result_out(i - 1).wait()

                both = pair_v[0].astype(F32) + pair_v[1].astype(F32)
                result_v[...] = (resid_v[...] + both).astype(BF)
                result_out(i).start()

        base = first_out

        def step(n, put):
            i = late + n - base

            @pl.when(i < blocks)
            def _():
                ffn_block(i, hid_v)

            put(n)

            @pl.when(i < blocks)
            def _():
                ffn_pass(i)

            red.tick(n + 1)
            post(n - base)

        hid_rows(late, hid_v).start()

        load_h1.start()

        def out_put(n):
            z_tile(n).wait()
            red.put_blocks(n, dot(tile_v[lax.rem(n, 2)], dy_v[...], 0, 0))

        for n in range(first_out, first_in):
            (z_tile if n + 1 < first_in else dp_tile)(n + 1).start()
            step(n, out_put)
        small_add(0)
        small_copy(1).start()
        load_h1.wait()

        def in_step(n, carry):
            @pl.when(n + 1 < count)
            def _():
                dp_tile(n + 1).start()

            def in_put(n):
                dp_tile(n).wait()
                red.put(n, dot(h2_v[...], tile_v[lax.rem(n, 2)], 0, 0))

            step(n, in_put)
            return carry

        third = (count - first_in) // 3
        lax.fori_loop(first_in, first_in + third, in_step, 0)
        small_add(1)
        small_copy(2).start()
        lax.fori_loop(first_in + third, first_in + 2 * third, in_step, 0)
        small_add(2)
        small_copy(3).start()
        lax.fori_loop(first_in + 2 * third, count, in_step, 0)
        small_add(3)
        small_out = pltpu.make_async_copy(small_v, small_ref, load_sem.at[0])
        small_out.start()

        def drain_step(n, carry):
            red.tick(n + 1)
            post(n - base)
            return carry

        lax.fori_loop(count, count + LAGS[-1] - 1, drain_step, 0)
        result_out(blocks - 1).wait()
        small_out.wait()
        for i in range(blocks):
            dh2_send(i).wait_send()
            ffn_send(i).wait_send()

    pl.run_scoped(
        tail,
        pltpu.VMEM((BLOCK, width), F32),
        pltpu.VMEM((2, BLOCK, width), BF),
        pltpu.VMEM((BLOCK, width), BF),
        pltpu.VMEM((2, BLOCK, hidden), BF),
    )


def block_backward(
    lengths, hid, slope, silu, h2, dy, gate_w, up_w, down_w, resid, x, keep, z, h1, in_full, out_full,
    values, taps,
):
    rows, hidden = hid.shape
    width = h2.shape[1]
    blocks = rows // BLOCK
    any_spec = pl.BlockSpec(memory_space=pl.ANY)
    vmem_spec = pl.BlockSpec(memory_space=pltpu.VMEM)
    dma = pltpu.SemaphoreType.DMA
    shape = jax.ShapeDtypeStruct
    low = shape((rows, width), BF)
    ring = [pltpu.VMEM((slots, TILE_ROWS, TILE_COLS), BF) for slots in (TILE_SLOTS, WHOLE_SLOTS)]
    ring += [
        pltpu.VMEM((slots, TILE_ROWS >> (s + 1), TILE_COLS), BF) for s, slots in enumerate(PART_SLOTS)
    ]
    return pl.pallas_call(
        back_kernel,
        out_shape=(
            shape(down_w.shape, BF),
            shape(gate_w.shape, BF),
            shape(up_w.shape, BF),
            shape((width // 2, width), BF),
            shape((3, width, width // 2), BF),
            shape((rows, 2 * hidden), BF),
            low,
            low,
            low,
            low,
            shape((rows, 3 * width // 2), BF),
            low,
            low,
            shape((8, width), F32),
        ),
        in_specs=[pl.BlockSpec(memory_space=pltpu.SMEM)] + [any_spec] * 15 + [vmem_spec] * 2,
        out_specs=(any_spec,) * 14,
        scratch_shapes=[
            pltpu.VMEM((rows, width), BF),
            pltpu.VMEM((rows, width), BF),
            pltpu.VMEM((width, 2 * hidden), BF),
            pltpu.VMEM(down_w.shape, BF),
            pltpu.VMEM((2, rows, TILE_COLS), BF),
            pltpu.VMEM((2, BLOCK, width), BF),
            pltpu.VMEM((8, width), F32),
            pltpu.VMEM((4, 8, width), F32),
            pltpu.VMEM((16, width), F32),
            *ring,
            dma((5,)),
            dma((2,)),
            dma((2, 4)),
            dma((2,)),
            dma((2,)),
            dma((2,)),
            dma,
            dma,
            dma((4,)),
            dma((4,)),
            dma((2 * blocks,)),
            dma((2 * blocks,)),
            dma((SLOTS, 8)),
            dma((SLOTS, 8)),
            dma((SLOTS, 4)),
        ],
        compiler_params=pltpu.CompilerParams(
            collective_id=1, has_side_effects=True, vmem_limit_bytes=VMEM_BYTES
        ),
    )(
        lengths, hid, slope, silu, h2, dy, gate_w, up_w, down_w, resid, x, keep, z, h1, in_full, out_full,
        values, taps,
    )


def pair_body(
    tokens,
    cotangent,
    lengths,
    mixer_gain,
    in_weight,
    conv_weight,
    out_weight,
    ffn_gain,
    gate_weight,
    up_weight,
    down_weight,
):
    side = lax.axis_index("tensor")
    half = out_weight.shape[0]
    width = tokens.shape[1]
    values = jnp.zeros((8, width), F32)
    values = values.at[0].set(mixer_gain.astype(F32)).at[1].set(ffn_gain.astype(F32))
    values = values.at[2:5, :half].set(conv_weight.astype(F32))
    h1b, keep, zb, resid, h2b, in_full, out_full, taps = mixer_forward(
        lengths, tokens, in_weight.transpose(1, 0, 2), out_weight, values
    )
    hidb, slope, silu = swiglu(h2b, gate_weight, up_weight)
    down_sum, gate_sum, up_sum, out_sum, in_sum, *_, input_grad, output, small = block_backward(
        lengths, hidb, slope, silu, h2b, cotangent, gate_weight, up_weight, down_weight, resid, tokens,
        keep, zb, h1b, in_full, out_full, values, taps,
    )
    return (
        output,
        input_grad,
        small[0],
        in_sum.astype(F32).transpose(1, 0, 2),
        lax.dynamic_slice_in_dim(small[2:5], side * half, half, 1),
        out_sum.astype(F32),
        small[1],
        gate_sum.astype(F32),
        up_sum.astype(F32),
        down_sum.astype(F32),
    )


def body(
    tokens,
    cotangent,
    lengths,
    mixer_gain,
    in_weight,
    conv_weight,
    out_weight,
    ffn_gain,
    gate_weight,
    up_weight,
    down_weight,
):
    rows = tokens.shape[0]
    dist = distances(lengths[0], rows)
    keep_one = (dist >= 1)[:, None].astype(jnp.float32)
    keep_two = (dist >= 2)[:, None].astype(jnp.float32)
    parts = lax.axis_size("tensor")
    share = rows // parts
    first = lax.axis_index("tensor") * share
    x = tokens.astype(jnp.float32)
    dy = cotangent.astype(jnp.float32)
    g1 = mixer_gain.astype(jnp.float32)
    g2 = ffn_gain.astype(jnp.float32)
    taps = conv_weight.astype(jnp.float32)
    scale1 = rms_scale(x)
    normed1 = x * scale1
    h1b = (normed1 * g1).astype(jnp.bfloat16)
    proj = jnp.einsum("td,dkc->tkc", h1b, in_weight, preferred_element_type=jnp.float32)
    b_part, c_part, x_part = (proj[:, 0], proj[:, 1], proj[:, 2])
    mixed = b_part * x_part
    mixed_one = shift_down(mixed, 1, keep_one)
    mixed_two = shift_down(mixed, 2, keep_two)
    conv_out = taps[0] * mixed + taps[1] * mixed_one + taps[2] * mixed_two
    zb = (c_part * conv_out).astype(jnp.bfloat16)
    mix_part = jnp.dot(zb, out_weight, preferred_element_type=jnp.float32)
    mix_rows = lax.psum_scatter(mix_part, "tensor", scatter_dimension=0, tiled=True)
    x_rows = lax.dynamic_slice_in_dim(x, first, share, 0)
    resid = x_rows + mix_rows
    scale2 = rms_scale(resid)
    normed2 = resid * scale2
    h2b = lax.all_gather((normed2 * g2).astype(jnp.bfloat16), "tensor", axis=0, tiled=True)
    gate = jnp.dot(h2b, gate_weight, preferred_element_type=jnp.float32)
    up = jnp.dot(h2b, up_weight, preferred_element_type=jnp.float32)
    sig = jax.nn.sigmoid(gate)
    silu = gate * sig
    hidb = (silu * up).astype(jnp.bfloat16)
    ffn_part = jnp.dot(hidb, down_weight, preferred_element_type=jnp.float32)
    down_grad = jnp.einsum("tf,td->fd", hidb, cotangent, preferred_element_type=jnp.float32)
    d_hid = jnp.einsum("td,fd->tf", cotangent, down_weight, preferred_element_type=jnp.float32)
    d_gate = (d_hid * up * sig * (1.0 + gate * (1.0 - sig))).astype(jnp.bfloat16)
    d_up = (d_hid * silu).astype(jnp.bfloat16)
    gate_grad = jnp.einsum("td,tf->df", h2b, d_gate, preferred_element_type=jnp.float32)
    up_grad = jnp.einsum("td,tf->df", h2b, d_up, preferred_element_type=jnp.float32)
    dh2_part = jnp.einsum("tf,df->td", d_gate, gate_weight, preferred_element_type=jnp.float32)
    dh2_part = dh2_part + jnp.einsum(
        "tf,df->td", d_up, up_weight, preferred_element_type=jnp.float32
    )
    ffn_rows = lax.psum_scatter(
        ffn_part.astype(jnp.bfloat16), "tensor", scatter_dimension=0, tiled=True
    ).astype(jnp.float32)
    output = lax.all_gather((resid + ffn_rows).astype(jnp.bfloat16), "tensor", axis=0, tiled=True)
    dh2_rows = lax.psum_scatter(dh2_part, "tensor", scatter_dimension=0, tiled=True)
    d_resid, g2_grad = norm_back(dh2_rows, normed2, scale2, g2)
    dr1 = lax.dynamic_slice_in_dim(dy, first, share, 0) + d_resid
    dr1b = lax.all_gather(dr1.astype(jnp.bfloat16), "tensor", axis=0, tiled=True)
    out_grad = jnp.einsum("tc,td->cd", zb, dr1b, preferred_element_type=jnp.float32)
    d_z = jnp.einsum("td,cd->tc", dr1b, out_weight, preferred_element_type=jnp.float32)
    d_c = d_z * conv_out
    d_conv = d_z * c_part
    conv_grad = jnp.stack(
        [
            jnp.sum(d_conv * mixed, axis=0),
            jnp.sum(d_conv * mixed_one, axis=0),
            jnp.sum(d_conv * mixed_two, axis=0),
        ],
        0,
    )
    d_mixed = (
        taps[0] * d_conv
        + taps[1] * shift_up(d_conv * keep_one, 1)
        + taps[2] * shift_up(d_conv * keep_two, 2)
    )
    d_proj = jnp.stack([d_mixed * x_part, d_c, d_mixed * b_part], 1).astype(jnp.bfloat16)
    in_grad_w = jnp.einsum("td,tkc->dkc", h1b, d_proj, preferred_element_type=jnp.float32)
    dh1_part = jnp.einsum("tkc,dkc->td", d_proj, in_weight, preferred_element_type=jnp.float32)
    dh1_rows = lax.psum_scatter(dh1_part, "tensor", scatter_dimension=0, tiled=True)
    normed1_rows = lax.dynamic_slice_in_dim(normed1, first, share, 0)
    scale1_rows = lax.dynamic_slice_in_dim(scale1, first, share, 0)
    d_input, g1_grad = norm_back(dh1_rows, normed1_rows, scale1_rows, g1)
    input_grad = lax.all_gather((dr1 + d_input).astype(jnp.bfloat16), "tensor", axis=0, tiled=True)
    g1_grad, g2_grad = lax.psum((g1_grad, g2_grad), "tensor")
    summed = lax.psum(
        (g1_grad, in_grad_w, conv_grad, out_grad, g2_grad, gate_grad, up_grad, down_grad), "dp"
    )
    return (
        output,
        input_grad,
        summed[0],
        summed[1],
        summed[2],
        summed[3],
        summed[4],
        summed[5],
        summed[6],
        summed[7],
    )


def solution(mesh):
    paired = mesh.shape["tensor"] == 2 and mesh.shape["dp"] == 16
    return jax.shard_map(
        pair_body if paired else body,
        mesh=mesh,
        in_specs=(
            P("dp", None),
            P("dp", None),
            P("dp", None),
            P(),
            P(None, None, "tensor"),
            P(None, "tensor"),
            P("tensor", None),
            P(),
            P(None, "tensor"),
            P(None, "tensor"),
            P("tensor", None),
        ),
        out_specs=(
            P("dp", None),
            P("dp", None),
            P(),
            P(None, None, "tensor"),
            P(None, "tensor"),
            P("tensor", None),
            P(),
            P(None, "tensor"),
            P(None, "tensor"),
            P("tensor", None),
        ),
        check_vma=False,
    )
```

```python
import jax
import jax.numpy as jnp
from jax import lax
from jax.experimental import pallas as pl
from jax.experimental.pallas import tpu as pltpu
from jax.sharding import PartitionSpec as P

EPS = 1e-05
F32 = jnp.float32
BF = jnp.bfloat16
MESH = pl.DeviceIdType.MESH
TILE_ROWS, TILE_COLS = 1024, 256
BLOCK = 256
SLOTS, TILE_SLOTS, PART_SLOTS, WHOLE_SLOTS = 16, 10, (9, 8, 8, 8), 15
LAGS = (1, 3, 5, 7, 9, 11, 13, 14, 15)
FRONT = 512
PIECES = 8
VMEM_BYTES = 61 << 20


def distances(lengths, count):
    ends = jnp.cumsum(lengths)
    starts = ends - lengths
    places = jnp.arange(count, dtype=jnp.int32)
    begin = jnp.max(jnp.where(starts[None, :] <= places[:, None], starts[None, :], 0), axis=1)
    return places - begin


def rms_scale(value):
    return lax.rsqrt(jnp.mean(value * value, axis=-1, keepdims=True) + EPS)


def shift_down(value, steps, keep):
    moved = jnp.concatenate([jnp.zeros_like(value[:steps]), value[:-steps]], 0)
    return moved * keep


def shift_up(value, steps):
    return jnp.concatenate([value[steps:], jnp.zeros_like(value[:steps])], 0)


def norm_back(grad_in, normed, scale, gain):
    weighted = grad_in * gain
    inner = jnp.mean(weighted * normed, axis=-1, keepdims=True)
    return (scale * (weighted - normed * inner), jnp.sum(grad_in * normed, axis=0))


def dot(a, b, ca, cb):
    return lax.dot_general(a, b, (((ca,), (cb,)), ((), ())), preferred_element_type=F32)


def block_keeps(lengths_ref, first, count):
    place = first + lax.broadcasted_iota(jnp.int32, (count, 1), 0)
    one = place != 0
    two = (place != 0) & (place != 1)
    start = 0
    for j in range(lengths_ref.shape[1] - 1):
        start = start + lengths_ref[0, j]
        one = one & (place != start)
        two = two & (place != start) & (place != start + 1)
    return one, two


def mixer_kernel(
    lengths_ref,
    x_ref,
    in_ref,
    out_ref,
    values_ref,
    h1_ref,
    keep_ref,
    z_ref,
    resid_ref,
    h2_ref,
    in_full_ref,
    out_full_ref,
    taps_full_ref,
    x_v,
    h1_v,
    z_v,
    in_v,
    out_v,
    taps_v,
    keep_v,
    resid_v,
    h2_v,
    last_v,
    load_sem,
    keep_sem,
    store_sem,
    side_sem,
    x_send,
    x_recv,
    y_send,
    y_recv,
    core_send,
    core_recv,
):
    me, side = lax.axis_index("dp"), lax.axis_index("tensor")
    other = 1 - side
    rows, width = x_v.shape
    half = width // 2
    blocks = rows // FRONT
    core_peer = me + 1 - 2 * lax.rem(me, 2)
    y_peer = me + 2 - 4 * ((me // 2) % 2)
    quarter = me % 4

    def piece(j, which, owner):
        if j < 6:
            size = width // 8
            at = pl.multiple_of(which * 2 * size + (j % 2) * size, size)
            return in_v.at[owner, pl.ds(at, size), pl.ds((j // 2) * half, half)]
        size = half // 8
        at = pl.multiple_of(which * 2 * size + (j % 2) * size, size)
        return out_v.at[owner, pl.ds(at, size)]

    def source(j):
        if j < 6:
            size = width // 8
            at = pl.multiple_of(quarter * 2 * size + (j % 2) * size, size)
            return in_ref.at[j // 2, pl.ds(at, size)]
        size = half // 8
        at = pl.multiple_of(quarter * 2 * size + (j % 2) * size, size)
        return out_ref.at[pl.ds(at, size)]

    def remote(src, dst, send, recv, device):
        return pltpu.make_async_remote_copy(
            src_ref=src, dst_ref=dst, send_sem=send, recv_sem=recv, device_id=device, device_id_type=MESH
        )

    def cross(j):
        return remote(source(j), piece(j, quarter, side), x_send.at[j], x_recv.at[j], (me, other))

    def along_y(j):
        ref = piece(j, quarter, other)
        return remote(ref, ref, y_send.at[j], y_recv.at[j], (y_peer, side))

    def to_core(j, which, slot):
        ref = piece(j, which, other)
        return remote(ref, ref, core_send.at[slot, j], core_recv.at[slot, j], (core_peer, side))

    y_quarter = quarter + 2 - 4 * (quarter // 2)
    first_core = lambda j: to_core(j, quarter, 0)
    second_core = lambda j: to_core(j, y_quarter, 1)
    taps_copy = remote(taps_v.at[side], taps_v.at[side], side_sem.at[0], side_sem.at[1], (me, other))

    def forward(j):
        cross(j).wait_recv()
        along_y(j).start()
        first_core(j).start()

    def forward_y(j):
        along_y(j).wait_recv()
        second_core(j).start()

    def arrived(j):
        first_core(j).wait_recv()
        second_core(j).wait_recv()

    load_x = pltpu.make_async_copy(x_ref, x_v, load_sem.at[0])
    load_out = pltpu.make_async_copy(out_ref, out_v.at[side], load_sem.at[2])
    load_in = [
        pltpu.make_async_copy(in_ref.at[k], in_v.at[side, :, pl.ds(k * half, half)], load_sem.at[3 + k])
        for k in range(3)
    ]
    taps_v[side] = values_ref[:, :half]
    load_x.start()
    for copy in load_in:
        copy.start()
    load_out.start()
    barrier = pltpu.get_barrier_semaphore()
    for device in ((me, other), (y_peer, side), (core_peer, side)):
        pl.semaphore_signal(barrier, inc=1, device_id=device, device_id_type=MESH)
    pl.semaphore_wait(barrier, 3)
    for j in range(PIECES):
        cross(j).start()
    taps_copy.start()
    last_v[...] = jnp.zeros_like(last_v)
    load_x.wait()
    for copy in load_in:
        copy.wait()

    def block_rows(i):
        return pl.ds(pl.multiple_of(i * FRONT, FRONT), FRONT)

    def keep_out(i, owner, slot):
        column = pl.multiple_of(owner * 4 * half, 4 * half)
        return pltpu.make_async_copy(
            keep_v.at[slot], keep_ref.at[block_rows(i), pl.ds(column, 4 * half)], keep_sem.at[slot]
        )

    def half_block(i, owner, slot):
        at = block_rows(i)
        parts = dot(h1_v[at, :], in_v[owner], 1, 0)
        b_part, c_part, x_part = (parts[:, :half], parts[:, half : 2 * half], parts[:, 2 * half :])
        m = b_part * x_part
        one, two = block_keeps(lengths_ref, i * FRONT, FRONT)
        row = lax.broadcasted_iota(jnp.int32, (FRONT, 1), 0)
        before = last_v[owner]
        m_one = jnp.where(row == 0, before[7:8], pltpu.roll(m, 1, 0))
        m_two = jnp.where(row == 0, before[6:7], jnp.where(row == 1, before[7:8], pltpu.roll(m, 2, 0)))
        last_v[owner] = m[FRONT - 8 :]
        taps = taps_v[owner]
        v = taps[2:3] * m + taps[3:4] * jnp.where(one, m_one, 0.0)
        v = v + taps[4:5] * jnp.where(two, m_two, 0.0)
        keep_v[slot, :, :half] = b_part.astype(BF)
        keep_v[slot, :, half : 2 * half] = c_part.astype(BF)
        keep_v[slot, :, 2 * half : 3 * half] = x_part.astype(BF)
        keep_v[slot, :, 3 * half :] = v.astype(BF)
        z_v[owner, at, :] = (c_part * v).astype(BF)

    for i in range(blocks):
        at = block_rows(i)
        x = x_v[at, :].astype(F32)
        h1_v[at, :] = (x * rms_scale(x) * values_ref[0:1, :]).astype(BF)
        if i >= 2:
            keep_out(i - 2, side, i % 2).wait()
        half_block(i, side, i % 2)
        keep_out(i, side, i % 2).start()
        forward(i)
    store_h1 = pltpu.make_async_copy(h1_v, h1_ref, store_sem.at[0])
    store_h1.start()
    for j in range(blocks, PIECES):
        forward_y(j - blocks)
        forward(j)
    for j in range(PIECES - blocks, PIECES - 2):
        forward_y(j)
    for j in range(PIECES - 2):
        arrived(j)
    taps_copy.wait()
    for copy in (keep_out(i, side, i % 2) for i in (blocks - 2, blocks - 1)):
        copy.wait()

    for i in range(blocks):
        if i >= 2:
            keep_out(i - 2, other, i % 2).wait()
        half_block(i, other, i % 2)
        keep_out(i, other, i % 2).start()
        if i == 1:
            forward_y(PIECES - 2)
        if i == 2:
            forward_y(PIECES - 1)
    store_z = pltpu.make_async_copy(z_v, z_ref, store_sem.at[1])
    store_z.start()
    load_out.wait()
    for j in (PIECES - 2, PIECES - 1):
        arrived(j)
    stores = [
        pltpu.make_async_copy(
            in_v.at[h], in_full_ref.at[:, pl.ds(h * 3 * half, 3 * half)], store_sem.at[2 + h]
        )
        for h in range(2)
    ]
    stores += [
        pltpu.make_async_copy(out_v.at[h], out_full_ref.at[pl.ds(h * half, half)], store_sem.at[4 + h])
        for h in range(2)
    ]
    stores += [
        pltpu.make_async_copy(
            taps_v.at[h], taps_full_ref.at[:, pl.ds(h * half, half)], store_sem.at[6 + h]
        )
        for h in range(2)
    ]
    for copy in stores:
        copy.start()
    for copy in (keep_out(i, other, i % 2) for i in (blocks - 2, blocks - 1)):
        copy.wait()

    def row_out(i):
        slot = lax.rem(i, 2)
        return (
            pltpu.make_async_copy(resid_v.at[slot], resid_ref.at[block_rows(i)], keep_sem.at[slot]),
            pltpu.make_async_copy(h2_v.at[slot], h2_ref.at[block_rows(i)], side_sem.at[2 + slot]),
        )

    for i in range(blocks):
        at = block_rows(i)
        if i >= 2:
            for copy in row_out(i - 2):
                copy.wait()
        z = jnp.concatenate([z_v[0, at, :], z_v[1, at, :]], 1)
        total = dot(z, out_v[...].reshape(width, width), 1, 0)
        resid = x_v[at, :].astype(F32) + total
        resid_v[i % 2] = resid
        h2_v[i % 2] = (resid * rms_scale(resid) * values_ref[1:2, :]).astype(BF)
        for copy in row_out(i):
            copy.start()
    for i in (blocks - 2, blocks - 1):
        for copy in row_out(i):
            copy.wait()
    for j in range(PIECES):
        cross(j).wait_send()
        along_y(j).wait_send()
        first_core(j).wait_send()
        second_core(j).wait_send()
    for copy in [store_h1, store_z, *stores]:
        copy.wait()


def mixer_forward(lengths, x, in_w, out_w, values):
    rows, width = x.shape
    half = out_w.shape[0]
    any_spec = pl.BlockSpec(memory_space=pl.ANY)
    vmem_spec = pl.BlockSpec(memory_space=pltpu.VMEM)
    dma = pltpu.SemaphoreType.DMA
    shape = jax.ShapeDtypeStruct
    low = shape((rows, width), BF)
    return pl.pallas_call(
        mixer_kernel,
        out_shape=(
            low,
            shape((rows, 4 * width), BF),
            shape((2, rows, half), BF),
            shape((rows, width), F32),
            low,
            shape((width, 3 * width), BF),
            shape((width, width), BF),
            shape((8, width), F32),
        ),
        in_specs=[pl.BlockSpec(memory_space=pltpu.SMEM)] + [any_spec] * 3 + [vmem_spec],
        out_specs=(any_spec,) * 8,
        scratch_shapes=[
            pltpu.VMEM((rows, width), BF),
            pltpu.VMEM((rows, width), BF),
            pltpu.VMEM((2, rows, half), BF),
            pltpu.VMEM((2, width, 3 * half), BF),
            pltpu.VMEM((2, half, width), BF),
            pltpu.VMEM((2, 8, half), F32),
            pltpu.VMEM((2, FRONT, 4 * half), BF),
            pltpu.VMEM((2, FRONT, width), F32),
            pltpu.VMEM((2, FRONT, width), BF),
            pltpu.VMEM((2, 8, half), F32),
            dma((6,)),
            dma((2,)),
            dma((8,)),
            dma((4,)),
            *[dma((PIECES,))] * 4,
            dma((2, PIECES)),
            dma((2, PIECES)),
        ],
        compiler_params=pltpu.CompilerParams(
            collective_id=2, has_side_effects=True, vmem_limit_bytes=VMEM_BYTES
        ),
    )(lengths, x, in_w, out_w, values)


def swiglu_kernel(h2_ref, gate_ref, up_ref, hid_ref, slope_ref, silu_ref):
    h2 = h2_ref[...]
    gate = dot(h2, gate_ref[...], 1, 0)
    up = dot(h2, up_ref[...], 1, 0)
    sig = jax.nn.sigmoid(gate)
    silu = gate * sig
    hid_ref[...] = (silu * up).astype(BF)
    slope_ref[...] = (up * sig * (1.0 + gate * (1.0 - sig))).astype(BF)
    silu_ref[...] = silu.astype(BF)


def swiglu(h2, gate_w, up_w):
    rows, width = h2.shape
    hidden = gate_w.shape[1]
    out = jax.ShapeDtypeStruct((rows, hidden), BF)
    row_spec = pl.BlockSpec((BLOCK, hidden), lambda i: (i, 0))
    whole = pl.BlockSpec((width, hidden), lambda i: (0, 0), pipeline_mode=pl.Buffered(1))
    return pl.pallas_call(
        swiglu_kernel,
        grid=(rows // BLOCK,),
        out_shape=(out, out, out),
        in_specs=[pl.BlockSpec((BLOCK, width), lambda i: (i, 0)), whole, whole],
        out_specs=(row_spec, row_spec, row_spec),
        compiler_params=pltpu.CompilerParams(vmem_limit_bytes=VMEM_BYTES),
    )(h2, gate_w, up_w)


class Reducer:
    def __init__(self, count, tiles, parts, whole, send, recv, kinds, out_sem):
        self.count = count
        self.tiles, self.parts, self.whole = tiles, parts, whole
        self.send, self.recv = send, recv
        self.kinds, self.out_sem = kinds, out_sem
        me, self.side = lax.axis_index("dp"), lax.axis_index("tensor")
        bit = [lax.rem(lax.div(me, 1 << b), 2) for b in range(4)]
        odd_core = bit[0] == 1
        self.plans = []
        for order in ((0, 1, 2, 3), (0, 2, 1, 3)):
            peer, keep, give, off = [], [], [], 0
            for s, b in enumerate(order):
                size = TILE_ROWS >> (s + 1)
                peer.append(me + (1 << b) * (1 - 2 * bit[b]))
                give.append(off + (1 - bit[b]) * size)
                off = off + bit[b] * size
                keep.append(off)
            self.plans.append((peer, keep, give))
        even, odd = self.plans
        self.plans[1] = tuple(
            [jnp.where(odd_core, o, e) for o, e in zip(odd[k], even[k])] for k in range(3)
        )

    def at(self, n, lag=0):
        sizes = (SLOTS, TILE_SLOTS, WHOLE_SLOTS) + PART_SLOTS
        if not isinstance(n, dict):
            n = {"n": n, "parity": lax.rem(n, 2), "slots": [lax.rem(n, size) for size in sizes]}
        slots = []
        for size, slot in zip(sizes, n["slots"]):
            back = slot - lag % size
            slots.append(jnp.where(back < 0, back + size, back) if lag % size else slot)
        parity = n["parity"] if lag % 2 == 0 else 1 - n["parity"]
        return {"n": n["n"] - lag, "parity": parity, "slots": slots}

    def plan(self, tile, s):
        even, odd = self.plans
        size = TILE_ROWS >> (s + 1)
        pick = [jnp.where(tile["parity"] == 1, odd[k][s], even[k][s]) for k in range(3)]
        return pick[0], pl.multiple_of(pick[1], size), pl.multiple_of(pick[2], size), size

    def scatter(self, tile, s):
        peer, keep, give, size = self.plan(tile, s)
        sem, slot, _, *part = tile["slots"]
        return pltpu.make_async_remote_copy(
            src_ref=self.tiles.at[slot, pl.ds(give, size)],
            dst_ref=self.parts[s].at[part[s]],
            send_sem=self.send.at[sem, s],
            recv_sem=self.recv.at[sem, s],
            device_id=(peer, self.side),
            device_id_type=MESH,
        )

    def gather(self, tile, s):
        peer, keep, give, size = self.plan(tile, s)
        sem, _, slot, *_ = tile["slots"]
        block = self.whole.at[slot, pl.ds(keep, size)]
        return pltpu.make_async_remote_copy(
            src_ref=block,
            dst_ref=block,
            send_sem=self.send.at[sem, 4 + s],
            recv_sem=self.recv.at[sem, 4 + s],
            device_id=(peer, self.side),
            device_id_type=MESH,
        )

    def write(self, tile, act):
        n = tile["n"]
        sem, _, slot, *_ = tile["slots"]
        for first, last, stride, pieces, place in self.kinds:
            size = TILE_ROWS // pieces

            @pl.when((n >= first) & (n < last) & (lax.rem(n - first, stride) == 0))
            def _():
                for q in range(pieces):
                    copy = pltpu.make_async_copy(
                        self.whole.at[slot, pl.ds(q * size, size)],
                        place(lax.div(n - first, stride), q),
                        self.out_sem.at[sem, q],
                    )
                    act(copy)

    def add(self, tile, s):
        peer, keep, give, size = self.plan(tile, s)
        _, slot, whole, *part = tile["slots"]
        rows = pl.ds(keep, size)
        total = self.tiles[slot, rows, :].astype(F32) + self.parts[s][part[s]].astype(F32)
        if s == 3:
            self.whole[whole, rows, :] = total.astype(BF)
        else:
            self.tiles[slot, rows, :] = total.astype(BF)

    def put(self, n, value):
        tile = self.at(n)
        self.tiles[tile["slots"][1]] = value.astype(BF)
        self.scatter(tile, 0).start()

    def put_blocks(self, n, value):
        tile = self.at(n)
        size = TILE_ROWS // 4
        for q in range(4):
            block = value[:, q * TILE_COLS : (q + 1) * TILE_COLS]
            self.tiles[tile["slots"][1], q * size : (q + 1) * size, :] = block.astype(BF)
        self.scatter(tile, 0).start()

    def tick(self, n):
        now = self.at(n)

        def stage(k, lag):
            m = now["n"] - lag

            @pl.when((m >= 0) & (m < self.count))
            def _():
                tile = self.at(now, lag)
                if k <= 4:
                    self.scatter(tile, k - 1).wait()
                    self.add(tile, k - 1)
                    if k < 4:
                        self.scatter(tile, k).start()
                    else:
                        self.gather(tile, 3).start()
                elif k <= 8:
                    self.gather(tile, 8 - k).wait()
                    if k < 8:
                        self.gather(tile, 7 - k).start()
                    else:
                        self.write(tile, lambda copy: copy.start())
                else:
                    self.write(tile, lambda copy: copy.wait())

        for k in (1, 6, 2, 3, 4, 5, 7, 8, 9):
            stage(k, LAGS[k - 1])


def back_kernel(
    lengths_ref,
    hid_ref,
    slope_ref,
    silu_ref,
    h2_ref,
    dy_ref,
    gate_ref,
    up_ref,
    down_ref,
    resid_ref,
    x_ref,
    keep_ref,
    z_ref,
    h1_ref,
    in_ref,
    out_ref,
    values_ref,
    taps_ref,
    down_sum_ref,
    gate_sum_ref,
    up_sum_ref,
    out_sum_ref,
    in_sum_ref,
    dgu_ref,
    dh2_own_ref,
    dh2_got_ref,
    ffn_own_ref,
    ffn_got_ref,
    dp_ref,
    grad_ref,
    result_ref,
    small_ref,
    dy_v,
    h2_v,
    wide_v,
    down_v,
    tile_v,
    row_v,
    small_v,
    small_in,
    next_v,
    tiles,
    whole,
    part0,
    part1,
    part2,
    part3,
    load_sem,
    tile_sem,
    stream_sem,
    dgu_sem,
    own_sem,
    hid_sem,
    dp_sem,
    grad_sem,
    small_send,
    small_recv,
    x_send,
    x_recv,
    send,
    recv,
    out_sem,
):
    me, side = lax.axis_index("dp"), lax.axis_index("tensor")
    rows, width = dy_v.shape
    hidden = hid_ref.shape[1]
    half = width // 2
    blocks = rows // BLOCK
    n_down = hidden // TILE_COLS
    n_out = half // TILE_COLS
    first_gate, first_out = n_down, 3 * n_down
    first_late = first_gate + 4
    first_in = first_out + n_out
    count = first_in + 3 * n_out

    def rows_of(ref):
        return lambda t, q: ref.at[
            pl.ds(pl.multiple_of(t * TILE_COLS, TILE_COLS), TILE_COLS), pl.ds(q * TILE_COLS, TILE_COLS)
        ]

    def columns_of(ref):
        return lambda t, q: ref.at[:, pl.ds(pl.multiple_of(t * TILE_COLS, TILE_COLS), TILE_COLS)]

    def in_place(t, q):
        column = pl.multiple_of(lax.rem(t, n_out) * TILE_COLS, TILE_COLS)
        return in_sum_ref.at[lax.div(t, n_out), :, pl.ds(column, TILE_COLS)]

    kinds = (
        (0, first_gate, 1, 4, rows_of(down_sum_ref)),
        (first_gate, first_out, 2, 1, columns_of(gate_sum_ref)),
        (first_gate + 1, first_out, 2, 1, columns_of(up_sum_ref)),
        (first_out, first_in, 1, 4, rows_of(out_sum_ref)),
        (first_in, count, 1, 1, in_place),
    )
    red = Reducer(count, tiles, (part0, part1, part2, part3), whole, send, recv, kinds, out_sem)

    def peer(bit):
        return me + bit * (1 - 2 * ((me // bit) % 2))

    def block_rows(i):
        return pl.ds(pl.multiple_of((blocks - 1 - i) * BLOCK, BLOCK), BLOCK)

    load_dy = pltpu.make_async_copy(dy_ref, dy_v, load_sem.at[0])
    load_down = pltpu.make_async_copy(down_ref, down_v, load_sem.at[1])
    load_gate = pltpu.make_async_copy(gate_ref, wide_v.at[:, pl.ds(0, hidden)], load_sem.at[2])
    load_up = pltpu.make_async_copy(up_ref, wide_v.at[:, pl.ds(hidden, hidden)], load_sem.at[3])
    load_h2 = pltpu.make_async_copy(h2_ref, h2_v, load_sem.at[4])
    load_in = pltpu.make_async_copy(in_ref, wide_v.at[:, pl.ds(0, 3 * width)], load_sem.at[2])
    load_out = pltpu.make_async_copy(out_ref, wide_v.at[:, pl.ds(3 * width, width)], load_sem.at[3])
    load_h1 = pltpu.make_async_copy(h1_ref, h2_v, load_sem.at[4])

    def tile_of(ref, column, n):
        column = pl.multiple_of(column, TILE_COLS)
        return pltpu.make_async_copy(
            ref.at[:, pl.ds(column, TILE_COLS)], tile_v.at[lax.rem(n, 2)], tile_sem.at[lax.rem(n, 2)]
        )

    def hid_tile(n):
        return tile_of(hid_ref, n * TILE_COLS, n)

    def dgu_tile(n):
        k = n - first_gate
        return tile_of(dgu_ref, lax.rem(k, 2) * hidden + lax.div(k, 2) * TILE_COLS, n)

    def z_tile(n):
        return tile_of(z_ref.at[side], (n - first_out) * TILE_COLS, n)

    def dp_tile(n):
        return tile_of(dp_ref, (n - first_in) * TILE_COLS, n)

    def row_own(i, ref):
        slot = lax.rem(i, 2)
        return pltpu.make_async_copy(row_v.at[slot], ref.at[block_rows(i)], own_sem.at[slot])

    def row_send(i, own, got, first):
        at = block_rows(i)
        return pltpu.make_async_remote_copy(
            src_ref=own.at[at],
            dst_ref=got.at[at],
            send_sem=x_send.at[first + i],
            recv_sem=x_recv.at[first + i],
            device_id=(me, 1 - side),
            device_id_type=MESH,
        )

    def dh2_send(i):
        return row_send(i, dh2_own_ref, dh2_got_ref, 0)

    def ffn_send(i):
        return row_send(i, ffn_own_ref, ffn_got_ref, blocks)

    def small_copy(s):
        return pltpu.make_async_remote_copy(
            src_ref=small_v,
            dst_ref=small_in.at[s],
            send_sem=small_send.at[s],
            recv_sem=small_recv.at[s],
            device_id=(peer(1 << s), side),
            device_id_type=MESH,
        )

    def small_add(s):
        small_copy(s).wait()
        small_v[...] = small_v[...] + small_in[s]

    load_dy.start()
    hid_tile(0).start()
    load_down.start()
    load_gate.start()
    load_up.start()
    load_h2.start()

    barrier = pltpu.get_barrier_semaphore()
    for bit in (1, 2, 4, 8):
        pl.semaphore_signal(barrier, inc=1, device_id=(peer(bit), side), device_id_type=MESH)
    pl.semaphore_signal(barrier, inc=1, device_id=(me, 1 - side), device_id_type=MESH)
    pl.semaphore_wait(barrier, 5)

    small_v[...] = jnp.zeros_like(small_v)
    next_v[...] = jnp.zeros_like(next_v)

    def down_step(n, carry):
        @pl.when(n + 1 < n_down)
        def _():
            hid_tile(n + 1).start()

        hid_tile(n).wait()
        red.put_blocks(n, dot(tile_v[lax.rem(n, 2)], dy_v[...], 0, 0))
        return carry

    def grads(slope_v, silu_v, dgu_v):
        def pair(i):
            at = block_rows(i)
            return (
                pltpu.make_async_copy(slope_ref.at[at], slope_v.at[lax.rem(i, 2)], stream_sem.at[lax.rem(i, 2), 0]),
                pltpu.make_async_copy(silu_ref.at[at], silu_v.at[lax.rem(i, 2)], stream_sem.at[lax.rem(i, 2), 1]),
            )

        def dgu_out(i):
            return pltpu.make_async_copy(
                dgu_v.at[lax.rem(i, 2)], dgu_ref.at[block_rows(i)], dgu_sem.at[lax.rem(i, 2)]
            )

        for copy in pair(0):
            copy.start()
        load_dy.wait()
        def down_group(g, carry):
            lax.fori_loop(3 * g, 3 * g + 3, down_step, 0)
            red.tick(1 + g)
            return carry

        lax.fori_loop(0, n_down // 3, down_group, 0)
        load_down.wait()
        load_gate.wait()
        load_up.wait()

        def early_tiles(j):
            column = pl.ds(pl.multiple_of(j * TILE_COLS, TILE_COLS), TILE_COLS)
            return (
                pltpu.make_async_copy(slope_ref.at[:, column], tile_v.at[0], tile_sem.at[0]),
                pltpu.make_async_copy(silu_ref.at[:, column], tile_v.at[1], tile_sem.at[1]),
            )

        def early(j):
            for copy in early_tiles(j):
                copy.wait()
            n = first_gate + 2 * j
            hidden_rows = pl.ds(pl.multiple_of(j * TILE_COLS, TILE_COLS), TILE_COLS)
            d_hid = dot(dy_v[...], down_v[hidden_rows, :], 1, 1)
            red.put(n, dot(h2_v[...], (d_hid * tile_v[0].astype(F32)).astype(BF), 0, 0))
            red.put(n + 1, dot(h2_v[...], (d_hid * tile_v[1].astype(F32)).astype(BF), 0, 0))
            red.tick(8 + 3 * j)

            @pl.when(j == 0)
            def _():
                for copy in early_tiles(1):
                    copy.start()

        for copy in early_tiles(0):
            copy.start()
        load_h2.wait()

        def grad_step(i, carry):
            slot = lax.rem(i, 2)

            @pl.when(i + 1 < blocks)
            def _():
                for copy in pair(i + 1):
                    copy.start()

            for copy in pair(i):
                copy.wait()

            @pl.when(i >= 2)
            def _():
                dgu_out(i - 2).wait()

            d_hid = dot(dy_v[block_rows(i), :], down_v[...], 1, 1)
            dgu_v[slot, :, :hidden] = (d_hid * slope_v[slot].astype(F32)).astype(BF)
            dgu_v[slot, :, hidden:] = (d_hid * silu_v[slot].astype(F32)).astype(BF)
            dgu_out(i).start()
            row_v[slot] = dot(dgu_v[slot], wide_v[...], 1, 1).astype(BF)
            row_own(i, dh2_own_ref).start()

            red.tick(4 + i + jnp.where(i >= 4, 1, 0) + jnp.where(i >= 6, 1, 0))
            row_own(i, dh2_own_ref).wait()
            dh2_send(i).start()

            @pl.when((i == 3) | (i == 5))
            def _():
                early(lax.div(i - 3, 2))
            return carry

        lax.fori_loop(0, blocks, grad_step, 0)
        load_in.start()
        load_out.start()
        for i in (blocks - 2, blocks - 1):
            dgu_out(i).wait()
        dgu_tile(first_late).start()

    pl.run_scoped(
        grads,
        pltpu.VMEM((2, BLOCK, hidden), BF),
        pltpu.VMEM((2, BLOCK, hidden), BF),
        pltpu.VMEM((2, BLOCK, 2 * hidden), BF),
    )

    def gate_put(n):
        dgu_tile(n).wait()
        red.put(n, dot(h2_v[...], tile_v[lax.rem(n, 2)], 0, 0))

    late = blocks // 2
    twice = first_out - first_late - blocks

    def hid_rows(i, hid_v):
        slot = lax.rem(i, 2)
        return pltpu.make_async_copy(hid_ref.at[block_rows(i)], hid_v.at[slot], hid_sem.at[slot])

    def ffn_block(i, hid_v):
        @pl.when((i + 1 < late) | ((i >= late) & (i + 1 < blocks)))
        def _():
            hid_rows(i + 1, hid_v).start()

        hid_rows(i, hid_v).wait()
        slot = lax.rem(i, 2)
        row_v[slot] = dot(hid_v[slot], down_v[...], 1, 0).astype(BF)
        row_own(i, ffn_own_ref).start()

    def ffn_pass(i):
        row_own(i, ffn_own_ref).wait()
        ffn_send(i).start()

    def mixer(keep_v, resid_v, x_v, pair_v, hid_v, dp_v, grad_v, dr1_v):
        def inputs(i):
            at, slot = block_rows(i), lax.rem(i, 2)
            return (
                pltpu.make_async_copy(keep_ref.at[at], keep_v.at[slot], stream_sem.at[slot, 0]),
                pltpu.make_async_copy(resid_ref.at[at], resid_v.at[slot], stream_sem.at[slot, 1]),
                pltpu.make_async_copy(x_ref.at[at], x_v.at[slot], stream_sem.at[slot, 2]),
                pltpu.make_async_copy(dh2_own_ref.at[at], pair_v.at[0], stream_sem.at[slot, 3]),
            )

        def got(i):
            return pltpu.make_async_copy(dh2_got_ref.at[block_rows(i)], pair_v.at[1], dgu_sem.at[0])

        def dp_out(i):
            column = pl.multiple_of(side * 3 * half, 3 * half)
            return pltpu.make_async_copy(
                dp_v.at[:, pl.ds(column, 3 * half)], dp_ref.at[block_rows(i)], dp_sem
            )

        def put_dp(k, value):
            for h in range(2):
                first = (3 * h + k) * half
                dp_v[:, first : first + half] = value[:, h * half : (h + 1) * half].astype(BF)

        def kept(slot, k):
            return jnp.concatenate(
                [keep_v[slot, :, (4 * h + k) * half : (4 * h + k + 1) * half] for h in range(2)], 1
            ).astype(F32)

        def grad_out(i):
            return pltpu.make_async_copy(grad_v, grad_ref.at[block_rows(i)], grad_sem)

        def finish(i):
            dp_out(i).wait()
            grad_out(i).wait()

        def mixer_first(i):
            slot = lax.rem(i, 2)
            at = block_rows(i)
            for copy in inputs(i):
                copy.wait()
            got(i).wait()

            @pl.when(i > 0)
            def _():
                finish(i - 1)

            resid = resid_v[slot]
            scale2 = rms_scale(resid)
            n2 = resid * scale2
            dh2 = pair_v[0].astype(F32) + pair_v[1].astype(F32)
            d_resid, gain2_part = norm_back(dh2, n2, scale2, values_ref[1:2, :])
            dr1 = dy_v[at, :].astype(F32) + d_resid
            dr1b = dr1.astype(BF)
            dr1_v[...] = dr1
            dy_v[at, :] = dr1b
            dz = dot(dr1b, wide_v[:, 3 * width : 4 * width], 1, 1)
            put_dp(1, dz * kept(slot, 3))
            dv = dz * kept(slot, 1)
            b_part = kept(slot, 0)
            x_part = kept(slot, 2)
            m = b_part * x_part
            one, two = block_keeps(lengths_ref, (blocks - 1 - i) * BLOCK, BLOCK)
            row = lax.broadcasted_iota(jnp.int32, (BLOCK, 1), 0)
            dv_one = jnp.where(one, dv, 0.0)
            dv_two = jnp.where(two, dv, 0.0)
            up_one = jnp.where(row == BLOCK - 1, next_v[0:1, :], pltpu.roll(dv_one, BLOCK - 1, 0))
            up_two = jnp.where(
                row == BLOCK - 2,
                next_v[8:9, :],
                jnp.where(row == BLOCK - 1, next_v[9:10, :], pltpu.roll(dv_two, BLOCK - 2, 0)),
            )
            next_v[0:8, :] = dv_one[0:8]
            next_v[8:16, :] = dv_two[0:8]
            taps = taps_ref[2:5, :]
            dm = taps[0:1] * dv + taps[1:2] * up_one + taps[2:3] * up_two
            put_dp(0, dm * x_part)
            put_dp(2, dm * b_part)
            dp_out(i).start()
            small_v[1:2, :] += gain2_part.reshape(1, width)
            small_v[2:3, :] += jnp.sum(dv * m, axis=0, keepdims=True)
            small_v[3:4, :] += jnp.sum(up_one * m, axis=0, keepdims=True)
            small_v[4:5, :] += jnp.sum(up_two * m, axis=0, keepdims=True)

        def mixer_second(i):
            dh1 = dot(dp_v[...], wide_v[:, : 3 * width], 1, 1)
            x = x_v[lax.rem(i, 2)].astype(F32)
            scale1 = rms_scale(x)
            d_input, gain1_part = norm_back(dh1, x * scale1, scale1, values_ref[0:1, :])
            grad_v[...] = (dr1_v[...] + d_input).astype(BF)
            grad_out(i).start()
            small_v[0:1, :] += gain1_part.reshape(1, width)

        hid_rows(0, hid_v).start()
        for copy in inputs(0):
            copy.start()
        load_in.wait()
        load_out.wait()

        def mixer_step(i, carry):
            n = first_late + i + jnp.minimum(i, twice)
            dh2_send(i).wait_recv()
            got(i).start()

            @pl.when(n + 1 < first_out)
            def _():
                dgu_tile(n + 1).start()

            @pl.when(n + 1 == first_out)
            def _():
                z_tile(n + 1).start()

            gate_put(n)
            mixer_first(i)
            red.tick(n + 1)
            mixer_second(i)

            @pl.when(i + 1 < blocks)
            def _():
                for copy in inputs(i + 1):
                    copy.start()

            @pl.when(i >= late)
            def _():
                ffn_block(i - late, hid_v)

            @pl.when(i < twice)
            def _():
                dgu_tile(n + 2).start()
                gate_put(n + 1)

            @pl.when(i >= late)
            def _():
                ffn_pass(i - late)

            @pl.when(i < twice)
            def _():
                red.tick(n + 2)

            return carry

        lax.fori_loop(0, blocks, mixer_step, 0)
        finish(blocks - 1)

    pl.run_scoped(
        mixer,
        pltpu.VMEM((2, BLOCK, 4 * width), BF),
        pltpu.VMEM((2, BLOCK, width), F32),
        pltpu.VMEM((2, BLOCK, width), BF),
        pltpu.VMEM((2, BLOCK, width), BF),
        pltpu.VMEM((2, BLOCK, hidden), BF),
        pltpu.VMEM((BLOCK, 3 * width), BF),
        pltpu.VMEM((BLOCK, width), BF),
        pltpu.VMEM((BLOCK, width), F32),
    )

    small_copy(0).start()

    def tail(resid_v, pair_v, result_v, hid_v):
        def inputs(i):
            at = block_rows(i)
            return (
                pltpu.make_async_copy(resid_ref.at[at], resid_v, stream_sem.at[0, 0]),
                pltpu.make_async_copy(ffn_own_ref.at[at], pair_v.at[0], stream_sem.at[0, 1]),
                pltpu.make_async_copy(ffn_got_ref.at[at], pair_v.at[1], stream_sem.at[0, 2]),
            )

        def result_out(i):
            return pltpu.make_async_copy(result_v, result_ref.at[block_rows(i)], grad_sem)

        def post(p):
            i = lax.div(p, 2)

            @pl.when((lax.rem(p, 2) == 0) & (i < blocks))
            def _():
                ffn_send(i).wait_recv()
                for copy in inputs(i):
                    copy.start()

            @pl.when((lax.rem(p, 2) == 1) & (i < blocks))
            def _():
                for copy in inputs(i):
                    copy.wait()

                @pl.when(i > 0)
                def _():
                    result_out(i - 1).wait()

                both = pair_v[0].astype(F32) + pair_v[1].astype(F32)
                result_v[...] = (resid_v[...] + both).astype(BF)
                result_out(i).start()

        base = first_out

        def step(n, put):
            i = late + n - base

            @pl.when(i < blocks)
            def _():
                ffn_block(i, hid_v)

            put(n)

            @pl.when(i < blocks)
            def _():
                ffn_pass(i)

            red.tick(n + 1)
            post(n - base)

        hid_rows(late, hid_v).start()

        load_h1.start()

        def out_put(n):
            z_tile(n).wait()
            red.put_blocks(n, dot(tile_v[lax.rem(n, 2)], dy_v[...], 0, 0))

        for n in range(first_out, first_in):
            (z_tile if n + 1 < first_in else dp_tile)(n + 1).start()
            step(n, out_put)
        small_add(0)
        small_copy(1).start()
        load_h1.wait()

        def in_step(n, carry):
            @pl.when(n + 1 < count)
            def _():
                dp_tile(n + 1).start()

            def in_put(n):
                dp_tile(n).wait()
                red.put(n, dot(h2_v[...], tile_v[lax.rem(n, 2)], 0, 0))

            step(n, in_put)
            return carry

        third = (count - first_in) // 3
        lax.fori_loop(first_in, first_in + third, in_step, 0)
        small_add(1)
        small_copy(2).start()
        lax.fori_loop(first_in + third, first_in + 2 * third, in_step, 0)
        small_add(2)
        small_copy(3).start()
        lax.fori_loop(first_in + 2 * third, count, in_step, 0)
        small_add(3)
        small_out = pltpu.make_async_copy(small_v, small_ref, load_sem.at[0])
        small_out.start()

        def drain_step(n, carry):
            red.tick(n + 1)
            post(n - base)
            return carry

        lax.fori_loop(count, count + LAGS[-1] - 1, drain_step, 0)
        result_out(blocks - 1).wait()
        small_out.wait()
        for i in range(blocks):
            dh2_send(i).wait_send()
            ffn_send(i).wait_send()

    pl.run_scoped(
        tail,
        pltpu.VMEM((BLOCK, width), F32),
        pltpu.VMEM((2, BLOCK, width), BF),
        pltpu.VMEM((BLOCK, width), BF),
        pltpu.VMEM((2, BLOCK, hidden), BF),
    )


def block_backward(
    lengths, hid, slope, silu, h2, dy, gate_w, up_w, down_w, resid, x, keep, z, h1, in_full, out_full,
    values, taps,
):
    rows, hidden = hid.shape
    width = h2.shape[1]
    blocks = rows // BLOCK
    any_spec = pl.BlockSpec(memory_space=pl.ANY)
    vmem_spec = pl.BlockSpec(memory_space=pltpu.VMEM)
    dma = pltpu.SemaphoreType.DMA
    shape = jax.ShapeDtypeStruct
    low = shape((rows, width), BF)
    ring = [pltpu.VMEM((slots, TILE_ROWS, TILE_COLS), BF) for slots in (TILE_SLOTS, WHOLE_SLOTS)]
    ring += [
        pltpu.VMEM((slots, TILE_ROWS >> (s + 1), TILE_COLS), BF) for s, slots in enumerate(PART_SLOTS)
    ]
    return pl.pallas_call(
        back_kernel,
        out_shape=(
            shape(down_w.shape, BF),
            shape(gate_w.shape, BF),
            shape(up_w.shape, BF),
            shape((width // 2, width), BF),
            shape((3, width, width // 2), BF),
            shape((rows, 2 * hidden), BF),
            low,
            low,
            low,
            low,
            shape((rows, 3 * width // 2), BF),
            low,
            low,
            shape((8, width), F32),
        ),
        in_specs=[pl.BlockSpec(memory_space=pltpu.SMEM)] + [any_spec] * 15 + [vmem_spec] * 2,
        out_specs=(any_spec,) * 14,
        scratch_shapes=[
            pltpu.VMEM((rows, width), BF),
            pltpu.VMEM((rows, width), BF),
            pltpu.VMEM((width, 2 * hidden), BF),
            pltpu.VMEM(down_w.shape, BF),
            pltpu.VMEM((2, rows, TILE_COLS), BF),
            pltpu.VMEM((2, BLOCK, width), BF),
            pltpu.VMEM((8, width), F32),
            pltpu.VMEM((4, 8, width), F32),
            pltpu.VMEM((16, width), F32),
            *ring,
            dma((5,)),
            dma((2,)),
            dma((2, 4)),
            dma((2,)),
            dma((2,)),
            dma((2,)),
            dma,
            dma,
            dma((4,)),
            dma((4,)),
            dma((2 * blocks,)),
            dma((2 * blocks,)),
            dma((SLOTS, 8)),
            dma((SLOTS, 8)),
            dma((SLOTS, 4)),
        ],
        compiler_params=pltpu.CompilerParams(
            collective_id=1, has_side_effects=True, vmem_limit_bytes=VMEM_BYTES
        ),
    )(
        lengths, hid, slope, silu, h2, dy, gate_w, up_w, down_w, resid, x, keep, z, h1, in_full, out_full,
        values, taps,
    )


def pair_body(
    tokens,
    cotangent,
    lengths,
    mixer_gain,
    in_weight,
    conv_weight,
    out_weight,
    ffn_gain,
    gate_weight,
    up_weight,
    down_weight,
):
    side = lax.axis_index("tensor")
    half = out_weight.shape[0]
    width = tokens.shape[1]
    values = jnp.zeros((8, width), F32)
    values = values.at[0].set(mixer_gain.astype(F32)).at[1].set(ffn_gain.astype(F32))
    values = values.at[2:5, :half].set(conv_weight.astype(F32))
    h1b, keep, zb, resid, h2b, in_full, out_full, taps = mixer_forward(
        lengths, tokens, in_weight.transpose(1, 0, 2), out_weight, values
    )
    hidb, slope, silu = swiglu(h2b, gate_weight, up_weight)
    down_sum, gate_sum, up_sum, out_sum, in_sum, *_, input_grad, output, small = block_backward(
        lengths, hidb, slope, silu, h2b, cotangent, gate_weight, up_weight, down_weight, resid, tokens,
        keep, zb, h1b, in_full, out_full, values, taps,
    )
    return (
        output,
        input_grad,
        small[0],
        in_sum.astype(F32).transpose(1, 0, 2),
        lax.dynamic_slice_in_dim(small[2:5], side * half, half, 1),
        out_sum.astype(F32),
        small[1],
        gate_sum.astype(F32),
        up_sum.astype(F32),
        down_sum.astype(F32),
    )


def body(
    tokens,
    cotangent,
    lengths,
    mixer_gain,
    in_weight,
    conv_weight,
    out_weight,
    ffn_gain,
    gate_weight,
    up_weight,
    down_weight,
):
    rows = tokens.shape[0]
    dist = distances(lengths[0], rows)
    keep_one = (dist >= 1)[:, None].astype(jnp.float32)
    keep_two = (dist >= 2)[:, None].astype(jnp.float32)
    parts = lax.axis_size("tensor")
    share = rows // parts
    first = lax.axis_index("tensor") * share
    x = tokens.astype(jnp.float32)
    dy = cotangent.astype(jnp.float32)
    g1 = mixer_gain.astype(jnp.float32)
    g2 = ffn_gain.astype(jnp.float32)
    taps = conv_weight.astype(jnp.float32)
    scale1 = rms_scale(x)
    normed1 = x * scale1
    h1b = (normed1 * g1).astype(jnp.bfloat16)
    proj = jnp.einsum("td,dkc->tkc", h1b, in_weight, preferred_element_type=jnp.float32)
    b_part, c_part, x_part = (proj[:, 0], proj[:, 1], proj[:, 2])
    mixed = b_part * x_part
    mixed_one = shift_down(mixed, 1, keep_one)
    mixed_two = shift_down(mixed, 2, keep_two)
    conv_out = taps[0] * mixed + taps[1] * mixed_one + taps[2] * mixed_two
    zb = (c_part * conv_out).astype(jnp.bfloat16)
    mix_part = jnp.dot(zb, out_weight, preferred_element_type=jnp.float32)
    mix_rows = lax.psum_scatter(mix_part, "tensor", scatter_dimension=0, tiled=True)
    x_rows = lax.dynamic_slice_in_dim(x, first, share, 0)
    resid = x_rows + mix_rows
    scale2 = rms_scale(resid)
    normed2 = resid * scale2
    h2b = lax.all_gather((normed2 * g2).astype(jnp.bfloat16), "tensor", axis=0, tiled=True)
    gate = jnp.dot(h2b, gate_weight, preferred_element_type=jnp.float32)
    up = jnp.dot(h2b, up_weight, preferred_element_type=jnp.float32)
    sig = jax.nn.sigmoid(gate)
    silu = gate * sig
    hidb = (silu * up).astype(jnp.bfloat16)
    ffn_part = jnp.dot(hidb, down_weight, preferred_element_type=jnp.float32)
    down_grad = jnp.einsum("tf,td->fd", hidb, cotangent, preferred_element_type=jnp.float32)
    d_hid = jnp.einsum("td,fd->tf", cotangent, down_weight, preferred_element_type=jnp.float32)
    d_gate = (d_hid * up * sig * (1.0 + gate * (1.0 - sig))).astype(jnp.bfloat16)
    d_up = (d_hid * silu).astype(jnp.bfloat16)
    gate_grad = jnp.einsum("td,tf->df", h2b, d_gate, preferred_element_type=jnp.float32)
    up_grad = jnp.einsum("td,tf->df", h2b, d_up, preferred_element_type=jnp.float32)
    dh2_part = jnp.einsum("tf,df->td", d_gate, gate_weight, preferred_element_type=jnp.float32)
    dh2_part = dh2_part + jnp.einsum(
        "tf,df->td", d_up, up_weight, preferred_element_type=jnp.float32
    )
    ffn_rows = lax.psum_scatter(
        ffn_part.astype(jnp.bfloat16), "tensor", scatter_dimension=0, tiled=True
    ).astype(jnp.float32)
    output = lax.all_gather((resid + ffn_rows).astype(jnp.bfloat16), "tensor", axis=0, tiled=True)
    dh2_rows = lax.psum_scatter(dh2_part, "tensor", scatter_dimension=0, tiled=True)
    d_resid, g2_grad = norm_back(dh2_rows, normed2, scale2, g2)
    dr1 = lax.dynamic_slice_in_dim(dy, first, share, 0) + d_resid
    dr1b = lax.all_gather(dr1.astype(jnp.bfloat16), "tensor", axis=0, tiled=True)
    out_grad = jnp.einsum("tc,td->cd", zb, dr1b, preferred_element_type=jnp.float32)
    d_z = jnp.einsum("td,cd->tc", dr1b, out_weight, preferred_element_type=jnp.float32)
    d_c = d_z * conv_out
    d_conv = d_z * c_part
    conv_grad = jnp.stack(
        [
            jnp.sum(d_conv * mixed, axis=0),
            jnp.sum(d_conv * mixed_one, axis=0),
            jnp.sum(d_conv * mixed_two, axis=0),
        ],
        0,
    )
    d_mixed = (
        taps[0] * d_conv
        + taps[1] * shift_up(d_conv * keep_one, 1)
        + taps[2] * shift_up(d_conv * keep_two, 2)
    )
    d_proj = jnp.stack([d_mixed * x_part, d_c, d_mixed * b_part], 1).astype(jnp.bfloat16)
    in_grad_w = jnp.einsum("td,tkc->dkc", h1b, d_proj, preferred_element_type=jnp.float32)
    dh1_part = jnp.einsum("tkc,dkc->td", d_proj, in_weight, preferred_element_type=jnp.float32)
    dh1_rows = lax.psum_scatter(dh1_part, "tensor", scatter_dimension=0, tiled=True)
    normed1_rows = lax.dynamic_slice_in_dim(normed1, first, share, 0)
    scale1_rows = lax.dynamic_slice_in_dim(scale1, first, share, 0)
    d_input, g1_grad = norm_back(dh1_rows, normed1_rows, scale1_rows, g1)
    input_grad = lax.all_gather((dr1 + d_input).astype(jnp.bfloat16), "tensor", axis=0, tiled=True)
    g1_grad, g2_grad = lax.psum((g1_grad, g2_grad), "tensor")
    summed = lax.psum(
        (g1_grad, in_grad_w, conv_grad, out_grad, g2_grad, gate_grad, up_grad, down_grad), "dp"
    )
    return (
        output,
        input_grad,
        summed[0],
        summed[1],
        summed[2],
        summed[3],
        summed[4],
        summed[5],
        summed[6],
        summed[7],
    )


def solution(mesh):
    paired = mesh.shape["tensor"] == 2 and mesh.shape["dp"] == 16
    return jax.shard_map(
        pair_body if paired else body,
        mesh=mesh,
        in_specs=(
            P("dp", None),
            P("dp", None),
            P("dp", None),
            P(),
            P(None, None, "tensor"),
            P(None, "tensor"),
            P("tensor", None),
            P(),
            P(None, "tensor"),
            P(None, "tensor"),
            P("tensor", None),
        ),
        out_specs=(
            P("dp", None),
            P("dp", None),
            P(),
            P(None, None, "tensor"),
            P(None, "tensor"),
            P("tensor", None),
            P(),
            P(None, "tensor"),
            P(None, "tensor"),
            P("tensor", None),
        ),
        check_vma=False,
    )
```
